32 devices in a mesh: gx: 2 (over x), gy: 4 (over y, core), gz: 4 (over z).
Axes of the slice: x: 2, y: 2, z: 4, core: 2. Of those that a mesh axis runs over, the one named last changes fastest.
Arguments:
- field: bfloat16 [64, 32, 64, 256], P(None, 'gz', 'gy', 'gx'), may hold values from -8 to 8
- conv_first: bfloat16 [3, 3, 3, 64, 128], replicated, may hold values from -0.15625 to 0.15625
- norm_gain: float32 [128], replicated, may hold values from 0.5 to 1.5
- norm_shift: float32 [128], replicated, may hold values from -3 to 3
- conv_second: bfloat16 [3, 3, 3, 128, 128], replicated, may hold values from -0.109375 to 0.109375
Outputs:
- result: bfloat16 [128, 16, 32, 128], P(None, 'gz', 'gy', 'gx')
The draws below stay inside these ranges and needn't reach their ends.
All inputs are finite; a program needn't handle non-finite values.
Results may differ from the reference program's by a relative error of at most 0.0017.
The reference program's roundings to bfloat16 on the way (of `activation`) count: a program that leaves them out, or rounds other values in their place, can miss the bound.
Values may be sent and summed in bfloat16 or wider, within the bound.
No kernel may reach another device: no remote copies, remote signals or barrier semaphores. Data moves between devices by JAX's collectives and lax.ppermute only.
A program may use at most 128 MiB of HBM per device.

```python
import jax
import jax.numpy as jnp
from jax import lax

CIN = 64
C = 128
NEWTON = 5
NX = 256
NY = 64
NZ = 32


def draw_field(key, part):
    key_one = jax.random.fold_in(key, 11)
    zpos = jnp.arange(NZ, dtype=jnp.float32) / NZ
    ypos = jnp.arange(NY, dtype=jnp.float32) / NY
    xpos = jnp.arange(NX, dtype=jnp.float32) / NX
    ramp = zpos[:, None, None] + ypos[None, :, None] + xpos[None, None, :]
    wider = (CIN, NZ + 1, NY + 1, NX + 1)
    samples = jax.random.normal(key_one, wider, jnp.float32)
    along_x = samples[:, :, :, 1:] + samples[:, :, :, :-1]
    along_y = along_x[:, :, 1:, :] + along_x[:, :, :-1, :]
    along_z = along_y[:, 1:, :, :] + along_y[:, :-1, :, :]
    smooth = along_z * 0.35355339
    amplitude = jnp.exp(0.5 * ramp * jnp.log(3.0))
    values = smooth * amplitude[None]
    return jnp.clip(values, -8.0, 8.0).astype(jnp.bfloat16)


def gaussian(rng, shape, deviation, bound, held_as=jnp.bfloat16):
    return jnp.clip(deviation * jax.random.normal(rng, shape, jnp.float32), -bound, bound).astype(held_as)


def setup_inputs(seed: int = 0) -> dict:
    streams_of = jax.random.split(jax.random.key(seed), 6)
    return {
        "field": draw_field(jax.random.fold_in(streams_of[5], 71), 0),
        "conv_first": gaussian(streams_of[1], (3, 3, 3, CIN, C), (27 * CIN) ** -0.5, 0.15625),
        "norm_gain": jnp.clip(1.0 + 0.1 * jax.random.normal(streams_of[2], (C,), jnp.float32), 0.5, 1.5),
        "norm_shift": gaussian(streams_of[3], (C,), 0.5, 3.0, jnp.float32),
        "conv_second": gaussian(streams_of[4], (3, 3, 3, C, C), (27 * C) ** -0.5, 0.109375),
    }


epsilon = 1e-05
leak_slope = 0.2

def strided_first(field, kernel):
    depth = field.shape[1] // 2
    height = field.shape[2] // 2
    width = field.shape[3] // 2
    padded = jnp.pad(field, ((0, 0), (1, 0), (1, 0), (1, 0)))
    kernel_wide = kernel.astype(jnp.float32)

    def plane(index_value):
        slab = lax.dynamic_slice_in_dim(padded, (2 * index_value).astype(jnp.int32), 3, axis=1)
        total = jnp.zeros((kernel.shape[4], height, width), jnp.float32)
        for tap_z in range(3):
            for tap_y in range(3):
                for tap_x in range(3):
                    piece = slab[:, tap_z, tap_y:tap_y + 2 * height - 1:2, tap_x:tap_x + 2 * width - 1:2].astype(jnp.float32)
                    total = total + jnp.einsum('io,iyx->oyx', kernel_wide[tap_z, tap_y, tap_x], piece, precision=lax.Precision.HIGHEST)
        return total
    planes = lax.map(plane, jnp.arange(depth, dtype=jnp.int32))
    return jnp.transpose(planes, (1, 0, 2, 3))

def same_second(volume, kernel):
    depth, height, width = (volume.shape[1], volume.shape[2], volume.shape[3])
    padded = jnp.pad(volume, ((0, 0), (1, 1), (1, 1), (1, 1)))
    kernel_wide = kernel.astype(jnp.float32)

    def plane(index_value):
        slab = lax.dynamic_slice_in_dim(padded, index_value.astype(jnp.int32), 3, axis=1)
        total = jnp.zeros((kernel.shape[4], height, width), jnp.float32)
        for tap_z in range(3):
            for tap_y in range(3):
                for tap_x in range(3):
                    piece = slab[:, tap_z, tap_y:tap_y + height, tap_x:tap_x + width].astype(jnp.float32)
                    total = total + jnp.einsum('io,iyx->oyx', kernel_wide[tap_z, tap_y, tap_x], piece, precision=lax.Precision.HIGHEST)
        return total.astype(jnp.bfloat16)
    planes = lax.map(plane, jnp.arange(depth, dtype=jnp.int32))
    return jnp.transpose(planes, (1, 0, 2, 3))

def newton_whitener(covariance):
    trace_value = jnp.trace(covariance, axis1=1, axis2=2)
    scaled = covariance / trace_value[:, None, None]
    identity = jnp.broadcast_to(jnp.eye(covariance.shape[-1], dtype=covariance.dtype), covariance.shape)
    newton_mat = identity
    for repeat in range(NEWTON):
        square = jnp.einsum('gij,gjk->gik', newton_mat, newton_mat, precision=lax.Precision.HIGHEST)
        cubed = jnp.einsum('gij,gjk->gik', square, newton_mat, precision=lax.Precision.HIGHEST)
        newton_mat = 1.5 * newton_mat - 0.5 * jnp.einsum('gij,gjk->gik', cubed, scaled, precision=lax.Precision.HIGHEST)
    return newton_mat / jnp.sqrt(trace_value)[:, None, None]

def whiten(block, average, whitener, norm_gain, norm_shift):
    shape = block.shape
    grouped = block.reshape(2, shape[0] // 2, -1) - average[:, :, None]
    mixed = jnp.einsum('gij,gjm->gim', whitener, grouped, precision=lax.Precision.HIGHEST).reshape(shape)
    scaled = mixed * norm_gain[:, None, None, None] + norm_shift[:, None, None, None]
    return jnp.where(scaled >= 0, scaled, leak_slope * scaled).astype(jnp.bfloat16)

def reference(field, conv_first, norm_gain, norm_shift, conv_second):
    features = strided_first(field, conv_first)
    channels = features.shape[0]
    grouped = features.reshape(2, channels // 2, -1)
    average = lax.optimization_barrier(jnp.mean(grouped, axis=2))
    centered = grouped - average[:, :, None]
    covariance = jnp.einsum('gim,gjm->gij', centered, centered, precision=lax.Precision.HIGHEST) / centered.shape[2]
    covariance = covariance + epsilon * jnp.eye(channels // 2, dtype=covariance.dtype)[None]
    whitener = newton_whitener(covariance)
    activation = whiten(features, average, whitener, norm_gain, norm_shift)
    return same_second(activation, conv_second)
```

```python
import functools

import jax
import jax.numpy as jnp
from jax import lax
from jax.experimental import pallas as pl
from jax.experimental.pallas import tpu as pltpu
from jax.sharding import PartitionSpec as P

NEWTON = 5
EPSILON = 1e-05
LEAK = 0.2
F32, BF16 = jnp.float32, jnp.bfloat16
VMEM_LIMIT = 56 * 1024 * 1024


def dot(a, b, dims=((1,), (0,))):
    return lax.dot_general(a, b, (dims, ((), ())), preferred_element_type=F32)


def dot_full(a, b):
    return lax.dot_general(
        a, b, (((1,), (0,)), ((), ())), precision=lax.Precision.HIGHEST, preferred_element_type=F32
    )


def split(value):
    hi = value.astype(BF16)
    lo = (value - hi.astype(F32)).astype(BF16)
    return hi, lo


def iota(shape, dim):
    return lax.broadcasted_iota(jnp.int32, shape, dim)


def relayout_kernel(field_ref, cells_ref, yface_ref, xface_ref, rows_ref):
    cin, _, height, width = field_ref.shape
    half = width // 2
    rows_ref[...] = field_ref[:, 0].astype(F32).reshape(cin * height, width)
    out = iota((width, width), 0)
    source = jnp.where(out < half, 2 * out, 2 * (out - half) + 1)
    pick = (source == iota((width, width), 1)).astype(F32).astype(BF16)
    last = []
    for pair in range(height // 4):
        lines = [rows_ref[pl.ds(4 * pair + k, cin, stride=height), :] for k in range(4)]
        block = jnp.concatenate(lines, axis=0).astype(BF16)
        turned = dot(pick, block, ((1,), (1,)))
        for k in range(2):
            row = (2 * pair + k) * half
            lanes = slice(2 * cin * k, 2 * cin * (k + 1))
            even = turned[:half, lanes]
            odd = turned[half:, lanes]
            cells_ref[0, row : row + half, : 2 * cin] = even.astype(BF16)
            cells_ref[0, row : row + half, 2 * cin :] = odd.astype(BF16)
            last.append(odd[half - 1 :, :])
    yface_ref[0] = jnp.concatenate([even[:, cin:], odd[:, cin:]], axis=1).astype(BF16)
    xface_ref[0] = jnp.concatenate(last, axis=0).astype(BF16)


def relayout(field):
    cin, depth, height, width = field.shape
    half, rows = width // 2, height // 2 * (width // 2)
    return pl.pallas_call(
        relayout_kernel,
        grid=(depth,),
        in_specs=[pl.BlockSpec((cin, 1, height, width), lambda z: (0, z, 0, 0))],
        out_specs=[
            pl.BlockSpec((1, rows, 4 * cin), lambda z: (z, 0, 0)),
            pl.BlockSpec((1, half, 2 * cin), lambda z: (z, 0, 0)),
            pl.BlockSpec((1, height // 2, 2 * cin), lambda z: (z, 0, 0)),
        ],
        out_shape=[
            jax.ShapeDtypeStruct((depth, rows, 4 * cin), BF16),
            jax.ShapeDtypeStruct((depth, half, 2 * cin), BF16),
            jax.ShapeDtypeStruct((depth, height // 2, 2 * cin), BF16),
        ],
        scratch_shapes=[pltpu.VMEM((cin * height, width), F32)],
        compiler_params=pltpu.CompilerParams(vmem_limit_bytes=VMEM_LIMIT),
        name="relayout",
    )(field)


def features_kernel(
    cells_ref, zhalo_ref, yhalo_ref, xhalo_ref, w_ref, feat_ref, mom_ref, xface_ref, w4_ref, wy_ref, wx_ref, acc_ref
):
    depth = cells_ref.shape[0] // 2
    cin, cout = w_ref.shape[3:]
    rows = cells_ref.shape[1]
    half = yhalo_ref.shape[1]
    lines = rows // half
    w4_ref[...] = jnp.zeros(w4_ref.shape, BF16)
    wx_ref[...] = jnp.zeros(wx_ref.shape, BF16)
    wy_ref[...] = jnp.zeros(wy_ref.shape, BF16)
    for dz in range(3):
        for px in range(2):
            for py in range(2):
                k = (2 * px + py) * cin
                w4_ref[dz, k : k + cin, :cout] = w_ref[dz, 1 + py, 1 + px]
                if py == 1:
                    w4_ref[dz, k : k + cin, cout : 2 * cout] = w_ref[dz, 0, 1 + px]
                if px == 1:
                    w4_ref[dz, k : k + cin, 2 * cout : 3 * cout] = w_ref[dz, 1 + py, 0]
                if px == 1 and py == 1:
                    w4_ref[dz, k : k + cin, 3 * cout :] = w_ref[dz, 0, 0]
            k = (2 * dz + px) * cin
            wy_ref[k : k + cin, :cout] = w_ref[dz, 0, 1 + px]
        k = (2 * dz + 1) * cin
        wy_ref[k : k + cin, cout:] = w_ref[dz, 0, 0]
        k = 4 * dz * cin
        wx_ref[k : k + cin, :] = w_ref[dz, 1, 0]
        wx_ref[k + cin : k + 2 * cin, :] = w_ref[dz, 2, 0]
        wx_ref[k + 3 * cin : k + 4 * cin, :] = w_ref[dz, 0, 0]
    first = iota((half, cout), 0) == 0
    xh = xhalo_ref[...].astype(F32)
    total = jnp.zeros((1, cout), F32)
    for zo in range(depth):
        before = zhalo_ref[...] if zo == 0 else cells_ref[2 * zo - 1]
        acc_ref[...] = dot(
            jnp.concatenate([before, cells_ref[2 * zo], cells_ref[2 * zo + 1]], axis=1),
            w4_ref[...].reshape(3 * 4 * cin, 4 * cout),
        )
        ysum = dot(jnp.concatenate([yhalo_ref[2 * zo + dz] for dz in range(3)], axis=1), wy_ref[...])
        xparts = []
        for dz in range(3):
            xparts += [xh[2 * zo + dz, 1 : lines + 1], xh[2 * zo + dz, :lines]]
        xsum = dot(jnp.concatenate(xparts, axis=1).astype(BF16), wx_ref[...])
        for line in range(lines):
            here = pl.ds(line * half, half)
            straight = acc_ref[here, :cout]
            shifted = acc_ref[here, 2 * cout : 3 * cout]
            if line == 0:
                straight = straight + ysum[:, :cout]
                shifted = shifted + ysum[:, cout:]
            else:
                above = pl.ds((line - 1) * half, half)
                straight = straight + acc_ref[above, cout : 2 * cout]
                shifted = shifted + acc_ref[above, 3 * cout :]
            moved = jnp.where(first, xsum[line : line + 1], pltpu.roll(shifted, 1, 0))
            value = straight + moved
            feat_ref[zo, here, :] = value
            xface_ref[0, zo * lines + line : zo * lines + line + 1, :] = value[:1]
            xface_ref[1, zo * lines + line : zo * lines + line + 1, :] = value[half - 1 :]
            total = total + jnp.sum(value, axis=0, keepdims=True)
    count = depth * rows
    mean = total * (1.0 / count)
    gram = jnp.zeros((cout, 2 * cout), F32)
    for zo in range(depth):
        hi, lo = split(feat_ref[zo] - mean)
        gram = gram + dot(hi, jnp.concatenate([hi, lo], axis=1), ((0,), (0,)))
    cross = gram[:, cout:]
    gram = gram[:, :cout] + cross + cross.T
    eye = iota((cout, cout), 0) == iota((cout, cout), 1)
    column = jnp.sum(jnp.where(eye, jnp.broadcast_to(mean, (cout, cout)), 0.0), axis=1, keepdims=True)
    gram = gram + (column * mean) * float(count)
    left = iota((cout // 2, cout), 1) < cout // 2
    mom_ref[: cout // 2, :] = jnp.where(left, gram[: cout // 2], gram[cout // 2 :])
    mom_ref[cout // 2 :, :] = jnp.broadcast_to(total, (8, cout))


def features_of(cells, zhalo, yhalo, xhalo, weights):
    depth, rows, wide = cells.shape
    cin, cout = weights.shape[3:]
    half = yhalo.shape[1]
    vmem = pl.BlockSpec(memory_space=pltpu.VMEM)
    return pl.pallas_call(
        features_kernel,
        in_specs=[vmem] * 5,
        out_specs=[vmem] * 3,
        out_shape=[
            jax.ShapeDtypeStruct((depth // 2, rows, cout), F32),
            jax.ShapeDtypeStruct((cout // 2 + 8, cout), F32),
            jax.ShapeDtypeStruct((2, depth // 2 * rows // half, cout), F32),
        ],
        scratch_shapes=[
            pltpu.VMEM((3, wide, 4 * cout), BF16),
            pltpu.VMEM((6 * cin, 2 * cout), BF16),
            pltpu.VMEM((12 * cin, cout), BF16),
            pltpu.VMEM((rows, 4 * cout), F32),
        ],
        compiler_params=pltpu.CompilerParams(vmem_limit_bytes=VMEM_LIMIT),
        name="features",
    )(cells, zhalo, yhalo, xhalo, weights)


def block_kernel(
    total_cells,
    inside_ref, mom_ref, gain_ref, shift_ref, feat_ref, xb_ref, xa_ref, yb_ref, ya_ref, zb_ref, za_ref, w_ref,
    out_ref, pad_ref, wide_ref,
):
    depth, rows, cout = feat_ref.shape
    lines = xb_ref.shape[0] // depth
    half = rows // lines
    group = cout // 2
    square = (cout, cout)
    ri, ci = iota(square, 0), iota(square, 1)
    eye = ri == ci
    same = (ri < group) == (ci < group)
    moments = mom_ref[:group, :] * (1.0 / total_cells)
    average = mom_ref[group : group + 1, :] * (1.0 / total_cells)
    column = jnp.sum(jnp.where(eye, jnp.broadcast_to(average, square), 0.0), axis=1, keepdims=True)
    cov = jnp.concatenate([moments, moments], axis=0) - column * average
    cov = jnp.where(same, cov, 0.0) + jnp.where(eye, EPSILON, 0.0)
    diag = jnp.where(eye, cov, 0.0)
    trace0 = jnp.sum(jnp.sum(diag[:group], axis=1, keepdims=True), axis=0, keepdims=True)
    trace1 = jnp.sum(jnp.sum(diag[group:], axis=1, keepdims=True), axis=0, keepdims=True)
    trace = jnp.where(ri < group, trace0, trace1)
    scaled = cov / trace
    mat = jnp.where(eye, 1.5, 0.0) - 0.5 * scaled
    for _ in range(NEWTON - 1):
        mat = 1.5 * mat - 0.5 * dot_full(dot_full(mat, mat), dot_full(mat, scaled))
    gain = jnp.sum(jnp.where(eye, jnp.broadcast_to(gain_ref[...], square), 0.0), axis=1, keepdims=True)
    mat = mat / jnp.sqrt(trace) * gain
    hi, lo = split(mat)
    mixer = jnp.concatenate(
        [jnp.concatenate([hi, hi], axis=1), jnp.concatenate([lo, jnp.zeros_like(lo)], axis=1)], axis=0
    )
    shift = shift_ref[...]

    def whiten(value):
        hi, lo = split(value - average)
        both = dot(jnp.concatenate([hi, lo], axis=1), mixer, ((1,), (1,)))
        scaled = both[:, :cout] + both[:, cout:] + shift
        return jnp.where(scaled >= 0, scaled, LEAK * scaled)

    base = 8
    xb_in, xa_in, yb_in, ya_in, zb_in, za_in = (inside_ref[k] != 0 for k in range(6))

    def put(zp, yp, middle, ends, inside):
        left, right = ends
        pad_ref[zp, yp, base : base + half, :] = jnp.where(inside, middle, 0.0) if inside is not True else middle
        l_in = xb_in if inside is True else jnp.logical_and(xb_in, inside)
        r_in = xa_in if inside is True else jnp.logical_and(xa_in, inside)
        pad_ref[zp, yp, base - 1 : base, :] = jnp.where(l_in, left, 0.0)
        pad_ref[zp, yp, base + half : base + half + 1, :] = jnp.where(r_in, right, 0.0)

    xb, xa = whiten(xb_ref[...]), whiten(xa_ref[...])
    yb, ya = whiten(yb_ref[...]), whiten(ya_ref[...])
    for z in range(depth):
        plane = whiten(feat_ref[z])
        for y in range(lines):
            k = z * lines + y
            put(z + 1, y + 1, plane[y * half : (y + 1) * half], (xb[k : k + 1], xa[k : k + 1]), True)
        for yp, side, inside in ((0, yb, yb_in), (lines + 1, ya, ya_in)):
            k = depth * half + z
            put(z + 1, yp, side[z * half : (z + 1) * half], (side[k : k + 1], side[k + depth : k + depth + 1]), inside)
    for zp, ref, inside in ((0, zb_ref, zb_in), (depth + 1, za_ref, za_in)):
        plane = whiten(ref[...])
        ends = rows + 2 * half
        for y in range(lines):
            k = ends + y
            put(zp, y + 1, plane[y * half : (y + 1) * half], (plane[k : k + 1], plane[k + lines : k + lines + 1]), inside)
        for n, (yp, y_in) in enumerate(((0, yb_in), (lines + 1, ya_in))):
            k = ends + 2 * lines + 2 * n
            put(
                zp, yp, plane[rows + n * half : rows + (n + 1) * half], (plane[k : k + 1], plane[k + 1 : k + 2]),
                jnp.logical_and(inside, y_in),
            )
    for zp in range(depth + 2):
        for yp in range(lines + 2):
            for dx in range(3):
                wide_ref[zp, yp * half : (yp + 1) * half, dx * cout : (dx + 1) * cout] = pad_ref[
                    zp, yp, base - 1 + dx : base - 1 + dx + half, :
                ].astype(BF16)
    for z in range(depth):
        acc = jnp.zeros((rows, cout), F32)
        for dz in range(3):
            for dy in range(3):
                acc = acc + dot(wide_ref[z + dz, dy * half : dy * half + rows, :], w_ref[dz, dy])
        turned = jnp.stack([acc[y * half : (y + 1) * half].T for y in range(lines)], axis=0)
        out_ref[:, z] = jnp.swapaxes(turned, 0, 1).astype(BF16)


def block(total_cells, inside, moments, gain, shift, feats, xb, xa, yb, ya, zb, za, weights):
    depth, rows, cout = feats.shape
    lines = xb.shape[0] // depth
    half = rows // lines
    vmem = pl.BlockSpec(memory_space=pltpu.VMEM)
    return pl.pallas_call(
        functools.partial(block_kernel, total_cells),
        in_specs=[pl.BlockSpec(memory_space=pltpu.SMEM)] + [vmem] * 11,
        out_specs=vmem,
        out_shape=jax.ShapeDtypeStruct((cout, depth, lines, half), BF16),
        scratch_shapes=[
            pltpu.VMEM((depth + 2, lines + 2, half + 16, cout), F32),
            pltpu.VMEM((depth + 2, (lines + 2) * half, 3 * cout), BF16),
        ],
        compiler_params=pltpu.CompilerParams(vmem_limit_bytes=VMEM_LIMIT),
        name="block",
    )(inside, moments, gain, shift, feats, xb, xa, yb, ya, zb, za, weights)


def exchange(axis, moments, low, high):
    size = lax.axis_size(axis)
    if size == 1:
        return moments, jnp.zeros_like(low), jnp.zeros_like(high)
    if size & (size - 1):
        up = [(i, i + 1) for i in range(size - 1)]
        before = lax.ppermute(high, axis, up)
        after = lax.ppermute(low, axis, [(j, i) for i, j in up])
        return lax.psum(moments, axis), before, after
    even = lax.axis_index(axis) % 2 == 0
    count = moments.shape[0]
    swap = [(i, i ^ 1) for i in range(size)]
    got = lax.ppermute(jnp.concatenate([moments, jnp.where(even, high, low)], axis=0), axis, swap)
    moments, one = moments + got[:count], got[count:]
    if size == 2:
        return moments, one, one
    swap = [(i, (i + 1 if i % 2 else i - 1) % size) for i in range(size)]
    got = lax.ppermute(jnp.concatenate([moments, jnp.where(even, low, high)], axis=0), axis, swap)
    moments, two = moments + got[:count], got[count:]
    step = 4
    while step < size:
        moments = moments + lax.ppermute(moments, axis, [(i, (i + step) % size) for i in range(size)])
        step *= 2
    return moments, jnp.where(even, two, one), jnp.where(even, one, two)


def up_pairs(axis):
    return [(i, i + 1) for i in range(lax.axis_size(axis) - 1)]


def body(field, conv_first, norm_gain, norm_shift, conv_second):
    cin, depth_in, height_in, width_in = field.shape
    cout = conv_second.shape[-1]
    depth, lines, half = depth_in // 2, height_in // 2, width_in // 2
    cells, yface, xface = relayout(field)

    last = cells[-1]
    zhalo = lax.ppermute(last, "gz", up_pairs("gz"))
    yhalo = lax.ppermute(yface, "gy", up_pairs("gy"))
    nz = lax.axis_size("gz")
    diagonal = [(a * nz + b, (a + 1) * nz + b + 1) for a, _ in up_pairs("gy") for b, _ in up_pairs("gz")]
    yzhalo = lax.ppermute(yface[-1], ("gy", "gz"), diagonal)
    yhalo = jnp.concatenate([yzhalo[None], yhalo], axis=0)
    ztop = zhalo.reshape(lines, half, 4 * cin)[:, -1, 2 * cin :]
    xown = jnp.concatenate([ztop[None], xface], axis=0)
    ytop = yhalo[:, -1, cin:]
    ytop = jnp.concatenate([jnp.zeros_like(ytop), ytop], axis=1)
    xsend = jnp.concatenate([ytop[:, None], xown], axis=1)
    xsend = jnp.pad(xsend, ((0, 0), (0, (-xsend.shape[1]) % 16), (0, 0)))
    xhalo = lax.ppermute(xsend, "gx", up_pairs("gx"))

    feats, moments, faces = features_of(cells, zhalo, yhalo, xhalo, conv_first)
    rows = lines * half
    moments, xb, xa = exchange("gx", moments, faces[0], faces[1])
    xb3, xa3 = xb.reshape(depth, lines, cout), xa.reshape(depth, lines, cout)
    grid = feats.reshape(depth, lines, half, cout)

    def yside(y):
        return jnp.concatenate([grid[:, y].reshape(depth * half, cout), xb3[:, y], xa3[:, y]], axis=0)

    moments, yb, ya = exchange("gy", moments, yside(0), yside(lines - 1))

    def zside(z):
        k = depth * half + z
        own = [feats[z], yb[z * half : (z + 1) * half], ya[z * half : (z + 1) * half], xb3[z], xa3[z]]
        own += [yb[k : k + 1], yb[k + depth : k + depth + 1], ya[k : k + 1], ya[k + depth : k + depth + 1]]
        own += [jnp.zeros((4, cout), F32)]
        return jnp.concatenate(own, axis=0)

    moments, zb, za = exchange("gz", moments, zside(0), zside(depth - 1))
    inside = []
    for axis in ("gx", "gy", "gz"):
        place = lax.axis_index(axis)
        inside += [place > 0, place < lax.axis_size(axis) - 1]
    inside = jnp.stack(inside).astype(jnp.int32)
    total_cells = rows * depth * lax.axis_size("gx") * lax.axis_size("gy") * lax.axis_size("gz")
    return block(
        total_cells, inside, moments, norm_gain[None], norm_shift[None], feats, xb, xa, yb, ya, zb, za,
        conv_second.reshape(3, 3, 3 * cout, cout),
    )


def solution(mesh):
    in_specs = (P(None, "gz", "gy", "gx"), P(), P(), P(), P())
    out_specs = P(None, "gz", "gy", "gx")
    return jax.shard_map(body, mesh=mesh, in_specs=in_specs, out_specs=out_specs, check_vma=False)
```

```python
import functools

import jax
import jax.numpy as jnp
from jax import lax
from jax.experimental import pallas as pl
from jax.experimental.pallas import tpu as pltpu
from jax.sharding import PartitionSpec as P

NEWTON = 5
EPSILON = 1e-05
LEAK = 0.2
F32, BF16 = jnp.float32, jnp.bfloat16
MIB = 1024 * 1024


def dot(a, b, dims=((1,), (0,))):
    return lax.dot_general(a, b, (dims, ((), ())), preferred_element_type=F32)


def dot_full(a, b):
    return lax.dot_general(
        a, b, (((1,), (0,)), ((), ())), precision=lax.Precision.HIGHEST, preferred_element_type=F32
    )


def split(value):
    hi = value.astype(BF16)
    lo = (value - hi.astype(F32)).astype(BF16)
    return hi, lo


def iota(shape, dim):
    return lax.broadcasted_iota(jnp.int32, shape, dim)


def relayout_kernel(field_ref, cells_ref, yface_ref, xface_ref, rows_ref):
    cin, planes, height, width = field_ref.shape
    half = width // 2
    out = iota((width, width), 0)
    source = jnp.where(out < half, 2 * out, 2 * (out - half) + 1)
    pick = (source == iota((width, width), 1)).astype(F32).astype(BF16)
    for z in range(planes):
        rows_ref[z] = field_ref[:, z].astype(F32).reshape(cin * height, width)
        last = []
        for pair in range(height // 4):
            lines = [rows_ref[z, pl.ds(4 * pair + k, cin, stride=height), :] for k in range(4)]
            block = jnp.concatenate(lines, axis=0).astype(BF16)
            turned = dot(pick, block, ((1,), (1,)))
            for k in range(2):
                row = (2 * pair + k) * half
                lanes = slice(2 * cin * k, 2 * cin * (k + 1))
                even = turned[:half, lanes]
                odd = turned[half:, lanes]
                cells_ref[z, row : row + half, : 2 * cin] = even.astype(BF16)
                cells_ref[z, row : row + half, 2 * cin :] = odd.astype(BF16)
                last.append(odd[half - 1 :, :])
        yface_ref[z] = jnp.concatenate([even[:, cin:], odd[:, cin:]], axis=1).astype(BF16)
        xface_ref[z] = jnp.concatenate(last, axis=0).astype(BF16)


def relayout(field):
    cin, depth, height, width = field.shape
    half, rows = width // 2, height // 2 * (width // 2)
    step = 4 if depth % 4 == 0 else 1
    return pl.pallas_call(
        relayout_kernel,
        grid=(depth // step,),
        in_specs=[pl.BlockSpec((cin, step, height, width), lambda z: (0, z, 0, 0))],
        out_specs=[
            pl.BlockSpec((step, rows, 4 * cin), lambda z: (z, 0, 0)),
            pl.BlockSpec((step, half, 2 * cin), lambda z: (z, 0, 0)),
            pl.BlockSpec((step, height // 2, 2 * cin), lambda z: (z, 0, 0)),
        ],
        out_shape=[
            jax.ShapeDtypeStruct((depth, rows, 4 * cin), BF16),
            jax.ShapeDtypeStruct((depth, half, 2 * cin), BF16),
            jax.ShapeDtypeStruct((depth, height // 2, 2 * cin), BF16),
        ],
        scratch_shapes=[pltpu.VMEM((step, cin * height, width), F32)],
        compiler_params=pltpu.CompilerParams(vmem_limit_bytes=16 * MIB),
        name="relayout",
    )(field)


def features_kernel(
    cells_ref, zhalo_ref, yhalo_ref, xhalo_ref, w_ref, feat_ref, mom_ref, xface_ref, w4_ref, wy_ref, wx_ref, acc_ref
):
    depth = cells_ref.shape[0] // 2
    cin, cout = w_ref.shape[3:]
    rows = cells_ref.shape[1]
    half = yhalo_ref.shape[1]
    lines = rows // half
    w4_ref[...] = jnp.zeros(w4_ref.shape, BF16)
    wx_ref[...] = jnp.zeros(wx_ref.shape, BF16)
    wy_ref[...] = jnp.zeros(wy_ref.shape, BF16)
    for dz in range(3):
        for px in range(2):
            for py in range(2):
                k = (2 * px + py) * cin
                w4_ref[dz, k : k + cin, :cout] = w_ref[dz, 1 + py, 1 + px]
                if py == 1:
                    w4_ref[dz, k : k + cin, cout : 2 * cout] = w_ref[dz, 0, 1 + px]
                if px == 1:
                    w4_ref[dz, k : k + cin, 2 * cout : 3 * cout] = w_ref[dz, 1 + py, 0]
                if px == 1 and py == 1:
                    w4_ref[dz, k : k + cin, 3 * cout :] = w_ref[dz, 0, 0]
            k = (2 * dz + px) * cin
            wy_ref[k : k + cin, :cout] = w_ref[dz, 0, 1 + px]
        k = (2 * dz + 1) * cin
        wy_ref[k : k + cin, cout:] = w_ref[dz, 0, 0]
        k = 4 * dz * cin
        wx_ref[k : k + cin, :] = w_ref[dz, 1, 0]
        wx_ref[k + cin : k + 2 * cin, :] = w_ref[dz, 2, 0]
        wx_ref[k + 3 * cin : k + 4 * cin, :] = w_ref[dz, 0, 0]
    first = iota((half, cout), 0) == 0
    xh = xhalo_ref[...].astype(F32)
    total = jnp.zeros((1, cout), F32)
    for zo in range(depth):
        before = zhalo_ref[...] if zo == 0 else cells_ref[2 * zo - 1]
        acc_ref[...] = dot(
            jnp.concatenate([before, cells_ref[2 * zo], cells_ref[2 * zo + 1]], axis=1),
            w4_ref[...].reshape(3 * 4 * cin, 4 * cout),
        )
        ysum = dot(jnp.concatenate([yhalo_ref[2 * zo + dz] for dz in range(3)], axis=1), wy_ref[...])
        xparts = []
        for dz in range(3):
            xparts += [xh[2 * zo + dz, 1 : lines + 1], xh[2 * zo + dz, :lines]]
        xsum = dot(jnp.concatenate(xparts, axis=1).astype(BF16), wx_ref[...])
        for line in range(lines):
            here = pl.ds(line * half, half)
            straight = acc_ref[here, :cout]
            shifted = acc_ref[here, 2 * cout : 3 * cout]
            if line == 0:
                straight = straight + ysum[:, :cout]
                shifted = shifted + ysum[:, cout:]
            else:
                above = pl.ds((line - 1) * half, half)
                straight = straight + acc_ref[above, cout : 2 * cout]
                shifted = shifted + acc_ref[above, 3 * cout :]
            moved = jnp.where(first, xsum[line : line + 1], pltpu.roll(shifted, 1, 0))
            value = straight + moved
            feat_ref[zo, here, :] = value
            xface_ref[0, zo * lines + line : zo * lines + line + 1, :] = value[:1]
            xface_ref[1, zo * lines + line : zo * lines + line + 1, :] = value[half - 1 :]
            total = total + jnp.sum(value, axis=0, keepdims=True)
    count = depth * rows
    mean = total * (1.0 / count)
    gram = jnp.zeros((cout, 2 * cout), F32)
    for zo in range(depth):
        hi, lo = split(feat_ref[zo] - mean)
        gram = gram + dot(hi, jnp.concatenate([hi, lo], axis=1), ((0,), (0,)))
    cross = gram[:, cout:]
    gram = gram[:, :cout] + cross + cross.T
    eye = iota((cout, cout), 0) == iota((cout, cout), 1)
    column = jnp.sum(jnp.where(eye, jnp.broadcast_to(mean, (cout, cout)), 0.0), axis=1, keepdims=True)
    gram = gram + (column * mean) * float(count)
    left = iota((cout // 2, cout), 1) < cout // 2
    mom_ref[: cout // 2, :] = jnp.where(left, gram[: cout // 2], gram[cout // 2 :])
    mom_ref[cout // 2 :, :] = jnp.broadcast_to(total, (8, cout))


def features_of(cells, zhalo, yhalo, xhalo, weights):
    depth, rows, wide = cells.shape
    cin, cout = weights.shape[3:]
    half = yhalo.shape[1]
    vmem = pl.BlockSpec(memory_space=pltpu.VMEM)
    return pl.pallas_call(
        features_kernel,
        in_specs=[vmem] * 5,
        out_specs=[vmem] * 3,
        out_shape=[
            jax.ShapeDtypeStruct((depth // 2, rows, cout), F32),
            jax.ShapeDtypeStruct((cout // 2 + 8, cout), F32),
            jax.ShapeDtypeStruct((2, depth // 2 * rows // half, cout), F32),
        ],
        scratch_shapes=[
            pltpu.VMEM((3, wide, 4 * cout), BF16),
            pltpu.VMEM((6 * cin, 2 * cout), BF16),
            pltpu.VMEM((12 * cin, cout), BF16),
            pltpu.VMEM((rows, 4 * cout), F32),
        ],
        compiler_params=pltpu.CompilerParams(vmem_limit_bytes=20 * MIB),
        name="features",
    )(cells, zhalo, yhalo, xhalo, weights)


def block_kernel(
    total_cells,
    place_ref, mom_ref, gain_ref, shift_ref, feat_ref, z1_ref, z2_ref, y1_ref, y2_ref, x1_ref, x2_ref, w_ref,
    out_ref, pad_ref, wide_ref,
):
    depth, rows, cout = feat_ref.shape
    half = y1_ref.shape[0] // (depth + 2)
    lines = rows // half
    group = cout // 2
    square = (cout, cout)
    ri, ci = iota(square, 0), iota(square, 1)
    eye = ri == ci
    same = (ri < group) == (ci < group)
    moments = mom_ref[:group, :] * (1.0 / total_cells)
    average = mom_ref[group : group + 1, :] * (1.0 / total_cells)
    column = jnp.sum(jnp.where(eye, jnp.broadcast_to(average, square), 0.0), axis=1, keepdims=True)
    cov = jnp.concatenate([moments, moments], axis=0) - column * average
    cov = jnp.where(same, cov, 0.0) + jnp.where(eye, EPSILON, 0.0)
    diag = jnp.where(eye, cov, 0.0)
    trace0 = jnp.sum(jnp.sum(diag[:group], axis=1, keepdims=True), axis=0, keepdims=True)
    trace1 = jnp.sum(jnp.sum(diag[group:], axis=1, keepdims=True), axis=0, keepdims=True)
    trace = jnp.where(ri < group, trace0, trace1)
    scaled = cov / trace
    mat = jnp.where(eye, 1.5, 0.0) - 0.5 * scaled
    for _ in range(NEWTON - 1):
        mat = 1.5 * mat - 0.5 * dot_full(dot_full(mat, mat), dot_full(mat, scaled))
    gain = jnp.sum(jnp.where(eye, jnp.broadcast_to(gain_ref[...], square), 0.0), axis=1, keepdims=True)
    mat = mat / jnp.sqrt(trace) * gain
    hi, lo = split(mat)
    mixer = jnp.concatenate(
        [jnp.concatenate([hi, hi], axis=1), jnp.concatenate([lo, jnp.zeros_like(lo)], axis=1)], axis=0
    )
    shift = shift_ref[...]

    def whiten(value):
        hi, lo = split(value - average)
        both = dot(jnp.concatenate([hi, lo], axis=1), mixer, ((1,), (1,)))
        scaled = both[:, :cout] + both[:, cout:] + shift
        return jnp.where(scaled >= 0, scaled, LEAK * scaled)

    base = 8
    x_even, y_even, z_even, xb_in, xa_in, yb_in, ya_in, zb_in, za_in = (place_ref[k] != 0 for k in range(9))

    def sides(even, one_ref, two_ref):
        one, two = one_ref[...], two_ref[...]
        return whiten(jnp.where(even, two, one)), whiten(jnp.where(even, one, two))

    def put(zp, yp, middle, left, right, inside):
        l_in, r_in = xb_in, xa_in
        if inside is not None:
            middle = jnp.where(inside, middle, 0.0)
            l_in, r_in = jnp.logical_and(l_in, inside), jnp.logical_and(r_in, inside)
        pad_ref[zp, yp, base : base + half, :] = middle
        pad_ref[zp, yp, base - 1 : base, :] = jnp.where(l_in, left, 0.0)
        pad_ref[zp, yp, base + half : base + half + 1, :] = jnp.where(r_in, right, 0.0)

    zsides = sides(z_even, z1_ref, z2_ref)
    ysides = sides(y_even, y1_ref, y2_ref)
    xsides = sides(x_even, x1_ref, x2_ref)
    spots = [(z + 1, None) for z in range(depth)] + [(0, zb_in), (depth + 1, za_in)]
    for n, (zp, z_in) in enumerate(spots):
        plane = whiten(feat_ref[n]) if n < depth else zsides[n - depth]
        for y in range(lines):
            k = n * lines + y
            put(zp, y + 1, plane[y * half : (y + 1) * half], xsides[0][k : k + 1], xsides[1][k : k + 1], z_in)
        for m, (yp, y_in) in enumerate(((0, yb_in), (lines + 1, ya_in))):
            k = (depth + 2) * (lines + m) + n
            inside = y_in if z_in is None else jnp.logical_and(z_in, y_in)
            put(zp, yp, ysides[m][n * half : (n + 1) * half], xsides[0][k : k + 1], xsides[1][k : k + 1], inside)
    for zp in range(depth + 2):
        for yp in range(lines + 2):
            for dx in range(3):
                wide_ref[zp, yp * half : (yp + 1) * half, dx * cout : (dx + 1) * cout] = pad_ref[
                    zp, yp, base - 1 + dx : base - 1 + dx + half, :
                ].astype(BF16)
    for z in range(depth):
        acc = jnp.zeros((rows, cout), F32)
        for dz in range(3):
            for dy in range(3):
                acc = acc + dot(wide_ref[z + dz, dy * half : dy * half + rows, :], w_ref[dz, dy])
        out_ref[z] = acc.astype(BF16)


def block(total_cells, place, moments, gain, shift, feats, zs, ys, xs, weights):
    depth, rows, cout = feats.shape
    half = ys[0].shape[0] // (depth + 2)
    lines = rows // half
    vmem = pl.BlockSpec(memory_space=pltpu.VMEM)
    return pl.pallas_call(
        functools.partial(block_kernel, total_cells),
        in_specs=[pl.BlockSpec(memory_space=pltpu.SMEM)] + [vmem] * 11,
        out_specs=vmem,
        out_shape=jax.ShapeDtypeStruct((depth, rows, cout), BF16),
        scratch_shapes=[
            pltpu.VMEM((depth + 2, lines + 2, half + 16, cout), F32),
            pltpu.VMEM((depth + 2, (lines + 2) * half, 3 * cout), BF16),
        ],
        compiler_params=pltpu.CompilerParams(vmem_limit_bytes=24 * MIB),
        name="block",
    )(place, moments, gain, shift, feats, *zs, *ys, *xs, weights)


def power_of_two(size):
    return size & (size - 1) == 0


def first_pairs(axis):
    return [(i, i ^ 1) for i in range(lax.axis_size(axis))]


def second_pairs(axis):
    size = lax.axis_size(axis)
    return [(i, (i + 1 if i % 2 else i - 1) % size) for i in range(size)]


def is_even(axis):
    size = lax.axis_size(axis)
    return lax.axis_index(axis) % 2 == 0 if size > 1 and power_of_two(size) else jnp.bool_(True)


def faces(axis, low, high):
    size = lax.axis_size(axis)
    if size == 1:
        return low, high
    if not power_of_two(size):
        up = up_pairs(axis)
        return lax.ppermute(low, axis, [(j, i) for i, j in up]), lax.ppermute(high, axis, up)
    even = is_even(axis)
    one = lax.ppermute(jnp.where(even, high, low), axis, first_pairs(axis))
    if size == 2:
        return one, one
    inner = [(i, j) for i, j in second_pairs(axis) if abs(i - j) == 1]
    return one, lax.ppermute(jnp.where(even, low, high), axis, inner)


def added(axis, value):
    size = lax.axis_size(axis)
    if size == 1:
        return value
    if not power_of_two(size):
        return lax.psum(value, axis)
    value = value + lax.ppermute(value, axis, first_pairs(axis))
    if size > 2:
        value = value + lax.ppermute(value, axis, second_pairs(axis))
    step = 4
    while step < size:
        value = value + lax.ppermute(value, axis, [(i, (i + step) % size) for i in range(size)])
        step *= 2
    return value


def sided(even, pair):
    one, two = pair
    return jnp.where(even, two, one), jnp.where(even, one, two)


def up_pairs(axis):
    return [(i, i + 1) for i in range(lax.axis_size(axis) - 1)]


def body(field, conv_first, norm_gain, norm_shift, conv_second):
    cin, depth_in, height_in, width_in = field.shape
    cout = conv_second.shape[-1]
    depth, lines, half = depth_in // 2, height_in // 2, width_in // 2
    cells, yface, xface = relayout(field)

    last = cells[-1]
    zhalo = lax.ppermute(last, "gz", up_pairs("gz"))
    yhalo = lax.ppermute(yface, "gy", up_pairs("gy"))
    nz = lax.axis_size("gz")
    diagonal = [(a * nz + b, (a + 1) * nz + b + 1) for a, _ in up_pairs("gy") for b, _ in up_pairs("gz")]
    yzhalo = lax.ppermute(yface[-1], ("gy", "gz"), diagonal)
    yhalo = jnp.concatenate([yzhalo[None], yhalo], axis=0)
    ztop = zhalo.reshape(lines, half, 4 * cin)[:, -1, 2 * cin :]
    xown = jnp.concatenate([ztop[None], xface], axis=0)
    ytop = yhalo[:, -1, cin:]
    ytop = jnp.concatenate([jnp.zeros_like(ytop), ytop], axis=1)
    xsend = jnp.concatenate([ytop[:, None], xown], axis=1)
    xsend = jnp.pad(xsend, ((0, 0), (0, (-xsend.shape[1]) % 16), (0, 0)))
    xhalo = lax.ppermute(xsend, "gx", up_pairs("gx"))

    feats, moments, xfaces = features_of(cells, zhalo, yhalo, xhalo, conv_first)
    rows = lines * half
    zs = faces("gz", feats[0], feats[-1])
    moments = added("gz", moments)
    zsides = sided(is_even("gz"), zs)

    def yside(y):
        here = slice(y * half, (y + 1) * half)
        return jnp.concatenate([feats[z, here] for z in range(depth)] + [side[here] for side in zsides], axis=0)

    ys = faces("gy", yside(0), yside(lines - 1))
    moments = added("gy", moments)
    ysides = sided(is_even("gy"), ys)

    def xside(n, x):
        own = [xfaces[n]] + [side.reshape(-1, half, cout)[:, x] for side in zsides + ysides]
        return jnp.concatenate(own, axis=0)

    low, high = xside(0, 0), xside(1, half - 1)
    if lax.axis_size("gx") == 2:
        count = moments.shape[0]
        both = jnp.concatenate([moments, jnp.where(is_even("gx"), high, low)], axis=0)
        both = lax.ppermute(both, "gx", first_pairs("gx"))
        moments = moments + both[:count]
        xs = (both[count:], both[count:])
    else:
        xs = faces("gx", low, high)
        moments = added("gx", moments)
    place = [is_even(axis) for axis in ("gx", "gy", "gz")]
    for axis in ("gx", "gy", "gz"):
        place += [lax.axis_index(axis) > 0, lax.axis_index(axis) < lax.axis_size(axis) - 1]
    place = jnp.stack(place).astype(jnp.int32)
    total_cells = rows * depth * lax.axis_size("gx") * lax.axis_size("gy") * lax.axis_size("gz")
    result = block(
        total_cells, place, moments, norm_gain[None], norm_shift[None], feats, zs, ys, xs,
        conv_second.reshape(3, 3, 3 * cout, cout),
    )
    return jnp.transpose(result.reshape(depth, lines, half, cout), (3, 0, 1, 2))


def solution(mesh):
    in_specs = (P(None, "gz", "gy", "gx"), P(), P(), P(), P())
    out_specs = P(None, "gz", "gy", "gx")
    return jax.shard_map(body, mesh=mesh, in_specs=in_specs, out_specs=out_specs, check_vma=False)
```

```python
import functools

import jax
import jax.numpy as jnp
from jax import lax
from jax.experimental import pallas as pl
from jax.experimental.pallas import tpu as pltpu
from jax.sharding import PartitionSpec as P

NEWTON = 5
EPSILON = 1e-05
LEAK = 0.2
F32, BF16 = jnp.float32, jnp.bfloat16
MIB = 1024 * 1024


def dot(a, b, dims=((1,), (0,))):
    return lax.dot_general(a, b, (dims, ((), ())), preferred_element_type=F32)


def dot_full(a, b):
    return lax.dot_general(
        a, b, (((1,), (0,)), ((), ())), precision=lax.Precision.HIGHEST, preferred_element_type=F32
    )


def split(value):
    hi = value.astype(BF16)
    lo = (value - hi.astype(F32)).astype(BF16)
    return hi, lo


def iota(shape, dim):
    return lax.broadcasted_iota(jnp.int32, shape, dim)


def relayout_kernel(field_ref, cells_ref, yface_ref, xface_ref, rows_ref):
    cin, planes, height, width = field_ref.shape
    half = width // 2
    out = iota((width, width), 0)
    source = jnp.where(out < half, 2 * out, 2 * (out - half) + 1)
    pick = (source == iota((width, width), 1)).astype(F32).astype(BF16)
    for z in range(planes):
        rows_ref[z] = field_ref[:, z].astype(F32).reshape(cin * height, width)
        last = []
        for pair in range(height // 4):
            lines = [rows_ref[z, pl.ds(4 * pair + k, cin, stride=height), :] for k in range(4)]
            block = jnp.concatenate(lines, axis=0).astype(BF16)
            turned = dot(pick, block, ((1,), (1,)))
            for k in range(2):
                row = (2 * pair + k) * half
                lanes = slice(2 * cin * k, 2 * cin * (k + 1))
                even = turned[:half, lanes]
                odd = turned[half:, lanes]
                cells_ref[z, row : row + half, : 2 * cin] = even.astype(BF16)
                cells_ref[z, row : row + half, 2 * cin :] = odd.astype(BF16)
                last.append(odd[half - 1 :, :])
        yface_ref[z] = jnp.concatenate([even[:, cin:], odd[:, cin:]], axis=1).astype(BF16)
        xface_ref[z] = jnp.concatenate(last, axis=0).astype(BF16)


def relayout(field):
    cin, depth, height, width = field.shape
    half, rows = width // 2, height // 2 * (width // 2)
    step = 4 if depth % 4 == 0 else 1
    return pl.pallas_call(
        relayout_kernel,
        grid=(depth // step,),
        in_specs=[pl.BlockSpec((cin, step, height, width), lambda z: (0, z, 0, 0))],
        out_specs=[
            pl.BlockSpec((step, rows, 4 * cin), lambda z: (z, 0, 0)),
            pl.BlockSpec((step, half, 2 * cin), lambda z: (z, 0, 0)),
            pl.BlockSpec((step, height // 2, 2 * cin), lambda z: (z, 0, 0)),
        ],
        out_shape=[
            jax.ShapeDtypeStruct((depth, rows, 4 * cin), BF16),
            jax.ShapeDtypeStruct((depth, half, 2 * cin), BF16),
            jax.ShapeDtypeStruct((depth, height // 2, 2 * cin), BF16),
        ],
        scratch_shapes=[pltpu.VMEM((step, cin * height, width), F32)],
        compiler_params=pltpu.CompilerParams(vmem_limit_bytes=16 * MIB),
        name="relayout",
    )(field)


def features_kernel(
    place_ref, cells_ref, zhalo_ref, yhalo_ref, yzhalo_ref, xhalo_ref, xzhalo_ref, w_ref,
    feat_ref, mom_ref, xface_ref, w4_ref, wy_ref, wx_ref, acc_ref,
):
    depth = cells_ref.shape[0] // 2
    cin, cout = w_ref.shape[3:]
    rows = cells_ref.shape[1]
    lines = xhalo_ref.shape[0] // (2 * depth)
    half = rows // lines
    y_in, z_in = place_ref[5] != 0, place_ref[7] != 0
    zhalo = jnp.where(z_in, zhalo_ref[...], jnp.zeros(zhalo_ref.shape, BF16))
    yrest = yhalo_ref[2 * depth * half :, :].astype(F32)
    yhalo = [yzhalo_ref[:half, :]] + [yhalo_ref[z * half : (z + 1) * half, :] for z in range(2 * depth)]
    yhalo = [jnp.where(y_in, value, jnp.zeros_like(value)) for value in yhalo]
    yhalo[0] = jnp.where(z_in, yhalo[0], jnp.zeros_like(yhalo[0]))
    corner = jnp.where(jnp.logical_and(y_in, z_in), yzhalo_ref[half:, :].astype(F32)[:1], 0.0)
    yrest = jnp.where(y_in, yrest, 0.0)
    here = [jnp.where(z_in, xzhalo_ref[...].astype(F32)[:lines], 0.0)]
    here += [xhalo_ref[...].astype(F32)[z * lines : (z + 1) * lines] for z in range(2 * depth)]
    over = [corner] + [yrest[z : z + 1] for z in range(2 * depth)]
    over = [jnp.concatenate([line, value[: lines - 1]], axis=0) for line, value in zip(over, here, strict=True)]
    w4_ref[...] = jnp.zeros(w4_ref.shape, BF16)
    wx_ref[...] = jnp.zeros(wx_ref.shape, BF16)
    wy_ref[...] = jnp.zeros(wy_ref.shape, BF16)
    for dz in range(3):
        for px in range(2):
            for py in range(2):
                k = (2 * px + py) * cin
                w4_ref[dz, k : k + cin, :cout] = w_ref[dz, 1 + py, 1 + px]
                if py == 1:
                    w4_ref[dz, k : k + cin, cout : 2 * cout] = w_ref[dz, 0, 1 + px]
                if px == 1:
                    w4_ref[dz, k : k + cin, 2 * cout : 3 * cout] = w_ref[dz, 1 + py, 0]
                if px == 1 and py == 1:
                    w4_ref[dz, k : k + cin, 3 * cout :] = w_ref[dz, 0, 0]
            k = (2 * dz + px) * cin
            wy_ref[k : k + cin, :cout] = w_ref[dz, 0, 1 + px]
        k = (2 * dz + 1) * cin
        wy_ref[k : k + cin, cout:] = w_ref[dz, 0, 0]
        k = 4 * dz * cin
        wx_ref[k : k + cin, :] = w_ref[dz, 1, 0]
        wx_ref[k + cin : k + 2 * cin, :] = w_ref[dz, 2, 0]
        wx_ref[k + 3 * cin : k + 4 * cin, :] = w_ref[dz, 0, 0]
    first = iota((half, cout), 0) == 0
    total = jnp.zeros((1, cout), F32)
    for zo in range(depth):
        before = zhalo if zo == 0 else cells_ref[2 * zo - 1]
        acc_ref[...] = dot(
            jnp.concatenate([before, cells_ref[2 * zo], cells_ref[2 * zo + 1]], axis=1),
            w4_ref[...].reshape(3 * 4 * cin, 4 * cout),
        )
        ysum = dot(jnp.concatenate(yhalo[2 * zo : 2 * zo + 3], axis=1), wy_ref[...])
        xparts = []
        for dz in range(3):
            xparts += [here[2 * zo + dz], over[2 * zo + dz]]
        xsum = dot(jnp.concatenate(xparts, axis=1).astype(BF16), wx_ref[...])
        for line in range(lines):
            span = pl.ds(line * half, half)
            straight = acc_ref[span, :cout]
            shifted = acc_ref[span, 2 * cout : 3 * cout]
            if line == 0:
                straight = straight + ysum[:, :cout]
                shifted = shifted + ysum[:, cout:]
            else:
                above = pl.ds((line - 1) * half, half)
                straight = straight + acc_ref[above, cout : 2 * cout]
                shifted = shifted + acc_ref[above, 3 * cout :]
            moved = jnp.where(first, xsum[line : line + 1], pltpu.roll(shifted, 1, 0))
            value = straight + moved
            feat_ref[zo, span, :] = value
            xface_ref[0, zo * lines + line : zo * lines + line + 1, :] = value[:1]
            xface_ref[1, zo * lines + line : zo * lines + line + 1, :] = value[half - 1 :]
            total = total + jnp.sum(value, axis=0, keepdims=True)
    count = depth * rows
    mean = total * (1.0 / count)
    gram = jnp.zeros((cout, 2 * cout), F32)
    for zo in range(depth):
        hi, lo = split(feat_ref[zo] - mean)
        gram = gram + dot(hi, jnp.concatenate([hi, lo], axis=1), ((0,), (0,)))
    cross = gram[:, cout:]
    gram = gram[:, :cout] + cross + cross.T
    eye = iota((cout, cout), 0) == iota((cout, cout), 1)
    column = jnp.sum(jnp.where(eye, jnp.broadcast_to(mean, (cout, cout)), 0.0), axis=1, keepdims=True)
    gram = gram + (column * mean) * float(count)
    left = iota((cout // 2, cout), 1) < cout // 2
    mom_ref[: cout // 2, :] = jnp.where(left, gram[: cout // 2], gram[cout // 2 :])
    mom_ref[cout // 2 :, :] = jnp.broadcast_to(total, (8, cout))


def features_of(place, cells, zhalo, yhalo, yzhalo, xhalo, xzhalo, weights):
    depth, rows, wide = cells.shape
    cin, cout = weights.shape[3:]
    lines = xhalo.shape[0] // depth
    vmem = pl.BlockSpec(memory_space=pltpu.VMEM)
    return pl.pallas_call(
        features_kernel,
        in_specs=[pl.BlockSpec(memory_space=pltpu.SMEM)] + [vmem] * 7,
        out_specs=[vmem] * 3,
        out_shape=[
            jax.ShapeDtypeStruct((depth // 2, rows, cout), F32),
            jax.ShapeDtypeStruct((cout // 2 + 8, cout), F32),
            jax.ShapeDtypeStruct((2, depth // 2 * lines, cout), F32),
        ],
        scratch_shapes=[
            pltpu.VMEM((3, wide, 4 * cout), BF16),
            pltpu.VMEM((6 * cin, 2 * cout), BF16),
            pltpu.VMEM((12 * cin, cout), BF16),
            pltpu.VMEM((rows, 4 * cout), F32),
        ],
        compiler_params=pltpu.CompilerParams(vmem_limit_bytes=20 * MIB),
        name="features",
    )(place, cells, zhalo, yhalo, yzhalo, xhalo, xzhalo, weights)


def block_kernel(
    total_cells,
    place_ref, mom_ref, gain_ref, shift_ref, feat_ref, z1_ref, z2_ref, y1_ref, y2_ref, x1_ref, x2_ref, w_ref,
    out_ref, pad_ref, wide_ref,
):
    depth, rows, cout = feat_ref.shape
    half = y1_ref.shape[0] // (depth + 2)
    lines = rows // half
    group = cout // 2
    square = (cout, cout)
    ri, ci = iota(square, 0), iota(square, 1)
    eye = ri == ci
    same = (ri < group) == (ci < group)
    moments = mom_ref[:group, :] * (1.0 / total_cells)
    average = mom_ref[group : group + 1, :] * (1.0 / total_cells)
    column = jnp.sum(jnp.where(eye, jnp.broadcast_to(average, square), 0.0), axis=1, keepdims=True)
    cov = jnp.concatenate([moments, moments], axis=0) - column * average
    cov = jnp.where(same, cov, 0.0) + jnp.where(eye, EPSILON, 0.0)
    diag = jnp.where(eye, cov, 0.0)
    trace0 = jnp.sum(jnp.sum(diag[:group], axis=1, keepdims=True), axis=0, keepdims=True)
    trace1 = jnp.sum(jnp.sum(diag[group:], axis=1, keepdims=True), axis=0, keepdims=True)
    trace = jnp.where(ri < group, trace0, trace1)
    scaled = cov / trace
    mat = jnp.where(eye, 1.5, 0.0) - 0.5 * scaled
    for _ in range(NEWTON - 1):
        mat = 1.5 * mat - 0.5 * dot_full(dot_full(mat, mat), dot_full(mat, scaled))
    gain = jnp.sum(jnp.where(eye, jnp.broadcast_to(gain_ref[...], square), 0.0), axis=1, keepdims=True)
    mat = mat / jnp.sqrt(trace) * gain
    hi, lo = split(mat)
    mixer = jnp.concatenate(
        [jnp.concatenate([hi, hi], axis=1), jnp.concatenate([lo, jnp.zeros_like(lo)], axis=1)], axis=0
    )
    shift = shift_ref[...]

    def whiten(value):
        hi, lo = split(value - average)
        both = dot(jnp.concatenate([hi, lo], axis=1), mixer, ((1,), (1,)))
        scaled = both[:, :cout] + both[:, cout:] + shift
        return jnp.where(scaled >= 0, scaled, LEAK * scaled)

    base = 8
    x_even, y_even, z_even, xb_in, xa_in, yb_in, ya_in, zb_in, za_in = (place_ref[k] != 0 for k in range(9))

    def sides(even, one_ref, two_ref):
        one, two = one_ref[...], two_ref[...]
        return whiten(jnp.where(even, two, one)), whiten(jnp.where(even, one, two))

    def put(zp, yp, middle, left, right, inside):
        l_in, r_in = xb_in, xa_in
        if inside is not None:
            middle = jnp.where(inside, middle, 0.0)
            l_in, r_in = jnp.logical_and(l_in, inside), jnp.logical_and(r_in, inside)
        pad_ref[zp, yp, base : base + half, :] = middle
        pad_ref[zp, yp, base - 1 : base, :] = jnp.where(l_in, left, 0.0)
        pad_ref[zp, yp, base + half : base + half + 1, :] = jnp.where(r_in, right, 0.0)

    zsides = sides(z_even, z1_ref, z2_ref)
    ysides = sides(y_even, y1_ref, y2_ref)
    xsides = sides(x_even, x1_ref, x2_ref)
    spots = [(z + 1, None) for z in range(depth)] + [(0, zb_in), (depth + 1, za_in)]
    for n, (zp, z_in) in enumerate(spots):
        plane = whiten(feat_ref[n]) if n < depth else zsides[n - depth]
        for y in range(lines):
            k = n * lines + y
            put(zp, y + 1, plane[y * half : (y + 1) * half], xsides[0][k : k + 1], xsides[1][k : k + 1], z_in)
        for m, (yp, y_in) in enumerate(((0, yb_in), (lines + 1, ya_in))):
            k = (depth + 2) * (lines + m) + n
            inside = y_in if z_in is None else jnp.logical_and(z_in, y_in)
            put(zp, yp, ysides[m][n * half : (n + 1) * half], xsides[0][k : k + 1], xsides[1][k : k + 1], inside)
    for zp in range(depth + 2):
        for yp in range(lines + 2):
            for dx in range(3):
                wide_ref[zp, yp * half : (yp + 1) * half, dx * cout : (dx + 1) * cout] = pad_ref[
                    zp, yp, base - 1 + dx : base - 1 + dx + half, :
                ].astype(BF16)
    for z in range(depth):
        acc = jnp.zeros((rows, cout), F32)
        for dz in range(3):
            for dy in range(3):
                acc = acc + dot(wide_ref[z + dz, dy * half : dy * half + rows, :], w_ref[dz, dy])
        out_ref[z] = acc.astype(BF16)


def block(total_cells, place, moments, gain, shift, feats, zs, ys, xs, weights):
    depth, rows, cout = feats.shape
    half = ys[0].shape[0] // (depth + 2)
    lines = rows // half
    vmem = pl.BlockSpec(memory_space=pltpu.VMEM)
    return pl.pallas_call(
        functools.partial(block_kernel, total_cells),
        in_specs=[pl.BlockSpec(memory_space=pltpu.SMEM)] + [vmem] * 11,
        out_specs=vmem,
        out_shape=jax.ShapeDtypeStruct((depth, rows, cout), BF16),
        scratch_shapes=[
            pltpu.VMEM((depth + 2, lines + 2, half + 16, cout), F32),
            pltpu.VMEM((depth + 2, (lines + 2) * half, 3 * cout), BF16),
        ],
        compiler_params=pltpu.CompilerParams(vmem_limit_bytes=24 * MIB),
        name="block",
    )(place, moments, gain, shift, feats, *zs, *ys, *xs, weights)


def power_of_two(size):
    return size & (size - 1) == 0


def first_pairs(axis):
    return [(i, i ^ 1) for i in range(lax.axis_size(axis))]


def second_pairs(axis):
    size = lax.axis_size(axis)
    return [(i, (i + 1 if i % 2 else i - 1) % size) for i in range(size)]


def is_even(axis):
    size = lax.axis_size(axis)
    return lax.axis_index(axis) % 2 == 0 if size > 1 and power_of_two(size) else jnp.bool_(True)


def faces(axis, low, high):
    size = lax.axis_size(axis)
    if size == 1:
        return low, high
    if not power_of_two(size):
        up = up_pairs(axis)
        return lax.ppermute(low, axis, [(j, i) for i, j in up]), lax.ppermute(high, axis, up)
    even = is_even(axis)
    one = lax.ppermute(jnp.where(even, high, low), axis, first_pairs(axis))
    if size == 2:
        return one, one
    inner = [(i, j) for i, j in second_pairs(axis) if abs(i - j) == 1]
    return one, lax.ppermute(jnp.where(even, low, high), axis, inner)


def added(axis, value, first=True):
    size = lax.axis_size(axis)
    if size == 1:
        return value
    if not power_of_two(size):
        return lax.psum(value, axis)
    if first:
        value = value + lax.ppermute(value, axis, first_pairs(axis))
    if size > 2:
        value = value + lax.ppermute(value, axis, second_pairs(axis))
    step = 4
    while step < size:
        value = value + lax.ppermute(value, axis, [(i, (i + step) % size) for i in range(size)])
        step *= 2
    return value


def added_with_faces(axis, value, low, high):
    size = lax.axis_size(axis)
    if size == 1 or not power_of_two(size):
        return added(axis, value), faces(axis, low, high)
    even, count = is_even(axis), value.shape[0]
    both = jnp.concatenate([value, jnp.where(even, high, low)], axis=0)
    both = lax.ppermute(both, axis, first_pairs(axis))
    value, one = value + both[:count], both[count:]
    if size == 2:
        return value, (one, one)
    inner = [(i, j) for i, j in second_pairs(axis) if abs(i - j) == 1]
    two = lax.ppermute(jnp.where(even, low, high), axis, inner)
    return added(axis, value, first=False), (one, two)


def sided(even, pair):
    one, two = pair
    return jnp.where(even, two, one), jnp.where(even, one, two)


def up_pairs(axis):
    return [(i, i + 1) for i in range(lax.axis_size(axis) - 1)]


def ring(axis):
    size = lax.axis_size(axis)
    return [(i, (i + 1) % size) for i in range(size)]


def stacked(parts):
    count = sum(part.shape[0] for part in parts)
    fill = jnp.zeros((-count % 16, parts[0].shape[1]), parts[0].dtype)
    return jnp.concatenate(parts + [fill], axis=0)


def body(field, conv_first, norm_gain, norm_shift, conv_second):
    cin, depth_in, height_in, width_in = field.shape
    cout = conv_second.shape[-1]
    depth, lines, half = depth_in // 2, height_in // 2, width_in // 2
    cells, yface, xface = relayout(field)

    place = [is_even(axis) for axis in ("gx", "gy", "gz")]
    for axis in ("gx", "gy", "gz"):
        place += [lax.axis_index(axis) > 0, lax.axis_index(axis) < lax.axis_size(axis) - 1]
    place = jnp.stack(place).astype(jnp.int32)
    zhalo = lax.ppermute(cells[-1], "gz", ring("gz"))
    xhalo = lax.ppermute(xface.reshape(depth_in * lines, 2 * cin), "gx", ring("gx"))
    xhalo = jnp.where(lax.axis_index("gx") > 0, xhalo, jnp.zeros_like(xhalo))
    rim = xhalo.reshape(depth_in, lines, 2 * cin)
    yhalo = lax.ppermute(stacked([yface.reshape(depth_in * half, 2 * cin), rim[:, -1]]), "gy", ring("gy"))
    ny, nz = lax.axis_size("gy"), lax.axis_size("gz")
    diagonal = [(a * nz + b, (a + 1) % ny * nz + (b + 1) % nz) for a in range(ny) for b in range(nz)]
    yzhalo = lax.ppermute(stacked([yface[-1], rim[-1, -1:]]), ("gy", "gz"), diagonal)
    xzhalo = lax.ppermute(stacked([rim[-1]]), "gz", ring("gz"))

    feats, moments, xfaces = features_of(place, cells, zhalo, yhalo, yzhalo, xhalo, xzhalo, conv_first)
    rows = lines * half
    zs = faces("gz", feats[0], feats[-1])
    moments = added("gz", moments)
    zsides = sided(is_even("gz"), zs)

    def yside(y):
        here = slice(y * half, (y + 1) * half)
        return jnp.concatenate([feats[z, here] for z in range(depth)] + [side[here] for side in zsides], axis=0)

    moments, ys = added_with_faces("gy", moments, yside(0), yside(lines - 1))
    ysides = sided(is_even("gy"), ys)

    def xside(n, x):
        own = [xfaces[n]] + [side.reshape(-1, half, cout)[:, x] for side in zsides + ysides]
        return jnp.concatenate(own, axis=0)

    low, high = xside(0, 0), xside(1, half - 1)
    moments, xs = added_with_faces("gx", moments, low, high)
    total_cells = rows * depth * lax.axis_size("gx") * lax.axis_size("gy") * lax.axis_size("gz")
    result = block(
        total_cells, place, moments, norm_gain[None], norm_shift[None], feats, zs, ys, xs,
        conv_second.reshape(3, 3, 3 * cout, cout),
    )
    return jnp.transpose(result.reshape(depth, lines, half, cout), (3, 0, 1, 2))


def solution(mesh):
    in_specs = (P(None, "gz", "gy", "gx"), P(), P(), P(), P())
    out_specs = P(None, "gz", "gy", "gx")
    return jax.shard_map(body, mesh=mesh, in_specs=in_specs, out_specs=out_specs, check_vma=False)
```

```python
import functools

import jax
import jax.numpy as jnp
from jax import lax
from jax.experimental import pallas as pl
from jax.experimental.pallas import tpu as pltpu
from jax.sharding import PartitionSpec as P

NEWTON = 5
EPSILON = 1e-05
LEAK = 0.2
F32, BF16 = jnp.float32, jnp.bfloat16
MIB = 1024 * 1024


def dot(a, b, dims=((1,), (0,))):
    return lax.dot_general(a, b, (dims, ((), ())), preferred_element_type=F32)


def thirds(value):
    one = value.astype(BF16)
    rest = value - one.astype(F32)
    two = rest.astype(BF16)
    return one, two, (rest - two.astype(F32)).astype(BF16)


def dot_full(a, b):
    (a1, a2, a3), (b1, b2, b3) = a, b
    pair = jnp.concatenate([b1, b2], axis=1)
    main = dot(jnp.concatenate([a1, a2], axis=1), jnp.concatenate([pair, pair], axis=0))
    rest = dot(jnp.concatenate([a3, a1], axis=1), jnp.concatenate([b1, b3], axis=0))
    width = b1.shape[1]
    return main[:, :width] + (main[:, width:] + rest)


def split(value):
    hi = value.astype(BF16)
    lo = (value - hi.astype(F32)).astype(BF16)
    return hi, lo


def iota(shape, dim):
    return lax.broadcasted_iota(jnp.int32, shape, dim)


def relayout_kernel(field_ref, cells_ref, yface_ref, xface_ref, rows_ref):
    cin, planes, height, width = field_ref.shape
    half = width // 2
    out = iota((width, width), 0)
    source = jnp.where(out < half, 2 * out, 2 * (out - half) + 1)
    pick = (source == iota((width, width), 1)).astype(F32).astype(BF16)
    for z in range(planes):
        rows_ref[z] = field_ref[:, z].astype(F32).reshape(cin * height, width)
        last = []
        for pair in range(height // 4):
            lines = [rows_ref[z, pl.ds(4 * pair + k, cin, stride=height), :] for k in range(4)]
            block = jnp.concatenate(lines, axis=0).astype(BF16)
            turned = dot(pick, block, ((1,), (1,)))
            for k in range(2):
                row = (2 * pair + k) * half
                lanes = slice(2 * cin * k, 2 * cin * (k + 1))
                even = turned[:half, lanes]
                odd = turned[half:, lanes]
                cells_ref[z, row : row + half, : 2 * cin] = even.astype(BF16)
                cells_ref[z, row : row + half, 2 * cin :] = odd.astype(BF16)
                last.append(odd[half - 1 :, :])
        yface_ref[z] = jnp.concatenate([even[:, cin:], odd[:, cin:]], axis=1).astype(BF16)
        xface_ref[z] = jnp.concatenate(last, axis=0).astype(BF16)


def relayout(field):
    cin, depth, height, width = field.shape
    half, rows = width // 2, height // 2 * (width // 2)
    step = 4 if depth % 4 == 0 else 1
    return pl.pallas_call(
        relayout_kernel,
        grid=(depth // step,),
        in_specs=[pl.BlockSpec((cin, step, height, width), lambda z: (0, z, 0, 0))],
        out_specs=[
            pl.BlockSpec((step, rows, 4 * cin), lambda z: (z, 0, 0)),
            pl.BlockSpec((step, half, 2 * cin), lambda z: (z, 0, 0)),
            pl.BlockSpec((step, height // 2, 2 * cin), lambda z: (z, 0, 0)),
        ],
        out_shape=[
            jax.ShapeDtypeStruct((depth, rows, 4 * cin), BF16),
            jax.ShapeDtypeStruct((depth, half, 2 * cin), BF16),
            jax.ShapeDtypeStruct((depth, height // 2, 2 * cin), BF16),
        ],
        scratch_shapes=[pltpu.VMEM((step, cin * height, width), F32)],
        compiler_params=pltpu.CompilerParams(vmem_limit_bytes=16 * MIB),
        name="relayout",
    )(field)


def moved_down(value):
    return jnp.where(iota(value.shape, 0) == 0, 0.0, pltpu.roll(value, 1, 0))


def line_sums(acc_ref, line, half, cout):
    span = pl.ds(line * half, half)
    straight = acc_ref[span, :cout]
    shifted = acc_ref[span, 2 * cout : 3 * cout]
    if line > 0:
        above = pl.ds((line - 1) * half, half)
        straight = straight + acc_ref[above, cout : 2 * cout]
        shifted = shifted + acc_ref[above, 3 * cout :]
    return straight + moved_down(shifted)


def interior_kernel(
    lines, cells_ref, w_ref, v_ref, part_ref, stat_ref, wz_ref, wy_ref, wx_ref, v3_ref, w4_ref, acc_ref
):
    depth = cells_ref.shape[0] // 2
    cin, cout = w_ref.shape[3:]
    rows = cells_ref.shape[1]
    half = rows // lines
    w4_ref[...] = jnp.zeros(w4_ref.shape, BF16)
    wx_ref[...] = jnp.zeros(wx_ref.shape, BF16)
    wy_ref[...] = jnp.zeros(wy_ref.shape, BF16)
    for dz in range(3):
        for px in range(2):
            for py in range(2):
                k = (2 * px + py) * cin
                w4_ref[dz, k : k + cin, :cout] = w_ref[dz, 1 + py, 1 + px]
                if py == 1:
                    w4_ref[dz, k : k + cin, cout : 2 * cout] = w_ref[dz, 0, 1 + px]
                if px == 1:
                    w4_ref[dz, k : k + cin, 2 * cout : 3 * cout] = w_ref[dz, 1 + py, 0]
                if px == 1 and py == 1:
                    w4_ref[dz, k : k + cin, 3 * cout :] = w_ref[dz, 0, 0]
            k = (2 * dz + px) * cin
            wy_ref[k : k + cin, :cout] = w_ref[dz, 0, 1 + px]
        k = (2 * dz + 1) * cin
        wy_ref[k : k + cin, cout:] = w_ref[dz, 0, 0]
        k = 4 * dz * cin
        wx_ref[k : k + cin, :] = w_ref[dz, 1, 0]
        wx_ref[k + cin : k + 2 * cin, :] = w_ref[dz, 2, 0]
        wx_ref[k + 3 * cin : k + 4 * cin, :] = w_ref[dz, 0, 0]
    wz_ref[...] = w4_ref[0]
    for dz in range(3):
        for dy in range(3):
            v3_ref[dy * 3 * cout : (dy + 1) * 3 * cout, (2 - dz) * cout : (3 - dz) * cout] = v_ref[dz, dy]
    for zo in range(depth):
        first = 0 if zo else 1
        planes = [cells_ref[2 * zo - 1 + dz] for dz in range(first, 3)]
        acc_ref[...] = dot(
            jnp.concatenate(planes, axis=1), w4_ref[first:].reshape((3 - first) * 4 * cin, 4 * cout)
        )
        for line in range(lines):
            part_ref[zo, pl.ds(line * half, half), :] = line_sums(acc_ref, line, half, cout)
    inner = (lines - 1) * half
    inside = iota((inner, cout), 0) % half != 0
    total = jnp.zeros((1, cout), F32)
    for zo in range(1, depth):
        total = total + jnp.sum(part_ref[zo, half:, :], axis=0, keepdims=True)
    offset = total * (1.0 / max(1, (depth - 1) * inner))
    gram, sums = jnp.zeros((cout, 2 * cout), F32), jnp.zeros((1, cout), F32)
    for zo in range(1, depth):
        value = jnp.where(inside, part_ref[zo, half:, :] - offset, 0.0)
        hi, lo = split(value)
        gram = gram + dot(hi, jnp.concatenate([hi, lo], axis=1), ((0,), (0,)))
        sums = sums + jnp.sum(value, axis=0, keepdims=True)
    stat_ref[:cout, :] = gram[:, :cout]
    stat_ref[cout : 2 * cout, :] = gram[:, cout:]
    stat_ref[2 * cout : 2 * cout + 8, :] = jnp.broadcast_to(sums, (8, cout))
    stat_ref[2 * cout + 8 :, :] = jnp.broadcast_to(offset, (8, cout))


def interior(lines, cells, weights, second):
    depth, rows, wide = cells.shape
    cin, cout = weights.shape[3:]
    vmem = pl.BlockSpec(memory_space=pltpu.VMEM)
    flops = depth // 2 * rows * 3 * wide * 8 * cout
    return pl.pallas_call(
        functools.partial(interior_kernel, lines),
        in_specs=[vmem] * 3,
        out_specs=[vmem] * 6,
        out_shape=[
            jax.ShapeDtypeStruct((depth // 2, rows, cout), F32),
            jax.ShapeDtypeStruct((2 * cout + 16, cout), F32),
            jax.ShapeDtypeStruct((wide, 4 * cout), BF16),
            jax.ShapeDtypeStruct((6 * cin, 2 * cout), BF16),
            jax.ShapeDtypeStruct((12 * cin, cout), BF16),
            jax.ShapeDtypeStruct((9 * cout, 3 * cout), BF16),
        ],
        scratch_shapes=[pltpu.VMEM((3, wide, 4 * cout), BF16), pltpu.VMEM((rows, 4 * cout), F32)],
        compiler_params=pltpu.CompilerParams(vmem_limit_bytes=20 * MIB),
        cost_estimate=pl.CostEstimate(flops=flops, bytes_accessed=6 * MIB, transcendentals=0),
        name="interior",
    )(cells, weights, second)


def finish_kernel(
    place_ref, part_ref, stat_ref, zhalo_ref, yhalo_ref, yzhalo_ref, xhalo_ref, xzhalo_ref, wz_ref, wy_ref, wx_ref,
    feat_ref, mom_ref, xface_ref, acc_ref, rim_ref,
):
    depth, rows, cout = part_ref.shape
    lines = xhalo_ref.shape[0] // (2 * depth)
    half = rows // lines
    y_in, z_in = place_ref[5] != 0, place_ref[7] != 0
    zhalo = jnp.where(z_in, zhalo_ref[...], jnp.zeros(zhalo_ref.shape, BF16))
    yrest = yhalo_ref[2 * depth * half :, :].astype(F32)
    yhalo = [yzhalo_ref[:half, :]] + [yhalo_ref[z * half : (z + 1) * half, :] for z in range(2 * depth)]
    yhalo = [jnp.where(y_in, value, jnp.zeros_like(value)) for value in yhalo]
    yhalo[0] = jnp.where(z_in, yhalo[0], jnp.zeros_like(yhalo[0]))
    corner = jnp.where(jnp.logical_and(y_in, z_in), yzhalo_ref[half:, :].astype(F32)[:1], 0.0)
    yrest = jnp.where(y_in, yrest, 0.0)
    here = [jnp.where(z_in, xzhalo_ref[...].astype(F32)[:lines], 0.0)]
    here += [xhalo_ref[...].astype(F32)[z * lines : (z + 1) * lines] for z in range(2 * depth)]
    over = [corner] + [yrest[z : z + 1] for z in range(2 * depth)]
    over = [jnp.concatenate([line, value[: lines - 1]], axis=0) for line, value in zip(over, here, strict=True)]
    xparts = []
    for zo in range(depth):
        row = [part for dz in range(3) for part in (here[2 * zo + dz], over[2 * zo + dz])]
        xparts.append(jnp.concatenate(row, axis=1))
    xsum = dot(jnp.concatenate(xparts, axis=0).astype(BF16), wx_ref[...])
    yparts = [jnp.concatenate(yhalo[2 * zo : 2 * zo + 3], axis=1) for zo in range(depth)]
    ysum = dot(jnp.concatenate(yparts, axis=0), wy_ref[...])
    acc_ref[...] = dot(zhalo, wz_ref[...])
    offset = stat_ref[2 * cout + 8 : 2 * cout + 9, :]
    rim_ref[...] = jnp.zeros(rim_ref.shape, F32)
    first = iota((8, cout), 0) == 0
    edges = rows + (depth - 1) * half
    for zo in range(depth):
        for line in range(lines):
            span = pl.ds(line * half, half)
            k = zo * lines + line
            if zo == 0 or line == 0:
                value = part_ref[zo, span, :]
                if zo == 0:
                    value = value + line_sums(acc_ref, line, half, cout)
                if line == 0:
                    more = ysum[zo * half : (zo + 1) * half]
                    value = value + (more[:, :cout] + moved_down(more[:, cout:]))
                value = value + jnp.where(iota((half, cout), 0) == 0, xsum[k : k + 1], 0.0)
                feat_ref[zo, span, :] = value
                spot = line * half if zo == 0 else rows + (zo - 1) * half
                rim_ref[spot : spot + half, :] = value - offset
                xface_ref[0, k : k + 1, :] = value[:1]
                xface_ref[1, k : k + 1, :] = value[half - 1 :]
            else:
                top = pl.ds(line * half, 8)
                value = part_ref[zo, top, :] + jnp.where(first, xsum[k : k + 1], 0.0)
                feat_ref[zo, top, :] = value
                feat_ref[zo, pl.ds(line * half + 8, half - 8), :] = part_ref[zo, pl.ds(line * half + 8, half - 8), :]
                spot = edges + (zo - 1) * (lines - 1) + line - 1
                rim_ref[spot : spot + 1, :] = value[:1] - offset
                xface_ref[0, k : k + 1, :] = value[:1]
                xface_ref[1, k : k + 1, :] = part_ref[zo, pl.ds((line + 1) * half - 1, 1), :]
    rim = rim_ref[...]
    hi, lo = split(rim)
    gram = dot(hi, jnp.concatenate([hi, lo], axis=1), ((0,), (0,)))
    cross = gram[:, cout:] + stat_ref[cout : 2 * cout, :]
    gram = gram[:, :cout] + stat_ref[:cout, :] + cross + cross.T
    sums = jnp.sum(rim, axis=0, keepdims=True) + stat_ref[2 * cout : 2 * cout + 1, :]
    total = sums + offset * float(depth * rows)
    eye = iota((cout, cout), 0) == iota((cout, cout), 1)
    sums_column = jnp.sum(jnp.where(eye, sums, 0.0), axis=1, keepdims=True)
    offset_column = jnp.sum(jnp.where(eye, offset, 0.0), axis=1, keepdims=True)
    gram = gram + (sums_column * offset + offset_column * total)
    left = iota((cout // 2, cout), 1) < cout // 2
    mom_ref[: cout // 2, :] = jnp.where(left, gram[: cout // 2], gram[cout // 2 :])
    mom_ref[cout // 2 :, :] = jnp.broadcast_to(total, (8, cout))


def finish(place, part, stats, zhalo, yhalo, yzhalo, xhalo, xzhalo, wz, wy, wx):
    depth, rows, cout = part.shape
    lines = xhalo.shape[0] // (2 * depth)
    half = rows // lines
    rim = rows + (depth - 1) * (half + lines - 1)
    vmem = pl.BlockSpec(memory_space=pltpu.VMEM)
    return pl.pallas_call(
        finish_kernel,
        in_specs=[pl.BlockSpec(memory_space=pltpu.SMEM)] + [vmem] * 10,
        out_specs=[vmem] * 3,
        out_shape=[
            jax.ShapeDtypeStruct((depth, rows, cout), F32),
            jax.ShapeDtypeStruct((cout // 2 + 8, cout), F32),
            jax.ShapeDtypeStruct((2, depth * lines, cout), F32),
        ],
        scratch_shapes=[pltpu.VMEM((rows, 4 * cout), F32), pltpu.VMEM((rim + (-rim) % 16, cout), F32)],
        compiler_params=pltpu.CompilerParams(vmem_limit_bytes=16 * MIB),
        name="finish",
    )(place, part, stats, zhalo, yhalo, yzhalo, xhalo, xzhalo, wz, wy, wx)


def block_kernel(
    total_cells,
    place_ref, mom_ref, gain_ref, shift_ref, feat_ref, z1_ref, z2_ref, y1_ref, y2_ref, x1_ref, x2_ref, w_ref,
    out_ref, pad_ref, wide_ref,
):
    depth, rows, cout = feat_ref.shape
    half = y1_ref.shape[0] // (depth + 2)
    lines = rows // half
    group = cout // 2
    square = (cout, cout)
    ri, ci = iota(square, 0), iota(square, 1)
    eye = ri == ci
    same = (ri < group) == (ci < group)
    moments = mom_ref[:group, :] * (1.0 / total_cells)
    average = mom_ref[group : group + 1, :] * (1.0 / total_cells)
    column = jnp.sum(jnp.where(eye, jnp.broadcast_to(average, square), 0.0), axis=1, keepdims=True)
    cov = jnp.concatenate([moments, moments], axis=0) - column * average
    cov = jnp.where(same, cov, 0.0) + jnp.where(eye, EPSILON, 0.0)
    diag = jnp.where(eye, cov, 0.0)
    trace0 = jnp.sum(jnp.sum(diag[:group], axis=1, keepdims=True), axis=0, keepdims=True)
    trace1 = jnp.sum(jnp.sum(diag[group:], axis=1, keepdims=True), axis=0, keepdims=True)
    trace = jnp.where(ri < group, trace0, trace1)
    scaled = cov / trace
    scaled_parts = thirds(scaled)
    mat = jnp.where(eye, 1.5, 0.0) - 0.5 * scaled
    for _ in range(NEWTON - 1):
        parts = thirds(mat)
        mat = 1.5 * mat - 0.5 * dot_full(thirds(dot_full(parts, parts)), thirds(dot_full(parts, scaled_parts)))
    gain = jnp.sum(jnp.where(eye, jnp.broadcast_to(gain_ref[...], square), 0.0), axis=1, keepdims=True)
    mat = mat / jnp.sqrt(trace) * gain
    hi, lo = split(mat)
    mixer = jnp.concatenate(
        [jnp.concatenate([hi, hi], axis=1), jnp.concatenate([lo, jnp.zeros_like(lo)], axis=1)], axis=0
    )
    shift = shift_ref[...]

    def whiten(value):
        hi, lo = split(value - average)
        both = dot(jnp.concatenate([hi, lo], axis=1), mixer, ((1,), (1,)))
        scaled = both[:, :cout] + both[:, cout:] + shift
        return jnp.where(scaled >= 0, scaled, LEAK * scaled)

    base = 8
    x_even, y_even, z_even, xb_in, xa_in, yb_in, ya_in, zb_in, za_in = (place_ref[k] != 0 for k in range(9))

    def sides(even, one_ref, two_ref):
        one, two = one_ref[...], two_ref[...]
        return whiten(jnp.where(even, two, one)), whiten(jnp.where(even, one, two))

    def put(zp, yp, middle, left, right, inside):
        l_in, r_in = xb_in, xa_in
        if inside is not None:
            middle = jnp.where(inside, middle, 0.0)
            l_in, r_in = jnp.logical_and(l_in, inside), jnp.logical_and(r_in, inside)
        pad_ref[zp, yp, base : base + half, :] = middle
        pad_ref[zp, yp, base - 1 : base, :] = jnp.where(l_in, left, 0.0)
        pad_ref[zp, yp, base + half : base + half + 1, :] = jnp.where(r_in, right, 0.0)

    zsides = sides(z_even, z1_ref, z2_ref)
    ysides = sides(y_even, y1_ref, y2_ref)
    xsides = sides(x_even, x1_ref, x2_ref)
    spots = [(z + 1, None) for z in range(depth)] + [(0, zb_in), (depth + 1, za_in)]
    for n, (zp, z_in) in enumerate(spots):
        plane = whiten(feat_ref[n]) if n < depth else zsides[n - depth]
        for y in range(lines):
            k = n * lines + y
            put(zp, y + 1, plane[y * half : (y + 1) * half], xsides[0][k : k + 1], xsides[1][k : k + 1], z_in)
        for m, (yp, y_in) in enumerate(((0, yb_in), (lines + 1, ya_in))):
            k = (depth + 2) * (lines + m) + n
            inside = y_in if z_in is None else jnp.logical_and(z_in, y_in)
            put(zp, yp, ysides[m][n * half : (n + 1) * half], xsides[0][k : k + 1], xsides[1][k : k + 1], inside)
    for zp in range(depth + 2):
        for yp in range(lines + 2):
            for dx in range(3):
                wide_ref[zp, yp * half : (yp + 1) * half, dx * cout : (dx + 1) * cout] = pad_ref[
                    zp, yp, base - 1 + dx : base - 1 + dx + half, :
                ].astype(BF16)
    sums = [None] * depth
    for zp in range(depth + 2):
        low, high = max(zp - 2, 0), min(zp, depth - 1)
        lanes = slice((low - zp + 2) * cout, (high - zp + 3) * cout)
        taken = [wide_ref[zp, dy * half : dy * half + rows, :] for dy in range(3)]
        got = dot(jnp.concatenate(taken, axis=1), w_ref[:, lanes])
        for n, z in enumerate(range(low, high + 1)):
            piece = got[:, n * cout : (n + 1) * cout]
            sums[z] = piece if sums[z] is None else sums[z] + piece
        if zp >= 2:
            out_ref[zp - 2] = sums[zp - 2].astype(BF16)


def block(total_cells, place, moments, gain, shift, feats, zs, ys, xs, weights):
    depth, rows, cout = feats.shape
    half = ys[0].shape[0] // (depth + 2)
    lines = rows // half
    vmem = pl.BlockSpec(memory_space=pltpu.VMEM)
    return pl.pallas_call(
        functools.partial(block_kernel, total_cells),
        in_specs=[pl.BlockSpec(memory_space=pltpu.SMEM)] + [vmem] * 11,
        out_specs=vmem,
        out_shape=jax.ShapeDtypeStruct((depth, rows, cout), BF16),
        scratch_shapes=[
            pltpu.VMEM((depth + 2, lines + 2, half + 16, cout), F32),
            pltpu.VMEM((depth + 2, (lines + 2) * half, 3 * cout), BF16),
        ],
        compiler_params=pltpu.CompilerParams(vmem_limit_bytes=24 * MIB),
        name="block",
    )(place, moments, gain, shift, feats, *zs, *ys, *xs, weights)


def power_of_two(size):
    return size & (size - 1) == 0


def first_pairs(axis):
    return [(i, i ^ 1) for i in range(lax.axis_size(axis))]


def second_pairs(axis):
    size = lax.axis_size(axis)
    return [(i, (i + 1 if i % 2 else i - 1) % size) for i in range(size)]


def is_even(axis):
    size = lax.axis_size(axis)
    return lax.axis_index(axis) % 2 == 0 if size > 1 and power_of_two(size) else jnp.bool_(True)


def faces(axis, low, high):
    size = lax.axis_size(axis)
    if size == 1:
        return low, high
    if not power_of_two(size):
        up = up_pairs(axis)
        return lax.ppermute(low, axis, [(j, i) for i, j in up]), lax.ppermute(high, axis, up)
    even = is_even(axis)
    one = lax.ppermute(jnp.where(even, high, low), axis, first_pairs(axis))
    if size == 2:
        return one, one
    inner = [(i, j) for i, j in second_pairs(axis) if abs(i - j) == 1]
    return one, lax.ppermute(jnp.where(even, low, high), axis, inner)


def added(axis, value, first=True):
    size = lax.axis_size(axis)
    if size == 1:
        return value
    if not power_of_two(size):
        return lax.psum(value, axis)
    if first:
        value = value + lax.ppermute(value, axis, first_pairs(axis))
    if size > 2:
        value = value + lax.ppermute(value, axis, second_pairs(axis))
    step = 4
    while step < size:
        value = value + lax.ppermute(value, axis, [(i, (i + step) % size) for i in range(size)])
        step *= 2
    return value


def added_with_faces(axis, value, low, high):
    size = lax.axis_size(axis)
    if size == 1 or not power_of_two(size):
        return added(axis, value), faces(axis, low, high)
    even, count = is_even(axis), value.shape[0]
    both = jnp.concatenate([value, jnp.where(even, high, low)], axis=0)
    both = lax.ppermute(both, axis, first_pairs(axis))
    value, one = value + both[:count], both[count:]
    if size == 2:
        return value, (one, one)
    inner = [(i, j) for i, j in second_pairs(axis) if abs(i - j) == 1]
    two = lax.ppermute(jnp.where(even, low, high), axis, inner)
    return added(axis, value, first=False), (one, two)


def sided(even, pair):
    one, two = pair
    return jnp.where(even, two, one), jnp.where(even, one, two)


def up_pairs(axis):
    return [(i, i + 1) for i in range(lax.axis_size(axis) - 1)]


def ring(axis):
    size = lax.axis_size(axis)
    return [(i, (i + 1) % size) for i in range(size)]


def stacked(parts):
    count = sum(part.shape[0] for part in parts)
    fill = jnp.zeros((-count % 16, parts[0].shape[1]), parts[0].dtype)
    return jnp.concatenate(parts + [fill], axis=0)


def body(field, conv_first, norm_gain, norm_shift, conv_second):
    cin, depth_in, height_in, width_in = field.shape
    cout = conv_second.shape[-1]
    depth, lines, half = depth_in // 2, height_in // 2, width_in // 2
    cells, yface, xface = relayout(field)

    place = [is_even(axis) for axis in ("gx", "gy", "gz")]
    for axis in ("gx", "gy", "gz"):
        place += [lax.axis_index(axis) > 0, lax.axis_index(axis) < lax.axis_size(axis) - 1]
    place = jnp.stack(place).astype(jnp.int32)
    zhalo = lax.ppermute(cells[-1], "gz", ring("gz"))
    xhalo = lax.ppermute(xface.reshape(depth_in * lines, 2 * cin), "gx", ring("gx"))
    xhalo = jnp.where(lax.axis_index("gx") > 0, xhalo, jnp.zeros_like(xhalo))
    rim = xhalo.reshape(depth_in, lines, 2 * cin)
    yhalo = lax.ppermute(stacked([yface.reshape(depth_in * half, 2 * cin), rim[:, -1]]), "gy", ring("gy"))
    ny, nz = lax.axis_size("gy"), lax.axis_size("gz")
    diagonal = [(a * nz + b, (a + 1) % ny * nz + (b + 1) % nz) for a in range(ny) for b in range(nz)]
    yzhalo = lax.ppermute(stacked([yface[-1], rim[-1, -1:]]), ("gy", "gz"), diagonal)
    xzhalo = lax.ppermute(stacked([rim[-1]]), "gz", ring("gz"))

    part, stats, wz, wy, wx, second = interior(lines, cells, conv_first, conv_second.reshape(3, 3, 3 * cout, cout))
    feats, moments, xfaces = finish(place, part, stats, zhalo, yhalo, yzhalo, xhalo, xzhalo, wz, wy, wx)
    rows = lines * half
    zs = faces("gz", feats[0], feats[-1])
    moments = added("gz", moments)
    zsides = sided(is_even("gz"), zs)

    def yside(y):
        here = slice(y * half, (y + 1) * half)
        return jnp.concatenate([feats[z, here] for z in range(depth)] + [side[here] for side in zsides], axis=0)

    moments, ys = added_with_faces("gy", moments, yside(0), yside(lines - 1))
    ysides = sided(is_even("gy"), ys)

    def xside(n, x):
        own = [xfaces[n]] + [side.reshape(-1, half, cout)[:, x] for side in zsides + ysides]
        return jnp.concatenate(own, axis=0)

    low, high = xside(0, 0), xside(1, half - 1)
    moments, xs = added_with_faces("gx", moments, low, high)
    total_cells = rows * depth * lax.axis_size("gx") * lax.axis_size("gy") * lax.axis_size("gz")
    result = block(
        total_cells, place, moments, norm_gain[None], norm_shift[None], feats, zs, ys, xs, second,
    )
    return jnp.transpose(result.reshape(depth, lines, half, cout), (3, 0, 1, 2))


def solution(mesh):
    in_specs = (P(None, "gz", "gy", "gx"), P(), P(), P(), P())
    out_specs = P(None, "gz", "gy", "gx")
    return jax.shard_map(body, mesh=mesh, in_specs=in_specs, out_specs=out_specs, check_vma=False)
```

```python
import functools

import jax
import jax.numpy as jnp
from jax import lax
from jax.experimental import pallas as pl
from jax.experimental.pallas import tpu as pltpu
from jax.sharding import PartitionSpec as P

NEWTON = 5
EPSILON = 1e-05
LEAK = 0.2
F32, BF16 = jnp.float32, jnp.bfloat16
MIB = 1024 * 1024


def places():
    even, inside = [], []
    for axis in ("gx", "gy", "gz"):
        size, place = lax.axis_size(axis), lax.axis_index(axis)
        even.append(lax.rem(place, 2) == 0 if size > 1 and power_of_two(size) else place >= 0)
        inside += [place > 0, place < size - 1]
    return even + inside


def in_vmem(*values):
    return [pltpu.with_memory_space_constraint(value, pltpu.VMEM) for value in values]


def dot(a, b, dims=((1,), (0,))):
    return lax.dot_general(a, b, (dims, ((), ())), preferred_element_type=F32)


def thirds(value):
    one = value.astype(BF16)
    rest = value - one.astype(F32)
    two = rest.astype(BF16)
    return one, two, (rest - two.astype(F32)).astype(BF16)


def dot_full(a, b):
    (a1, a2, a3), (b1, b2, b3) = a, b
    pair = jnp.concatenate([b1, b2], axis=1)
    main = dot(jnp.concatenate([a1, a2], axis=1), jnp.concatenate([pair, pair], axis=0))
    rest = dot(jnp.concatenate([a3, a1], axis=1), jnp.concatenate([b1, b3], axis=0))
    width = b1.shape[1]
    return main[:, :width] + (main[:, width:] + rest)


def split(value):
    hi = value.astype(BF16)
    lo = (value - hi.astype(F32)).astype(BF16)
    return hi, lo


def iota(shape, dim):
    return lax.broadcasted_iota(jnp.int32, shape, dim)


def relayout_kernel(field_ref, cells_ref, yface_ref, xface_ref, flag_ref, rows_ref):
    for k, flag in enumerate(places()):
        flag_ref[k : k + 1, :] = jnp.full((1, flag_ref.shape[1]), flag.astype(jnp.int32)).astype(F32)
    cin, planes, height, width = field_ref.shape
    half = width // 2
    out = iota((width, width), 0)
    source = jnp.where(out < half, 2 * out, 2 * (out - half) + 1)
    pick = (source == iota((width, width), 1)).astype(F32).astype(BF16)
    for z in range(planes):
        rows_ref[z] = field_ref[:, z].astype(F32).reshape(cin * height, width)
        last = []
        for pair in range(height // 4):
            lines = [rows_ref[z, pl.ds(4 * pair + k, cin, stride=height), :] for k in range(4)]
            block = jnp.concatenate(lines, axis=0).astype(BF16)
            turned = dot(pick, block, ((1,), (1,)))
            for k in range(2):
                row = (2 * pair + k) * half
                lanes = slice(2 * cin * k, 2 * cin * (k + 1))
                even = turned[:half, lanes]
                odd = turned[half:, lanes]
                cells_ref[z, row : row + half, : 2 * cin] = even.astype(BF16)
                cells_ref[z, row : row + half, 2 * cin :] = odd.astype(BF16)
                last.append(odd[half - 1 :, :])
        yface_ref[z] = jnp.concatenate([even[:, cin:], odd[:, cin:]], axis=1).astype(BF16)
        xface_ref[z] = jnp.concatenate(last, axis=0).astype(BF16)


def relayout(field):
    cin, depth, height, width = field.shape
    half, rows = width // 2, height // 2 * (width // 2)
    step = 4 if depth % 4 == 0 else 1
    return pl.pallas_call(
        relayout_kernel,
        grid=(depth // step,),
        in_specs=[pl.BlockSpec((cin, step, height, width), lambda z: (0, z, 0, 0))],
        out_specs=[
            pl.BlockSpec((step, rows, 4 * cin), lambda z: (z, 0, 0)),
            pl.BlockSpec((step, half, 2 * cin), lambda z: (z, 0, 0)),
            pl.BlockSpec((step, height // 2, 2 * cin), lambda z: (z, 0, 0)),
            pl.BlockSpec((16, 2 * cin), lambda z: (0, 0)),
        ],
        out_shape=[
            pltpu.VMEM((depth, rows, 4 * cin), BF16),
            pltpu.VMEM((depth, half, 2 * cin), BF16),
            pltpu.VMEM((depth, height // 2, 2 * cin), BF16),
            pltpu.VMEM((16, 2 * cin), F32),
        ],
        scratch_shapes=[pltpu.VMEM((step, cin * height, width), F32)],
        compiler_params=pltpu.CompilerParams(vmem_limit_bytes=16 * MIB),
        name="relayout",
    )(field)


def moved_down(value):
    return jnp.where(iota(value.shape, 0) == 0, 0.0, pltpu.roll(value, 1, 0))


def line_sums(acc_ref, line, half, cout):
    span = pl.ds(line * half, half)
    straight = acc_ref[span, :cout]
    shifted = acc_ref[span, 2 * cout : 3 * cout]
    if line > 0:
        above = pl.ds((line - 1) * half, half)
        straight = straight + acc_ref[above, cout : 2 * cout]
        shifted = shifted + acc_ref[above, 3 * cout :]
    return straight + moved_down(shifted)


def interior_kernel(
    lines, cells_ref, w_ref, v_ref, part_ref, stat_ref, wz_ref, wy_ref, wx_ref, v3_ref, w4_ref, acc_ref
):
    depth = cells_ref.shape[0] // 2
    cin, cout = w_ref.shape[3:]
    rows = cells_ref.shape[1]
    half = rows // lines
    w4_ref[...] = jnp.zeros(w4_ref.shape, BF16)
    wx_ref[...] = jnp.zeros(wx_ref.shape, BF16)
    wy_ref[...] = jnp.zeros(wy_ref.shape, BF16)
    for dz in range(3):
        for px in range(2):
            for py in range(2):
                k = (2 * px + py) * cin
                w4_ref[dz, k : k + cin, :cout] = w_ref[dz, 1 + py, 1 + px]
                if py == 1:
                    w4_ref[dz, k : k + cin, cout : 2 * cout] = w_ref[dz, 0, 1 + px]
                if px == 1:
                    w4_ref[dz, k : k + cin, 2 * cout : 3 * cout] = w_ref[dz, 1 + py, 0]
                if px == 1 and py == 1:
                    w4_ref[dz, k : k + cin, 3 * cout :] = w_ref[dz, 0, 0]
            k = (2 * dz + px) * cin
            wy_ref[k : k + cin, :cout] = w_ref[dz, 0, 1 + px]
        k = (2 * dz + 1) * cin
        wy_ref[k : k + cin, cout:] = w_ref[dz, 0, 0]
        k = 4 * dz * cin
        wx_ref[k : k + cin, :] = w_ref[dz, 1, 0]
        wx_ref[k + cin : k + 2 * cin, :] = w_ref[dz, 2, 0]
        wx_ref[k + 3 * cin : k + 4 * cin, :] = w_ref[dz, 0, 0]
    wz_ref[...] = w4_ref[0]
    for dz in range(3):
        for dy in range(3):
            v3_ref[dy * 3 * cout : (dy + 1) * 3 * cout, (2 - dz) * cout : (3 - dz) * cout] = v_ref[dz, dy]
    for zo in range(depth):
        first = 0 if zo else 1
        planes = [cells_ref[2 * zo - 1 + dz] for dz in range(first, 3)]
        acc_ref[...] = dot(
            jnp.concatenate(planes, axis=1), w4_ref[first:].reshape((3 - first) * 4 * cin, 4 * cout)
        )
        for line in range(lines):
            part_ref[zo, pl.ds(line * half, half), :] = line_sums(acc_ref, line, half, cout)
    inner = (lines - 1) * half
    inside = iota((inner, cout), 0) % half != 0
    total = jnp.zeros((1, cout), F32)
    for zo in range(1, depth):
        total = total + jnp.sum(part_ref[zo, half:, :], axis=0, keepdims=True)
    offset = total * (1.0 / max(1, (depth - 1) * inner))
    gram, sums = jnp.zeros((cout, 2 * cout), F32), jnp.zeros((1, cout), F32)
    for zo in range(1, depth):
        value = jnp.where(inside, part_ref[zo, half:, :] - offset, 0.0)
        hi, lo = split(value)
        gram = gram + dot(hi, jnp.concatenate([hi, lo], axis=1), ((0,), (0,)))
        sums = sums + jnp.sum(value, axis=0, keepdims=True)
    stat_ref[:cout, :] = gram[:, :cout]
    stat_ref[cout : 2 * cout, :] = gram[:, cout:]
    stat_ref[2 * cout : 2 * cout + 8, :] = jnp.broadcast_to(sums, (8, cout))
    stat_ref[2 * cout + 8 :, :] = jnp.broadcast_to(offset, (8, cout))


def interior(lines, cells, weights, second):
    depth, rows, wide = cells.shape
    cin, cout = weights.shape[3:]
    vmem = pl.BlockSpec(memory_space=pltpu.VMEM)
    flops = depth // 2 * rows * 3 * wide * 8 * cout
    return pl.pallas_call(
        functools.partial(interior_kernel, lines),
        in_specs=[vmem] * 3,
        out_specs=[vmem] * 6,
        out_shape=[
            pltpu.VMEM((depth // 2, rows, cout), F32),
            pltpu.VMEM((2 * cout + 16, cout), F32),
            pltpu.VMEM((wide, 4 * cout), BF16),
            pltpu.VMEM((6 * cin, 2 * cout), BF16),
            pltpu.VMEM((12 * cin, cout), BF16),
            pltpu.VMEM((9 * cout, 3 * cout), BF16),
        ],
        scratch_shapes=[pltpu.VMEM((3, wide, 4 * cout), BF16), pltpu.VMEM((rows, 4 * cout), F32)],
        compiler_params=pltpu.CompilerParams(vmem_limit_bytes=20 * MIB),
        cost_estimate=pl.CostEstimate(flops=flops, bytes_accessed=6 * MIB, transcendentals=0),
        name="interior",
    )(*in_vmem(cells), weights, second)


def finish_kernel(
    part_ref, stat_ref, zhalo_ref, yhalo_ref, yzhalo_ref, xhalo_ref, xzhalo_ref, wz_ref, wy_ref, wx_ref,
    feat_ref, mom_ref, xface_ref, acc_ref, rim_ref,
):
    depth, rows, cout = part_ref.shape
    lines = xhalo_ref.shape[0] // (2 * depth)
    half = rows // lines
    _, _, _, _, _, y_in, _, z_in, _ = places()
    zhalo = jnp.where(z_in, zhalo_ref[...], jnp.zeros(zhalo_ref.shape, BF16))
    yrest = yhalo_ref[2 * depth * half :, :].astype(F32)
    yhalo = [yzhalo_ref[:half, :]] + [yhalo_ref[z * half : (z + 1) * half, :] for z in range(2 * depth)]
    yhalo = [jnp.where(y_in, value, jnp.zeros_like(value)) for value in yhalo]
    yhalo[0] = jnp.where(z_in, yhalo[0], jnp.zeros_like(yhalo[0]))
    corner = jnp.where(jnp.logical_and(y_in, z_in), yzhalo_ref[half:, :].astype(F32)[:1], 0.0)
    yrest = jnp.where(y_in, yrest, 0.0)
    here = [jnp.where(z_in, xzhalo_ref[...].astype(F32)[:lines], 0.0)]
    here += [xhalo_ref[...].astype(F32)[z * lines : (z + 1) * lines] for z in range(2 * depth)]
    over = [corner] + [yrest[z : z + 1] for z in range(2 * depth)]
    over = [jnp.concatenate([line, value[: lines - 1]], axis=0) for line, value in zip(over, here, strict=True)]
    xparts = []
    for zo in range(depth):
        row = [part for dz in range(3) for part in (here[2 * zo + dz], over[2 * zo + dz])]
        xparts.append(jnp.concatenate(row, axis=1))
    xsum = dot(jnp.concatenate(xparts, axis=0).astype(BF16), wx_ref[...])
    yparts = [jnp.concatenate(yhalo[2 * zo : 2 * zo + 3], axis=1) for zo in range(depth)]
    ysum = dot(jnp.concatenate(yparts, axis=0), wy_ref[...])
    acc_ref[...] = dot(zhalo, wz_ref[...])
    offset = stat_ref[2 * cout + 8 : 2 * cout + 9, :]
    rim_ref[...] = jnp.zeros(rim_ref.shape, F32)
    first = iota((8, cout), 0) == 0
    edges = rows + (depth - 1) * half
    for zo in range(depth):
        for line in range(lines):
            span = pl.ds(line * half, half)
            k = zo * lines + line
            if zo == 0 or line == 0:
                value = part_ref[zo, span, :]
                if zo == 0:
                    value = value + line_sums(acc_ref, line, half, cout)
                if line == 0:
                    more = ysum[zo * half : (zo + 1) * half]
                    value = value + (more[:, :cout] + moved_down(more[:, cout:]))
                value = value + jnp.where(iota((half, cout), 0) == 0, xsum[k : k + 1], 0.0)
                feat_ref[zo, span, :] = value
                spot = line * half if zo == 0 else rows + (zo - 1) * half
                rim_ref[spot : spot + half, :] = value - offset
                xface_ref[0, k : k + 1, :] = value[:1]
                xface_ref[1, k : k + 1, :] = value[half - 1 :]
            else:
                top = pl.ds(line * half, 8)
                value = part_ref[zo, top, :] + jnp.where(first, xsum[k : k + 1], 0.0)
                feat_ref[zo, top, :] = value
                feat_ref[zo, pl.ds(line * half + 8, half - 8), :] = part_ref[zo, pl.ds(line * half + 8, half - 8), :]
                spot = edges + (zo - 1) * (lines - 1) + line - 1
                rim_ref[spot : spot + 1, :] = value[:1] - offset
                xface_ref[0, k : k + 1, :] = value[:1]
                xface_ref[1, k : k + 1, :] = part_ref[zo, pl.ds((line + 1) * half - 1, 1), :]
    rim = rim_ref[...]
    hi, lo = split(rim)
    gram = dot(hi, jnp.concatenate([hi, lo], axis=1), ((0,), (0,)))
    cross = gram[:, cout:] + stat_ref[cout : 2 * cout, :]
    gram = gram[:, :cout] + stat_ref[:cout, :] + cross + cross.T
    sums = jnp.sum(rim, axis=0, keepdims=True) + stat_ref[2 * cout : 2 * cout + 1, :]
    total = sums + offset * float(depth * rows)
    eye = iota((cout, cout), 0) == iota((cout, cout), 1)
    sums_column = jnp.sum(jnp.where(eye, sums, 0.0), axis=1, keepdims=True)
    offset_column = jnp.sum(jnp.where(eye, offset, 0.0), axis=1, keepdims=True)
    gram = gram + (sums_column * offset + offset_column * total)
    left = iota((cout // 2, cout), 1) < cout // 2
    mom_ref[: cout // 2, :] = jnp.where(left, gram[: cout // 2], gram[cout // 2 :])
    mom_ref[cout // 2 :, :] = jnp.broadcast_to(total, (8, cout))


def finish(part, stats, zhalo, yhalo, yzhalo, xhalo, xzhalo, wz, wy, wx):
    depth, rows, cout = part.shape
    lines = xhalo.shape[0] // (2 * depth)
    half = rows // lines
    rim = rows + (depth - 1) * (half + lines - 1)
    vmem = pl.BlockSpec(memory_space=pltpu.VMEM)
    return pl.pallas_call(
        finish_kernel,
        in_specs=[vmem] * 10,
        out_specs=[vmem] * 3,
        out_shape=[
            pltpu.VMEM((depth, rows, cout), F32),
            pltpu.VMEM((cout // 2 + 8, cout), F32),
            pltpu.VMEM((2, depth * lines, cout), F32),
        ],
        scratch_shapes=[pltpu.VMEM((rows, 4 * cout), F32), pltpu.VMEM((rim + (-rim) % 16, cout), F32)],
        compiler_params=pltpu.CompilerParams(vmem_limit_bytes=16 * MIB),
        name="finish",
    )(*in_vmem(part, stats, zhalo, yhalo, yzhalo, xhalo, xzhalo, wz, wy, wx))


def block_kernel(
    total_cells,
    mom_ref, gain_ref, shift_ref, feat_ref, z1_ref, z2_ref, y1_ref, y2_ref, x1_ref, x2_ref, w_ref,
    out_ref, pad_ref, wide_ref,
):
    depth, rows, cout = feat_ref.shape
    half = y1_ref.shape[0] // (depth + 2)
    lines = rows // half
    group = cout // 2
    square = (cout, cout)
    ri, ci = iota(square, 0), iota(square, 1)
    eye = ri == ci
    same = (ri < group) == (ci < group)
    moments = mom_ref[:group, :] * (1.0 / total_cells)
    average = mom_ref[group : group + 1, :] * (1.0 / total_cells)
    column = jnp.sum(jnp.where(eye, jnp.broadcast_to(average, square), 0.0), axis=1, keepdims=True)
    cov = jnp.concatenate([moments, moments], axis=0) - column * average
    cov = jnp.where(same, cov, 0.0) + jnp.where(eye, EPSILON, 0.0)
    diag = jnp.where(eye, cov, 0.0)
    trace0 = jnp.sum(jnp.sum(diag[:group], axis=1, keepdims=True), axis=0, keepdims=True)
    trace1 = jnp.sum(jnp.sum(diag[group:], axis=1, keepdims=True), axis=0, keepdims=True)
    trace = jnp.where(ri < group, trace0, trace1)
    scaled = cov / trace
    scaled_parts = thirds(scaled)
    mat = jnp.where(eye, 1.5, 0.0) - 0.5 * scaled
    for _ in range(NEWTON - 1):
        parts = thirds(mat)
        mat = 1.5 * mat - 0.5 * dot_full(thirds(dot_full(parts, parts)), thirds(dot_full(parts, scaled_parts)))
    gain = jnp.sum(jnp.where(eye, jnp.broadcast_to(gain_ref[...], square), 0.0), axis=1, keepdims=True)
    mat = mat / jnp.sqrt(trace) * gain
    hi, lo = split(mat)
    mixer = jnp.concatenate(
        [jnp.concatenate([hi, hi], axis=1), jnp.concatenate([lo, jnp.zeros_like(lo)], axis=1)], axis=0
    )
    shift = shift_ref[...]

    def whiten(value):
        hi, lo = split(value - average)
        both = dot(jnp.concatenate([hi, lo], axis=1), mixer, ((1,), (1,)))
        scaled = both[:, :cout] + both[:, cout:] + shift
        return jnp.where(scaled >= 0, scaled, LEAK * scaled)

    base = 8
    x_even, y_even, z_even, xb_in, xa_in, yb_in, ya_in, zb_in, za_in = places()

    def sides(even, one_ref, two_ref):
        one, two = one_ref[...], two_ref[...]
        return whiten(jnp.where(even, two, one)), whiten(jnp.where(even, one, two))

    def put(zp, yp, middle, left, right, inside):
        l_in, r_in = xb_in, xa_in
        if inside is not None:
            middle = jnp.where(inside, middle, 0.0)
            l_in, r_in = jnp.logical_and(l_in, inside), jnp.logical_and(r_in, inside)
        pad_ref[zp, yp, base : base + half, :] = middle
        pad_ref[zp, yp, base - 1 : base, :] = jnp.where(l_in, left, 0.0)
        pad_ref[zp, yp, base + half : base + half + 1, :] = jnp.where(r_in, right, 0.0)

    zsides = sides(z_even, z1_ref, z2_ref)
    ysides = sides(y_even, y1_ref, y2_ref)
    xsides = sides(x_even, x1_ref, x2_ref)
    spots = [(z + 1, None) for z in range(depth)] + [(0, zb_in), (depth + 1, za_in)]
    for n, (zp, z_in) in enumerate(spots):
        plane = whiten(feat_ref[n]) if n < depth else zsides[n - depth]
        for y in range(lines):
            k = n * lines + y
            put(zp, y + 1, plane[y * half : (y + 1) * half], xsides[0][k : k + 1], xsides[1][k : k + 1], z_in)
        for m, (yp, y_in) in enumerate(((0, yb_in), (lines + 1, ya_in))):
            k = (depth + 2) * (lines + m) + n
            inside = y_in if z_in is None else jnp.logical_and(z_in, y_in)
            put(zp, yp, ysides[m][n * half : (n + 1) * half], xsides[0][k : k + 1], xsides[1][k : k + 1], inside)
    for zp in range(depth + 2):
        for yp in range(lines + 2):
            for dx in range(3):
                wide_ref[zp, yp * half : (yp + 1) * half, dx * cout : (dx + 1) * cout] = pad_ref[
                    zp, yp, base - 1 + dx : base - 1 + dx + half, :
                ].astype(BF16)
    sums = [None] * depth
    for zp in range(depth + 2):
        low, high = max(zp - 2, 0), min(zp, depth - 1)
        lanes = slice((low - zp + 2) * cout, (high - zp + 3) * cout)
        taken = [wide_ref[zp, dy * half : dy * half + rows, :] for dy in range(3)]
        got = dot(jnp.concatenate(taken, axis=1), w_ref[:, lanes])
        for n, z in enumerate(range(low, high + 1)):
            piece = got[:, n * cout : (n + 1) * cout]
            sums[z] = piece if sums[z] is None else sums[z] + piece
        if zp >= 2:
            out_ref[zp - 2] = sums[zp - 2].astype(BF16)


def block(total_cells, moments, gain, shift, feats, zs, ys, xs, weights):
    depth, rows, cout = feats.shape
    half = ys[0].shape[0] // (depth + 2)
    lines = rows // half
    vmem = pl.BlockSpec(memory_space=pltpu.VMEM)
    return pl.pallas_call(
        functools.partial(block_kernel, total_cells),
        in_specs=[vmem] * 11,
        out_specs=vmem,
        out_shape=jax.ShapeDtypeStruct((depth, rows, cout), BF16),
        scratch_shapes=[
            pltpu.VMEM((depth + 2, lines + 2, half + 16, cout), F32),
            pltpu.VMEM((depth + 2, (lines + 2) * half, 3 * cout), BF16),
        ],
        compiler_params=pltpu.CompilerParams(vmem_limit_bytes=24 * MIB),
        name="block",
    )(moments, gain, shift, *in_vmem(feats, *zs, *ys, *xs, weights))


def power_of_two(size):
    return size & (size - 1) == 0


def first_pairs(axis):
    return [(i, i ^ 1) for i in range(lax.axis_size(axis))]


def second_pairs(axis):
    size = lax.axis_size(axis)
    return [(i, (i + 1 if i % 2 else i - 1) % size) for i in range(size)]


def faces(axis, even, low, high):
    size = lax.axis_size(axis)
    if size == 1:
        return low, high
    if not power_of_two(size):
        up = up_pairs(axis)
        return lax.ppermute(low, axis, [(j, i) for i, j in up]), lax.ppermute(high, axis, up)
    one = lax.ppermute(jnp.where(even, high, low), axis, first_pairs(axis))
    if size == 2:
        return one, one
    inner = [(i, j) for i, j in second_pairs(axis) if abs(i - j) == 1]
    return one, lax.ppermute(jnp.where(even, low, high), axis, inner)


def added(axis, value, first=True):
    size = lax.axis_size(axis)
    if size == 1:
        return value
    if not power_of_two(size):
        return lax.psum(value, axis)
    if first:
        value = value + lax.ppermute(value, axis, first_pairs(axis))
    if size > 2:
        value = value + lax.ppermute(value, axis, second_pairs(axis))
    step = 4
    while step < size:
        value = value + lax.ppermute(value, axis, [(i, (i + step) % size) for i in range(size)])
        step *= 2
    return value


def added_with_faces(axis, even, value, low, high):
    size = lax.axis_size(axis)
    if size == 1 or not power_of_two(size):
        return added(axis, value), faces(axis, even, low, high)
    count = value.shape[0]
    both = jnp.concatenate([value, jnp.where(even, high, low)], axis=0)
    both = lax.ppermute(both, axis, first_pairs(axis))
    value, one = value + both[:count], both[count:]
    if size == 2:
        return value, (one, one)
    inner = [(i, j) for i, j in second_pairs(axis) if abs(i - j) == 1]
    two = lax.ppermute(jnp.where(even, low, high), axis, inner)
    return added(axis, value, first=False), (one, two)


def sided(even, pair):
    one, two = pair
    return jnp.where(even, two, one), jnp.where(even, one, two)


def up_pairs(axis):
    return [(i, i + 1) for i in range(lax.axis_size(axis) - 1)]


def ring(axis):
    size = lax.axis_size(axis)
    return [(i, (i + 1) % size) for i in range(size)]


def stacked(parts):
    count = sum(part.shape[0] for part in parts)
    fill = jnp.zeros((-count % 16, parts[0].shape[1]), parts[0].dtype)
    return jnp.concatenate(parts + [fill], axis=0)


def body(field, conv_first, norm_gain, norm_shift, conv_second):
    cin, depth_in, height_in, width_in = field.shape
    cout = conv_second.shape[-1]
    depth, lines, half = depth_in // 2, height_in // 2, width_in // 2
    cells, yface, xface, flags = relayout(field)
    x_even, y_even, z_even, x_in = (flags[k : k + 1, :] > 0 for k in range(4))
    zhalo = lax.ppermute(cells[-1], "gz", ring("gz"))
    xhalo = lax.ppermute(xface.reshape(depth_in * lines, 2 * cin), "gx", ring("gx"))
    xhalo = jnp.where(x_in, xhalo, jnp.zeros_like(xhalo))
    rim = xhalo.reshape(depth_in, lines, 2 * cin)
    yhalo = lax.ppermute(stacked([yface.reshape(depth_in * half, 2 * cin), rim[:, -1]]), "gy", ring("gy"))
    ny, nz = lax.axis_size("gy"), lax.axis_size("gz")
    diagonal = [(a * nz + b, (a + 1) % ny * nz + (b + 1) % nz) for a in range(ny) for b in range(nz)]
    yzhalo = lax.ppermute(stacked([yface[-1], rim[-1, -1:]]), ("gy", "gz"), diagonal)
    xzhalo = lax.ppermute(stacked([rim[-1]]), "gz", ring("gz"))

    part, stats, wz, wy, wx, second = interior(lines, cells, conv_first, conv_second.reshape(3, 3, 3 * cout, cout))
    feats, moments, xfaces = finish(part, stats, zhalo, yhalo, yzhalo, xhalo, xzhalo, wz, wy, wx)
    rows = lines * half
    zs = faces("gz", z_even, feats[0], feats[-1])
    moments = added("gz", moments)
    zsides = sided(z_even, zs)

    def yside(y):
        here = slice(y * half, (y + 1) * half)
        return jnp.concatenate([feats[z, here] for z in range(depth)] + [side[here] for side in zsides], axis=0)

    moments, ys = added_with_faces("gy", y_even, moments, yside(0), yside(lines - 1))
    ysides = sided(y_even, ys)

    def xside(n, x):
        own = [xfaces[n]] + [side.reshape(-1, half, cout)[:, x] for side in zsides + ysides]
        return jnp.concatenate(own, axis=0)

    low, high = xside(0, 0), xside(1, half - 1)
    moments, xs = added_with_faces("gx", x_even, moments, low, high)
    total_cells = rows * depth * lax.axis_size("gx") * lax.axis_size("gy") * lax.axis_size("gz")
    result = block(
        total_cells, moments, norm_gain[None], norm_shift[None], feats, zs, ys, xs, second,
    )
    return jnp.transpose(result.reshape(depth, lines, half, cout), (3, 0, 1, 2))


def solution(mesh):
    in_specs = (P(None, "gz", "gy", "gx"), P(), P(), P(), P())
    out_specs = P(None, "gz", "gy", "gx")
    return jax.shard_map(body, mesh=mesh, in_specs=in_specs, out_specs=out_specs, check_vma=False)
```

```python
import functools

import jax
import jax.numpy as jnp
from jax import lax
from jax.experimental import pallas as pl
from jax.experimental.pallas import tpu as pltpu
from jax.sharding import PartitionSpec as P

NEWTON = 5
EPSILON = 1e-05
LEAK = 0.2
F32, BF16 = jnp.float32, jnp.bfloat16
MIB = 1024 * 1024


def places():
    even, inside = [], []
    for axis in ("gx", "gy", "gz"):
        size, place = lax.axis_size(axis), lax.axis_index(axis)
        even.append(lax.rem(place, 2) == 0 if size > 1 and power_of_two(size) else place >= 0)
        inside += [place > 0, place < size - 1]
    return even + inside


def in_vmem(*values):
    return [pltpu.with_memory_space_constraint(value, pltpu.VMEM) for value in values]


def dot(a, b, dims=((1,), (0,))):
    return lax.dot_general(a, b, (dims, ((), ())), preferred_element_type=F32)


def thirds(value):
    one = value.astype(BF16)
    rest = value - one.astype(F32)
    two = rest.astype(BF16)
    return one, two, (rest - two.astype(F32)).astype(BF16)


def dot_full(a, b):
    (a1, a2, a3), (b1, b2, b3) = a, b
    pair = jnp.concatenate([b1, b2], axis=1)
    main = dot(jnp.concatenate([a1, a2], axis=1), jnp.concatenate([pair, pair], axis=0))
    rest = dot(jnp.concatenate([a3, a1], axis=1), jnp.concatenate([b1, b3], axis=0))
    width = b1.shape[1]
    return main[:, :width] + (main[:, width:] + rest)


def split(value):
    hi = value.astype(BF16)
    lo = (value - hi.astype(F32)).astype(BF16)
    return hi, lo


def iota(shape, dim):
    return lax.broadcasted_iota(jnp.int32, shape, dim)


def pick_matrix(width):
    out, half = iota((width, width), 0), width // 2
    source = jnp.where(out < half, 2 * out, 2 * (out - half) + 1)
    return (source == iota((width, width), 1)).astype(F32).astype(BF16)


def turn_plane(pick, plane, rows_ref, cells_ref):
    cin, height, width = plane.shape
    half, last = width // 2, []
    rows_ref[...] = plane.astype(F32).reshape(cin * height, width)
    for pair in range(height // 4):
        lines = [rows_ref[pl.ds(4 * pair + k, cin, stride=height), :] for k in range(4)]
        turned = dot(pick, jnp.concatenate(lines, axis=0).astype(BF16), ((1,), (1,)))
        for k in range(2):
            span = pl.ds((2 * pair + k) * half, half)
            lanes = slice(2 * cin * k, 2 * cin * (k + 1))
            cells_ref[span, : 2 * cin] = turned[:half, lanes].astype(BF16)
            cells_ref[span, 2 * cin :] = turned[half:, lanes].astype(BF16)
            last.append(turned[width - 1 :, lanes])
    return jnp.concatenate(last, axis=0)


def faces_kernel(field_ref, cells_ref, yface_ref, xface_ref, flag_ref, rows_ref, edge_ref):
    cin, depth, height, width = field_ref.shape
    half, part = width // 2, edge_ref.shape[1] // cin
    for k, flag in enumerate(places()):
        flag_ref[k : k + 1, :] = jnp.full((1, flag_ref.shape[1]), flag.astype(jnp.int32)).astype(F32)
    pick = pick_matrix(width)
    xface_ref[...] = turn_plane(pick, field_ref[:, depth - 1], rows_ref, cells_ref).astype(BF16)
    for z in range(depth):
        edge_ref[z] = field_ref[:, z].astype(F32)[:, height - part :].reshape(cin * part, width)
    group = 4 if depth % 4 == 0 else 1
    for first in range(0, depth, group):
        lines = [edge_ref[first + k, pl.ds(part - 1, cin, stride=part), :] for k in range(group)]
        turned = dot(pick, jnp.concatenate(lines, axis=0).astype(BF16), ((1,), (1,)))
        for k in range(group):
            line = turned[:, cin * k : cin * (k + 1)]
            span = pl.ds((first + k) * half, half)
            yface_ref[span, :] = jnp.concatenate([line[:half], line[half:]], axis=1).astype(BF16)


def planes_kernel(field_ref, xlast_ref, cells_ref, xface_ref, rows_ref):
    xface_ref[field_ref.shape[1] - 1] = xlast_ref[...]
    pick = pick_matrix(field_ref.shape[3])
    for z in range(field_ref.shape[1] - 1):
        xface_ref[z] = turn_plane(pick, field_ref[:, z], rows_ref.at[z], cells_ref.at[z]).astype(BF16)


def relayout(field):
    cin, depth, height, width = field.shape
    half, lines = width // 2, height // 2
    part = 8 if height % 8 == 0 else height
    vmem = pl.BlockSpec(memory_space=pltpu.VMEM)
    faces = pl.pallas_call(
        faces_kernel,
        in_specs=[vmem],
        out_specs=[vmem] * 4,
        out_shape=[
            pltpu.VMEM((lines * half, 4 * cin), BF16),
            pltpu.VMEM((depth * half, 2 * cin), BF16),
            pltpu.VMEM((lines, 2 * cin), BF16),
            pltpu.VMEM((16, 2 * cin), F32),
        ],
        scratch_shapes=[pltpu.VMEM((cin * height, width), F32), pltpu.VMEM((depth, cin * part, width), F32)],
        compiler_params=pltpu.CompilerParams(vmem_limit_bytes=12 * MIB),
        name="faces",
    )(*in_vmem(field))
    planes = pl.pallas_call(
        planes_kernel,
        in_specs=[vmem] * 2,
        out_specs=[vmem] * 2,
        out_shape=[
            pltpu.VMEM((depth - 1, lines * half, 4 * cin), BF16),
            pltpu.VMEM((depth, lines, 2 * cin), BF16),
        ],
        scratch_shapes=[pltpu.VMEM((depth - 1, cin * height, width), F32)],
        compiler_params=pltpu.CompilerParams(vmem_limit_bytes=12 * MIB),
        name="planes",
    )(*in_vmem(field, faces[2]))
    return faces, planes


def moved_down(value):
    return jnp.where(iota(value.shape, 0) == 0, 0.0, pltpu.roll(value, 1, 0))


def line_sums(acc_ref, line, half, cout):
    span = pl.ds(line * half, half)
    straight = acc_ref[span, :cout]
    shifted = acc_ref[span, 2 * cout : 3 * cout]
    if line > 0:
        above = pl.ds((line - 1) * half, half)
        straight = straight + acc_ref[above, cout : 2 * cout]
        shifted = shifted + acc_ref[above, 3 * cout :]
    return straight + moved_down(shifted)


def interior_kernel(
    lines, cells_ref, last_ref, w_ref, v_ref, part_ref, stat_ref, wz_ref, wy_ref, wx_ref, v3_ref, w4_ref, acc_ref
):
    depth = (cells_ref.shape[0] + 1) // 2
    cin, cout = w_ref.shape[3:]
    rows = cells_ref.shape[1]
    half = rows // lines
    w4_ref[...] = jnp.zeros(w4_ref.shape, BF16)
    wx_ref[...] = jnp.zeros(wx_ref.shape, BF16)
    wy_ref[...] = jnp.zeros(wy_ref.shape, BF16)
    for dz in range(3):
        for px in range(2):
            for py in range(2):
                k = (2 * px + py) * cin
                w4_ref[dz, k : k + cin, :cout] = w_ref[dz, 1 + py, 1 + px]
                if py == 1:
                    w4_ref[dz, k : k + cin, cout : 2 * cout] = w_ref[dz, 0, 1 + px]
                if px == 1:
                    w4_ref[dz, k : k + cin, 2 * cout : 3 * cout] = w_ref[dz, 1 + py, 0]
                if px == 1 and py == 1:
                    w4_ref[dz, k : k + cin, 3 * cout :] = w_ref[dz, 0, 0]
            k = (2 * dz + px) * cin
            wy_ref[k : k + cin, :cout] = w_ref[dz, 0, 1 + px]
        k = (2 * dz + 1) * cin
        wy_ref[k : k + cin, cout:] = w_ref[dz, 0, 0]
        k = 4 * dz * cin
        wx_ref[k : k + cin, :] = w_ref[dz, 1, 0]
        wx_ref[k + cin : k + 2 * cin, :] = w_ref[dz, 2, 0]
        wx_ref[k + 3 * cin : k + 4 * cin, :] = w_ref[dz, 0, 0]
    wz_ref[...] = w4_ref[0]
    for dz in range(3):
        for dy in range(3):
            v3_ref[dy * 3 * cout : (dy + 1) * 3 * cout, (2 - dz) * cout : (3 - dz) * cout] = v_ref[dz, dy]
    for zo in range(depth):
        first = 0 if zo else 1
        planes = [cells_ref[z] if z < 2 * depth - 1 else last_ref[...] for z in range(2 * zo - 1 + first, 2 * zo + 2)]
        acc_ref[...] = dot(
            jnp.concatenate(planes, axis=1), w4_ref[first:].reshape((3 - first) * 4 * cin, 4 * cout)
        )
        for line in range(lines):
            part_ref[zo, pl.ds(line * half, half), :] = line_sums(acc_ref, line, half, cout)
    inner = (lines - 1) * half
    inside = iota((inner, cout), 0) % half != 0
    total = jnp.zeros((1, cout), F32)
    for zo in range(1, depth):
        total = total + jnp.sum(part_ref[zo, half:, :], axis=0, keepdims=True)
    offset = total * (1.0 / max(1, (depth - 1) * inner))
    gram, sums = jnp.zeros((cout, 2 * cout), F32), jnp.zeros((1, cout), F32)
    for zo in range(1, depth):
        value = jnp.where(inside, part_ref[zo, half:, :] - offset, 0.0)
        hi, lo = split(value)
        gram = gram + dot(hi, jnp.concatenate([hi, lo], axis=1), ((0,), (0,)))
        sums = sums + jnp.sum(value, axis=0, keepdims=True)
    stat_ref[:cout, :] = gram[:, :cout]
    stat_ref[cout : 2 * cout, :] = gram[:, cout:]
    stat_ref[2 * cout : 2 * cout + 8, :] = jnp.broadcast_to(sums, (8, cout))
    stat_ref[2 * cout + 8 :, :] = jnp.broadcast_to(offset, (8, cout))


def interior(lines, cells, last, weights, second):
    depth, rows, wide = cells.shape
    depth += 1
    cin, cout = weights.shape[3:]
    vmem = pl.BlockSpec(memory_space=pltpu.VMEM)
    flops = depth // 2 * rows * 3 * wide * 8 * cout
    return pl.pallas_call(
        functools.partial(interior_kernel, lines),
        in_specs=[vmem] * 4,
        out_specs=[vmem] * 6,
        out_shape=[
            pltpu.VMEM((depth // 2, rows, cout), F32),
            pltpu.VMEM((2 * cout + 16, cout), F32),
            pltpu.VMEM((wide, 4 * cout), BF16),
            pltpu.VMEM((6 * cin, 2 * cout), BF16),
            pltpu.VMEM((12 * cin, cout), BF16),
            pltpu.VMEM((9 * cout, 3 * cout), BF16),
        ],
        scratch_shapes=[pltpu.VMEM((3, wide, 4 * cout), BF16), pltpu.VMEM((rows, 4 * cout), F32)],
        compiler_params=pltpu.CompilerParams(vmem_limit_bytes=20 * MIB),
        cost_estimate=pl.CostEstimate(flops=flops, bytes_accessed=6 * MIB, transcendentals=0),
        name="interior",
    )(*in_vmem(cells, last), weights, second)


def finish_kernel(
    part_ref, stat_ref, zhalo_ref, yhalo_ref, yzhalo_ref, xhalo_ref, xzhalo_ref, wz_ref, wy_ref, wx_ref,
    feat_ref, mom_ref, xface_ref, acc_ref, rim_ref,
):
    depth, rows, cout = part_ref.shape
    half = yzhalo_ref.shape[0]
    lines = rows // half
    _, _, _, x_in, _, y_in, _, z_in, _ = places()
    zhalo = jnp.where(z_in, zhalo_ref[...], jnp.zeros(zhalo_ref.shape, BF16))
    yhalo = [yzhalo_ref[...]] + [yhalo_ref[z * half : (z + 1) * half, :] for z in range(2 * depth)]
    yhalo = [jnp.where(y_in, value, jnp.zeros_like(value)) for value in yhalo]
    yhalo[0] = jnp.where(z_in, yhalo[0], jnp.zeros_like(yhalo[0]))
    xhalo = jnp.where(x_in, xhalo_ref[...].astype(F32), 0.0)
    here = [jnp.where(jnp.logical_and(x_in, z_in), xzhalo_ref[...].astype(F32)[:lines], 0.0)]
    here += [xhalo[z * lines : (z + 1) * lines] for z in range(2 * depth)]
    spot = 2 * depth * lines
    over = [xhalo[spot + 2 * depth : spot + 2 * depth + 1]] + [xhalo[spot + z : spot + z + 1] for z in range(2 * depth)]
    over = [jnp.where(y_in, value, 0.0) for value in over]
    over[0] = jnp.where(z_in, over[0], 0.0)
    over = [jnp.concatenate([line, value[: lines - 1]], axis=0) for line, value in zip(over, here, strict=True)]
    xparts = []
    for zo in range(depth):
        row = [part for dz in range(3) for part in (here[2 * zo + dz], over[2 * zo + dz])]
        xparts.append(jnp.concatenate(row, axis=1))
    xsum = dot(jnp.concatenate(xparts, axis=0).astype(BF16), wx_ref[...])
    yparts = [jnp.concatenate(yhalo[2 * zo : 2 * zo + 3], axis=1) for zo in range(depth)]
    ysum = dot(jnp.concatenate(yparts, axis=0), wy_ref[...])
    acc_ref[...] = dot(zhalo, wz_ref[...])
    offset = stat_ref[2 * cout + 8 : 2 * cout + 9, :]
    rim_ref[...] = jnp.zeros(rim_ref.shape, F32)
    first = iota((8, cout), 0) == 0
    edges = rows + (depth - 1) * half
    for zo in range(depth):
        for line in range(lines):
            span = pl.ds(line * half, half)
            k = zo * lines + line
            if zo == 0 or line == 0:
                value = part_ref[zo, span, :]
                if zo == 0:
                    value = value + line_sums(acc_ref, line, half, cout)
                if line == 0:
                    more = ysum[zo * half : (zo + 1) * half]
                    value = value + (more[:, :cout] + moved_down(more[:, cout:]))
                value = value + jnp.where(iota((half, cout), 0) == 0, xsum[k : k + 1], 0.0)
                feat_ref[zo, span, :] = value
                spot = line * half if zo == 0 else rows + (zo - 1) * half
                rim_ref[spot : spot + half, :] = value - offset
                xface_ref[0, k : k + 1, :] = value[:1]
                xface_ref[1, k : k + 1, :] = value[half - 1 :]
            else:
                top = pl.ds(line * half, 8)
                value = part_ref[zo, top, :] + jnp.where(first, xsum[k : k + 1], 0.0)
                feat_ref[zo, top, :] = value
                feat_ref[zo, pl.ds(line * half + 8, half - 8), :] = part_ref[zo, pl.ds(line * half + 8, half - 8), :]
                spot = edges + (zo - 1) * (lines - 1) + line - 1
                rim_ref[spot : spot + 1, :] = value[:1] - offset
                xface_ref[0, k : k + 1, :] = value[:1]
                xface_ref[1, k : k + 1, :] = part_ref[zo, pl.ds((line + 1) * half - 1, 1), :]
    rim = rim_ref[...]
    hi, lo = split(rim)
    gram = dot(hi, jnp.concatenate([hi, lo], axis=1), ((0,), (0,)))
    cross = gram[:, cout:] + stat_ref[cout : 2 * cout, :]
    gram = gram[:, :cout] + stat_ref[:cout, :] + cross + cross.T
    sums = jnp.sum(rim, axis=0, keepdims=True) + stat_ref[2 * cout : 2 * cout + 1, :]
    total = sums + offset * float(depth * rows)
    eye = iota((cout, cout), 0) == iota((cout, cout), 1)
    sums_column = jnp.sum(jnp.where(eye, sums, 0.0), axis=1, keepdims=True)
    offset_column = jnp.sum(jnp.where(eye, offset, 0.0), axis=1, keepdims=True)
    gram = gram + (sums_column * offset + offset_column * total)
    left = iota((cout // 2, cout), 1) < cout // 2
    mom_ref[: cout // 2, :] = jnp.where(left, gram[: cout // 2], gram[cout // 2 :])
    mom_ref[cout // 2 :, :] = jnp.broadcast_to(total, (8, cout))


def finish(part, stats, zhalo, yhalo, yzhalo, xhalo, xzhalo, wz, wy, wx):
    depth, rows, cout = part.shape
    half = yzhalo.shape[0]
    lines = rows // half
    rim = rows + (depth - 1) * (half + lines - 1)
    vmem = pl.BlockSpec(memory_space=pltpu.VMEM)
    return pl.pallas_call(
        finish_kernel,
        in_specs=[vmem] * 10,
        out_specs=[vmem] * 3,
        out_shape=[
            pltpu.VMEM((depth, rows, cout), F32),
            pltpu.VMEM((cout // 2 + 8, cout), F32),
            pltpu.VMEM((2, depth * lines, cout), F32),
        ],
        scratch_shapes=[pltpu.VMEM((rows, 4 * cout), F32), pltpu.VMEM((rim + (-rim) % 16, cout), F32)],
        compiler_params=pltpu.CompilerParams(vmem_limit_bytes=16 * MIB),
        name="finish",
    )(*in_vmem(part, stats, zhalo, yhalo, yzhalo, xhalo, xzhalo, wz, wy, wx))


def block_kernel(
    total_cells,
    mom_ref, gain_ref, shift_ref, feat_ref, z1_ref, z2_ref, y1_ref, y2_ref, x1_ref, x2_ref, w_ref,
    out_ref, pad_ref, wide_ref, split_ref,
):
    depth, rows, cout = feat_ref.shape
    half = y1_ref.shape[0] // (depth + 2)
    lines = rows // half
    group = cout // 2
    square = (cout, cout)
    ri, ci = iota(square, 0), iota(square, 1)
    eye = ri == ci
    same = (ri < group) == (ci < group)
    moments = mom_ref[:group, :] * (1.0 / total_cells)
    average = mom_ref[group : group + 1, :] * (1.0 / total_cells)
    column = jnp.sum(jnp.where(eye, jnp.broadcast_to(average, square), 0.0), axis=1, keepdims=True)
    cov = jnp.concatenate([moments, moments], axis=0) - column * average
    cov = jnp.where(same, cov, 0.0) + jnp.where(eye, EPSILON, 0.0)
    diag = jnp.where(eye, cov, 0.0)
    trace0 = jnp.sum(jnp.sum(diag[:group], axis=1, keepdims=True), axis=0, keepdims=True)
    trace1 = jnp.sum(jnp.sum(diag[group:], axis=1, keepdims=True), axis=0, keepdims=True)
    trace = jnp.where(ri < group, trace0, trace1)
    scaled = cov / trace
    x_even, y_even, z_even, xb_in, xa_in, yb_in, ya_in, zb_in, za_in = places()
    starts, jobs, spot = [], [], 0

    def centre(read, start, count):
        hi, lo = split(read() - average)
        split_ref[start : start + count, :cout] = hi
        split_ref[start : start + count, cout:] = lo

    for n in range(depth):
        starts.append((spot, rows))
        jobs.append(functools.partial(centre, functools.partial(feat_ref.__getitem__, n), *starts[-1]))
        spot += rows
    for even, one_ref, two_ref in ((z_even, z1_ref, z2_ref), (y_even, y1_ref, y2_ref), (x_even, x1_ref, x2_ref)):
        for before, after in ((two_ref, one_ref), (one_ref, two_ref)):
            starts.append((spot, one_ref.shape[0]))
            read = lambda even=even, a=before, b=after: jnp.where(even, a[...], b[...])
            jobs.append(functools.partial(centre, read, *starts[-1]))
            spot += one_ref.shape[0]

    def some_jobs(count):
        for _ in range(min(count, len(jobs))):
            jobs.pop(0)()

    scaled_parts = thirds(scaled)
    mat = jnp.where(eye, 1.5, 0.0) - 0.5 * scaled
    for _ in range(NEWTON - 1):
        parts = thirds(mat)
        twice, once = dot_full(parts, parts), dot_full(parts, scaled_parts)
        some_jobs(1)
        mat = 1.5 * mat - 0.5 * dot_full(thirds(twice), thirds(once))
        some_jobs(2)
    some_jobs(len(jobs))
    gain = jnp.sum(jnp.where(eye, jnp.broadcast_to(gain_ref[...], square), 0.0), axis=1, keepdims=True)
    mat = mat / jnp.sqrt(trace) * gain
    hi, lo = split(mat)
    mixer = jnp.concatenate(
        [jnp.concatenate([hi, hi], axis=1), jnp.concatenate([lo, jnp.zeros_like(lo)], axis=1)], axis=0
    )
    shift = shift_ref[...]

    def whitened(n):
        start, count = starts[n]
        both = dot(split_ref[start : start + count, :], mixer, ((1,), (1,)))
        scaled = both[:, :cout] + both[:, cout:] + shift
        return jnp.where(scaled >= 0, scaled, LEAK * scaled)

    base = 8
    def put(zp, yp, middle, left, right, inside):
        l_in, r_in = xb_in, xa_in
        if inside is not None:
            middle = jnp.where(inside, middle, 0.0)
            l_in, r_in = jnp.logical_and(l_in, inside), jnp.logical_and(r_in, inside)
        pad_ref[zp, yp, base : base + half, :] = middle
        wide_ref[zp, yp * half : (yp + 1) * half, cout : 2 * cout] = middle.astype(BF16)
        pad_ref[zp, yp, base - 1 : base, :] = jnp.where(l_in, left, 0.0)
        pad_ref[zp, yp, base + half : base + half + 1, :] = jnp.where(r_in, right, 0.0)

    ysides = [whitened(depth + 2 + m) for m in range(2)]
    xsides = [whitened(depth + 4 + m) for m in range(2)]
    spots = [(z + 1, None) for z in range(depth)] + [(0, zb_in), (depth + 1, za_in)]
    for n, (zp, z_in) in enumerate(spots):
        plane = whitened(n)
        for y in range(lines):
            k = n * lines + y
            put(zp, y + 1, plane[y * half : (y + 1) * half], xsides[0][k : k + 1], xsides[1][k : k + 1], z_in)
        for m, (yp, y_in) in enumerate(((0, yb_in), (lines + 1, ya_in))):
            k = (depth + 2) * (lines + m) + n
            inside = y_in if z_in is None else jnp.logical_and(z_in, y_in)
            put(zp, yp, ysides[m][n * half : (n + 1) * half], xsides[0][k : k + 1], xsides[1][k : k + 1], inside)
    for zp in range(depth + 2):
        for yp in range(lines + 2):
            for dx in (0, 2):
                wide_ref[zp, yp * half : (yp + 1) * half, dx * cout : (dx + 1) * cout] = pad_ref[
                    zp, yp, base - 1 + dx : base - 1 + dx + half, :
                ].astype(BF16)
    sums = [None] * depth
    for zp in range(depth + 2):
        low, high = max(zp - 2, 0), min(zp, depth - 1)
        lanes = slice((low - zp + 2) * cout, (high - zp + 3) * cout)
        taken = [wide_ref[zp, dy * half : dy * half + rows, :] for dy in range(3)]
        got = dot(jnp.concatenate(taken, axis=1), w_ref[:, lanes])
        for n, z in enumerate(range(low, high + 1)):
            piece = got[:, n * cout : (n + 1) * cout]
            sums[z] = piece if sums[z] is None else sums[z] + piece
        if zp >= 2:
            out_ref[zp - 2] = sums[zp - 2].astype(BF16)


def block(total_cells, moments, gain, shift, feats, zs, ys, xs, weights):
    depth, rows, cout = feats.shape
    half = ys[0].shape[0] // (depth + 2)
    lines = rows // half
    vmem = pl.BlockSpec(memory_space=pltpu.VMEM)
    return pl.pallas_call(
        functools.partial(block_kernel, total_cells),
        in_specs=[vmem] * 11,
        out_specs=vmem,
        out_shape=jax.ShapeDtypeStruct((depth, rows, cout), BF16),
        scratch_shapes=[
            pltpu.VMEM((depth + 2, lines + 2, half + 16, cout), F32),
            pltpu.VMEM((depth + 2, (lines + 2) * half, 3 * cout), BF16),
            pltpu.VMEM((depth * rows + 2 * sum(pair[0].shape[0] for pair in (zs, ys, xs)), 2 * cout), BF16),
        ],
        compiler_params=pltpu.CompilerParams(vmem_limit_bytes=24 * MIB),
        name="block",
    )(moments, gain, shift, *in_vmem(feats, *zs, *ys, *xs, weights))


def power_of_two(size):
    return size & (size - 1) == 0


def first_pairs(axis):
    return [(i, i ^ 1) for i in range(lax.axis_size(axis))]


def second_pairs(axis):
    size = lax.axis_size(axis)
    return [(i, (i + 1 if i % 2 else i - 1) % size) for i in range(size)]


def second_face(axis, value):
    size = lax.axis_size(axis)
    inner = [(i, j) for i, j in second_pairs(axis) if abs(i - j) == 1]
    other = {"gz": "gy", "gy": "gx", "gx": "gy"}[axis]
    count = lax.axis_size(other)
    if count % 2:
        return lax.ppermute(value, axis, inner)
    place = (lambda k, i: i * count + k) if axis == "gx" else (lambda k, i: k * size + i)
    pairs = [(place(k, i), place(k, j)) for k in range(count) for i, j in inner]
    pairs += [(place(k, i), place(k ^ 1, i)) for k in range(count) for i in (0, size - 1)]
    return lax.ppermute(value, (axis, other) if axis == "gx" else (other, axis), pairs)


def faces(axis, even, low, high):
    size = lax.axis_size(axis)
    if size == 1:
        return low, high
    if not power_of_two(size):
        up = up_pairs(axis)
        return lax.ppermute(low, axis, [(j, i) for i, j in up]), lax.ppermute(high, axis, up)
    one = lax.ppermute(jnp.where(even, high, low), axis, first_pairs(axis))
    return one, one if size == 2 else second_face(axis, jnp.where(even, low, high))


def added(axis, value, first=True):
    size = lax.axis_size(axis)
    if size > 1 and not power_of_two(size):
        return lax.psum(value, axis)
    if first and size > 1:
        value = value + lax.ppermute(value, axis, first_pairs(axis))
    if size > 2:
        value = value + lax.ppermute(value, axis, second_pairs(axis))
    step = 4
    while step < size:
        value = value + lax.ppermute(value, axis, [(i, (i + step) % size) for i in range(size)])
        step *= 2
    return value


def added_with_faces(axis, even, value, low, high):
    size = lax.axis_size(axis)
    if size == 1 or not power_of_two(size):
        return added(axis, value), faces(axis, even, low, high)
    count = value.shape[0]
    both = jnp.concatenate([value, jnp.where(even, high, low)], axis=0)
    both = lax.ppermute(both, axis, first_pairs(axis))
    value, one = value + both[:count], both[count:]
    if size == 2:
        return value, (one, one)
    two = second_face(axis, jnp.where(even, low, high))
    return added(axis, value, first=False), (one, two)


def sided(even, pair):
    one, two = pair
    return jnp.where(even, two, one), jnp.where(even, one, two)


def up_pairs(axis):
    return [(i, i + 1) for i in range(lax.axis_size(axis) - 1)]


def ring(axis):
    size = lax.axis_size(axis)
    return [(i, (i + 1) % size) for i in range(size)]


def diagonal(first, second):
    n, m = lax.axis_size(first), lax.axis_size(second)
    return [(a * m + b, (a + 1) % n * m + (b + 1) % m) for a in range(n) for b in range(m)]


def stacked(parts):
    count = sum(part.shape[0] for part in parts)
    count += -count % 16
    total, spot, zero = None, 0, jnp.zeros((), parts[0].dtype)
    for part in parts:
        wide = lax.pad(part, zero, ((spot, count - spot - part.shape[0], 0), (0, 0, 0)))
        total = wide if total is None else total + wide
        spot += part.shape[0]
    return total


def body(field, conv_first, norm_gain, norm_shift, conv_second):
    cin, depth_in, height_in, width_in = field.shape
    cout = conv_second.shape[-1]
    depth, lines, half = depth_in // 2, height_in // 2, width_in // 2
    (last, yface, _, flags), (cells, xface) = relayout(field)
    x_even, y_even, z_even = (flags[k : k + 1, :] > 0 for k in range(3))
    yzhalo = lax.ppermute(yface[-half:], ("gy", "gz"), diagonal("gy", "gz"))
    zhalo = lax.ppermute(last, "gz", ring("gz"))
    yhalo = lax.ppermute(yface, "gy", ring("gy"))
    xzhalo = lax.ppermute(stacked([xface[-1]]), ("gx", "gz"), diagonal("gx", "gz"))
    xown = [xface.reshape(depth_in * lines, 2 * cin)]
    xown += [yhalo.reshape(depth_in, half, 2 * cin)[:, -1], yzhalo[-1:]]
    xhalo = lax.ppermute(stacked(xown), "gx", ring("gx"))

    part, stats, wz, wy, wx, second = interior(lines, cells, last, conv_first, conv_second.reshape(3, 3, 3 * cout, cout))
    feats, moments, xfaces = finish(part, stats, zhalo, yhalo, yzhalo, xhalo, xzhalo, wz, wy, wx)
    rows = lines * half
    zs = faces("gz", z_even, feats[0], feats[-1])
    moments = added("gz", moments)
    zsides = sided(z_even, zs)

    def yside(y):
        here = slice(y * half, (y + 1) * half)
        return jnp.concatenate([feats[z, here] for z in range(depth)] + [side[here] for side in zsides], axis=0)

    moments, ys = added_with_faces("gy", y_even, moments, yside(0), yside(lines - 1))
    ysides = sided(y_even, ys)

    def xside(n, x):
        own = [xfaces[n]] + [side.reshape(-1, half, cout)[:, x] for side in zsides + ysides]
        return stacked(own)

    low, high = xside(0, 0), xside(1, half - 1)
    moments, xs = added_with_faces("gx", x_even, moments, low, high)
    total_cells = rows * depth * lax.axis_size("gx") * lax.axis_size("gy") * lax.axis_size("gz")
    result = block(
        total_cells, moments, norm_gain[None], norm_shift[None], feats, zs, ys, xs, second,
    )
    return jnp.transpose(result.reshape(depth, lines, half, cout), (3, 0, 1, 2))


def solution(mesh):
    in_specs = (P(None, "gz", "gy", "gx"), P(), P(), P(), P())
    out_specs = P(None, "gz", "gy", "gx")
    return jax.shard_map(body, mesh=mesh, in_specs=in_specs, out_specs=out_specs, check_vma=False)
```

```python
import functools

import jax
import jax.numpy as jnp
from jax import lax
from jax.experimental import pallas as pl
from jax.experimental.pallas import tpu as pltpu
from jax.sharding import PartitionSpec as P

NEWTON = 5
EPSILON = 1e-05
LEAK = 0.2
F32, BF16 = jnp.float32, jnp.bfloat16
MIB = 1024 * 1024


def places():
    even, inside = [], []
    for axis in ("gx", "gy", "gz"):
        size, place = lax.axis_size(axis), lax.axis_index(axis)
        even.append(lax.rem(place, 2) == 0 if size > 1 and power_of_two(size) else place >= 0)
        inside += [place > 0, place < size - 1]
    return even + inside


def in_vmem(*values):
    return [pltpu.with_memory_space_constraint(value, pltpu.VMEM) for value in values]


def dot(a, b, dims=((1,), (0,))):
    return lax.dot_general(a, b, (dims, ((), ())), preferred_element_type=F32)


def thirds(value):
    one = value.astype(BF16).astype(F32)
    rest = value - one
    two = rest.astype(BF16).astype(F32)
    return one, two, rest - two


def as_left(parts):
    one, two, three = (part.astype(BF16) for part in parts)
    return jnp.concatenate([one, two], axis=1), jnp.concatenate([three, one], axis=1)


def as_right(parts):
    count, width = parts[0].shape
    left = iota((count, width), 1) < width // 2
    one, two, three = (
        jnp.concatenate([jnp.where(left, part, 0.0), jnp.where(left, 0.0, part)], axis=0).astype(BF16) for part in parts
    )
    pair = jnp.concatenate([one, two], axis=1)
    return jnp.concatenate([pair, pair], axis=0), jnp.concatenate([one, three], axis=0)


def dot_blocks(a, b):
    main, rest = dot(a[0], b[0]), dot(a[1], b[1])
    width = rest.shape[1]
    return main[:, :width] + (main[:, width:] + rest)


def split(value):
    hi = value.astype(BF16)
    lo = (value - hi.astype(F32)).astype(BF16)
    return hi, lo


def iota(shape, dim):
    return lax.broadcasted_iota(jnp.int32, shape, dim)


def pick_matrix(width):
    out, half = iota((width, width), 0), width // 2
    source = jnp.where(out < half, 2 * out, 2 * (out - half) + 1)
    return (source == iota((width, width), 1)).astype(F32).astype(BF16)


def turn_plane(pick, plane, rows_ref, cells_ref):
    cin, height, width = plane.shape
    half, last = width // 2, []
    rows_ref[...] = plane.astype(F32).reshape(cin * height, width)
    for pair in range(height // 4):
        lines = [rows_ref[pl.ds(4 * pair + k, cin, stride=height), :] for k in range(4)]
        turned = dot(pick, jnp.concatenate(lines, axis=0).astype(BF16), ((1,), (1,)))
        for k in range(2):
            span = pl.ds((2 * pair + k) * half, half)
            lanes = slice(2 * cin * k, 2 * cin * (k + 1))
            cells_ref[span, : 2 * cin] = turned[:half, lanes].astype(BF16)
            cells_ref[span, 2 * cin :] = turned[half:, lanes].astype(BF16)
            last.append(turned[width - 1 :, lanes])
    return jnp.concatenate(last, axis=0)


def faces_kernel(field_ref, cells_ref, yface_ref, xface_ref, flag_ref, rows_ref, edge_ref):
    cin, depth, height, width = field_ref.shape
    half, part = width // 2, edge_ref.shape[1] // cin
    for k, flag in enumerate(places()):
        flag_ref[k : k + 1, :] = jnp.full((1, flag_ref.shape[1]), flag.astype(jnp.int32)).astype(F32)
    pick = pick_matrix(width)
    xface_ref[...] = turn_plane(pick, field_ref[:, depth - 1], rows_ref, cells_ref).astype(BF16)
    for z in range(depth):
        edge_ref[z] = field_ref[:, z].astype(F32)[:, height - part :].reshape(cin * part, width)
    group = 4 if depth % 4 == 0 else 1
    for first in range(0, depth, group):
        lines = [edge_ref[first + k, pl.ds(part - 1, cin, stride=part), :] for k in range(group)]
        turned = dot(pick, jnp.concatenate(lines, axis=0).astype(BF16), ((1,), (1,)))
        for k in range(group):
            line = turned[:, cin * k : cin * (k + 1)]
            span = pl.ds((first + k) * half, half)
            yface_ref[span, :] = jnp.concatenate([line[:half], line[half:]], axis=1).astype(BF16)


def planes_kernel(field_ref, xlast_ref, cells_ref, xface_ref, rows_ref):
    xface_ref[field_ref.shape[1] - 1] = xlast_ref[...]
    pick = pick_matrix(field_ref.shape[3])
    for z in range(field_ref.shape[1] - 1):
        xface_ref[z] = turn_plane(pick, field_ref[:, z], rows_ref.at[z], cells_ref.at[z]).astype(BF16)


def relayout(field):
    cin, depth, height, width = field.shape
    half, lines = width // 2, height // 2
    part = 8 if height % 8 == 0 else height
    vmem = pl.BlockSpec(memory_space=pltpu.VMEM)
    faces = pl.pallas_call(
        faces_kernel,
        in_specs=[vmem],
        out_specs=[vmem] * 4,
        out_shape=[
            pltpu.VMEM((lines * half, 4 * cin), BF16),
            pltpu.VMEM((depth * half, 2 * cin), BF16),
            pltpu.VMEM((lines, 2 * cin), BF16),
            pltpu.VMEM((16, 2 * cin), F32),
        ],
        scratch_shapes=[pltpu.VMEM((cin * height, width), F32), pltpu.VMEM((depth, cin * part, width), F32)],
        compiler_params=pltpu.CompilerParams(vmem_limit_bytes=12 * MIB),
        name="faces",
    )(*in_vmem(field))
    planes = pl.pallas_call(
        planes_kernel,
        in_specs=[vmem] * 2,
        out_specs=[vmem] * 2,
        out_shape=[
            pltpu.VMEM((depth - 1, lines * half, 4 * cin), BF16),
            pltpu.VMEM((depth, lines, 2 * cin), BF16),
        ],
        scratch_shapes=[pltpu.VMEM((depth - 1, cin * height, width), F32)],
        compiler_params=pltpu.CompilerParams(vmem_limit_bytes=12 * MIB),
        name="planes",
    )(*in_vmem(field, faces[2]))
    return faces, planes


def moved_down(value):
    return jnp.where(iota(value.shape, 0) == 0, 0.0, pltpu.roll(value, 1, 0))


def line_sums(acc_ref, line, half, cout):
    span = pl.ds(line * half, half)
    straight = acc_ref[span, :cout]
    shifted = acc_ref[span, 2 * cout : 3 * cout]
    if line > 0:
        above = pl.ds((line - 1) * half, half)
        straight = straight + acc_ref[above, cout : 2 * cout]
        shifted = shifted + acc_ref[above, 3 * cout :]
    return straight + moved_down(shifted)


def interior_kernel(
    lines, cells_ref, last_ref, w_ref, v_ref, part_ref, stat_ref, wz_ref, wy_ref, wx_ref, v3_ref, w4_ref, acc_ref
):
    depth = (cells_ref.shape[0] + 1) // 2
    cin, cout = w_ref.shape[3:]
    rows = cells_ref.shape[1]
    half = rows // lines
    w4_ref[...] = jnp.zeros(w4_ref.shape, BF16)
    wx_ref[...] = jnp.zeros(wx_ref.shape, BF16)
    wy_ref[...] = jnp.zeros(wy_ref.shape, BF16)
    for dz in range(3):
        for px in range(2):
            for py in range(2):
                k = (2 * px + py) * cin
                w4_ref[dz, k : k + cin, :cout] = w_ref[dz, 1 + py, 1 + px]
                if py == 1:
                    w4_ref[dz, k : k + cin, cout : 2 * cout] = w_ref[dz, 0, 1 + px]
                if px == 1:
                    w4_ref[dz, k : k + cin, 2 * cout : 3 * cout] = w_ref[dz, 1 + py, 0]
                if px == 1 and py == 1:
                    w4_ref[dz, k : k + cin, 3 * cout :] = w_ref[dz, 0, 0]
            k = (2 * dz + px) * cin
            wy_ref[k : k + cin, :cout] = w_ref[dz, 0, 1 + px]
        k = (2 * dz + 1) * cin
        wy_ref[k : k + cin, cout:] = w_ref[dz, 0, 0]
        k = 4 * dz * cin
        wx_ref[k : k + cin, :] = w_ref[dz, 1, 0]
        wx_ref[k + cin : k + 2 * cin, :] = w_ref[dz, 2, 0]
        wx_ref[k + 3 * cin : k + 4 * cin, :] = w_ref[dz, 0, 0]
    wz_ref[...] = w4_ref[0]
    for dz in range(3):
        for dy in range(3):
            v3_ref[dy * 3 * cout : (dy + 1) * 3 * cout, (2 - dz) * cout : (3 - dz) * cout] = v_ref[dz, dy]
    for zo in range(depth):
        first = 0 if zo else 1
        planes = [cells_ref[z] if z < 2 * depth - 1 else last_ref[...] for z in range(2 * zo - 1 + first, 2 * zo + 2)]
        acc_ref[...] = dot(
            jnp.concatenate(planes, axis=1), w4_ref[first:].reshape((3 - first) * 4 * cin, 4 * cout)
        )
        for line in range(lines):
            part_ref[zo, pl.ds(line * half, half), :] = line_sums(acc_ref, line, half, cout)
    inner = (lines - 1) * half
    inside = iota((inner, cout), 0) % half != 0
    total = jnp.zeros((1, cout), F32)
    for zo in range(1, depth):
        total = total + jnp.sum(part_ref[zo, half:, :], axis=0, keepdims=True)
    offset = total * (1.0 / max(1, (depth - 1) * inner))
    gram, sums = jnp.zeros((cout, 2 * cout), F32), jnp.zeros((1, cout), F32)
    for zo in range(1, depth):
        value = jnp.where(inside, part_ref[zo, half:, :] - offset, 0.0)
        hi, lo = split(value)
        gram = gram + dot(hi, jnp.concatenate([hi, lo], axis=1), ((0,), (0,)))
        sums = sums + jnp.sum(value, axis=0, keepdims=True)
    stat_ref[:cout, :] = gram[:, :cout]
    stat_ref[cout : 2 * cout, :] = gram[:, cout:]
    stat_ref[2 * cout : 2 * cout + 8, :] = jnp.broadcast_to(sums, (8, cout))
    stat_ref[2 * cout + 8 :, :] = jnp.broadcast_to(offset, (8, cout))


def interior(lines, cells, last, weights, second):
    depth, rows, wide = cells.shape
    depth += 1
    cin, cout = weights.shape[3:]
    vmem = pl.BlockSpec(memory_space=pltpu.VMEM)
    flops = depth // 2 * rows * 3 * wide * 8 * cout
    return pl.pallas_call(
        functools.partial(interior_kernel, lines),
        in_specs=[vmem] * 4,
        out_specs=[vmem] * 6,
        out_shape=[
            pltpu.VMEM((depth // 2, rows, cout), F32),
            pltpu.VMEM((2 * cout + 16, cout), F32),
            pltpu.VMEM((wide, 4 * cout), BF16),
            pltpu.VMEM((6 * cin, 2 * cout), BF16),
            pltpu.VMEM((12 * cin, cout), BF16),
            pltpu.VMEM((9 * cout, 3 * cout), BF16),
        ],
        scratch_shapes=[pltpu.VMEM((3, wide, 4 * cout), BF16), pltpu.VMEM((rows, 4 * cout), F32)],
        compiler_params=pltpu.CompilerParams(vmem_limit_bytes=20 * MIB),
        cost_estimate=pl.CostEstimate(flops=flops, bytes_accessed=6 * MIB, transcendentals=0),
        name="interior",
    )(*in_vmem(cells, last), weights, second)


def finish_kernel(
    part_ref, stat_ref, zhalo_ref, yhalo_ref, yzhalo_ref, xhalo_ref, xzhalo_ref, wz_ref, wy_ref, wx_ref,
    feat_ref, mom_ref, xface_ref, acc_ref, rim_ref,
):
    depth, rows, cout = part_ref.shape
    half = yzhalo_ref.shape[0]
    lines = rows // half
    _, _, _, x_in, _, y_in, _, z_in, _ = places()
    zhalo = jnp.where(z_in, zhalo_ref[...], jnp.zeros(zhalo_ref.shape, BF16))
    yhalo = [yzhalo_ref[...]] + [yhalo_ref[z * half : (z + 1) * half, :] for z in range(2 * depth)]
    yhalo = [jnp.where(y_in, value, jnp.zeros_like(value)) for value in yhalo]
    yhalo[0] = jnp.where(z_in, yhalo[0], jnp.zeros_like(yhalo[0]))
    xhalo = jnp.where(x_in, xhalo_ref[...].astype(F32), 0.0)
    here = [jnp.where(jnp.logical_and(x_in, z_in), xzhalo_ref[...].astype(F32)[:lines], 0.0)]
    here += [xhalo[z * lines : (z + 1) * lines] for z in range(2 * depth)]
    spot = 2 * depth * lines
    over = [xhalo[spot + 2 * depth : spot + 2 * depth + 1]] + [xhalo[spot + z : spot + z + 1] for z in range(2 * depth)]
    over = [jnp.where(y_in, value, 0.0) for value in over]
    over[0] = jnp.where(z_in, over[0], 0.0)
    over = [jnp.concatenate([line, value[: lines - 1]], axis=0) for line, value in zip(over, here, strict=True)]
    xparts = []
    for zo in range(depth):
        row = [part for dz in range(3) for part in (here[2 * zo + dz], over[2 * zo + dz])]
        xparts.append(jnp.concatenate(row, axis=1))
    xsum = dot(jnp.concatenate(xparts, axis=0).astype(BF16), wx_ref[...])
    yparts = [jnp.concatenate(yhalo[2 * zo : 2 * zo + 3], axis=1) for zo in range(depth)]
    ysum = dot(jnp.concatenate(yparts, axis=0), wy_ref[...])
    acc_ref[...] = dot(zhalo, wz_ref[...])
    offset = stat_ref[2 * cout + 8 : 2 * cout + 9, :]
    rim_ref[...] = jnp.zeros(rim_ref.shape, F32)
    first = iota((8, cout), 0) == 0
    edges = rows + (depth - 1) * half
    for zo in range(depth):
        for line in range(lines):
            span = pl.ds(line * half, half)
            k = zo * lines + line
            if zo == 0 or line == 0:
                value = part_ref[zo, span, :]
                if zo == 0:
                    value = value + line_sums(acc_ref, line, half, cout)
                if line == 0:
                    more = ysum[zo * half : (zo + 1) * half]
                    value = value + (more[:, :cout] + moved_down(more[:, cout:]))
                value = value + jnp.where(iota((half, cout), 0) == 0, xsum[k : k + 1], 0.0)
                feat_ref[zo, span, :] = value
                spot = line * half if zo == 0 else rows + (zo - 1) * half
                rim_ref[spot : spot + half, :] = value - offset
                xface_ref[0, k : k + 1, :] = value[:1]
                xface_ref[1, k : k + 1, :] = value[half - 1 :]
            else:
                top = pl.ds(line * half, 8)
                value = part_ref[zo, top, :] + jnp.where(first, xsum[k : k + 1], 0.0)
                feat_ref[zo, top, :] = value
                feat_ref[zo, pl.ds(line * half + 8, half - 8), :] = part_ref[zo, pl.ds(line * half + 8, half - 8), :]
                spot = edges + (zo - 1) * (lines - 1) + line - 1
                rim_ref[spot : spot + 1, :] = value[:1] - offset
                xface_ref[0, k : k + 1, :] = value[:1]
                xface_ref[1, k : k + 1, :] = part_ref[zo, pl.ds((line + 1) * half - 1, 1), :]
    rim = rim_ref[...]
    hi, lo = split(rim)
    gram = dot(hi, jnp.concatenate([hi, lo], axis=1), ((0,), (0,)))
    cross = gram[:, cout:] + stat_ref[cout : 2 * cout, :]
    gram = gram[:, :cout] + stat_ref[:cout, :] + cross + cross.T
    sums = jnp.sum(rim, axis=0, keepdims=True) + stat_ref[2 * cout : 2 * cout + 1, :]
    total = sums + offset * float(depth * rows)
    eye = iota((cout, cout), 0) == iota((cout, cout), 1)
    sums_column = jnp.sum(jnp.where(eye, sums, 0.0), axis=1, keepdims=True)
    offset_column = jnp.sum(jnp.where(eye, offset, 0.0), axis=1, keepdims=True)
    gram = gram + (sums_column * offset + offset_column * total)
    left = iota((cout // 2, cout), 1) < cout // 2
    mom_ref[: cout // 2, :] = jnp.where(left, gram[: cout // 2], gram[cout // 2 :])
    mom_ref[cout // 2 :, :] = jnp.broadcast_to(total, (8, cout))


def finish(part, stats, zhalo, yhalo, yzhalo, xhalo, xzhalo, wz, wy, wx):
    depth, rows, cout = part.shape
    half = yzhalo.shape[0]
    lines = rows // half
    rim = rows + (depth - 1) * (half + lines - 1)
    vmem = pl.BlockSpec(memory_space=pltpu.VMEM)
    return pl.pallas_call(
        finish_kernel,
        in_specs=[vmem] * 10,
        out_specs=[vmem] * 3,
        out_shape=[
            pltpu.VMEM((depth, rows, cout), F32),
            pltpu.VMEM((cout // 2 + 8, cout), F32),
            pltpu.VMEM((2, depth * lines, cout), F32),
        ],
        scratch_shapes=[pltpu.VMEM((rows, 4 * cout), F32), pltpu.VMEM((rim + (-rim) % 16, cout), F32)],
        compiler_params=pltpu.CompilerParams(vmem_limit_bytes=16 * MIB),
        name="finish",
    )(*in_vmem(part, stats, zhalo, yhalo, yzhalo, xhalo, xzhalo, wz, wy, wx))


def block_kernel(
    total_cells,
    mom_ref, gain_ref, shift_ref, feat_ref, z1_ref, z2_ref, y1_ref, y2_ref, x1_ref, x2_ref, w_ref,
    out_ref, pad_ref, wide_ref, split_ref, done_ref, sem_ref,
):
    depth, rows, cout = feat_ref.shape
    half = y1_ref.shape[0] // (depth + 2)
    lines = rows // half
    group = cout // 2
    side = (group, cout)
    left = iota(side, 1) < group
    eye = iota(side, 0) == iota(side, 1) % group
    moments = mom_ref[:group, :] * (1.0 / total_cells)
    average = mom_ref[group : group + 1, :] * (1.0 / total_cells)

    def own(value, fill=0.0):
        one = jnp.sum(jnp.where(left, value, fill), axis=1, keepdims=True)
        two = jnp.sum(jnp.where(left, fill, value), axis=1, keepdims=True)
        return jnp.where(left, one, two)

    column = own(jnp.where(eye, average, 0.0))
    cov = moments - column * average + jnp.where(eye, EPSILON, 0.0)
    trace = jnp.sum(own(jnp.where(eye, cov, 0.0)), axis=0, keepdims=True)
    scaled = cov / trace
    x_even, y_even, z_even, xb_in, xa_in, yb_in, ya_in, zb_in, za_in = places()
    starts, jobs, spot = [], [], 0

    def centre(read, start, count):
        hi, lo = split(read() - average)
        split_ref[start : start + count, :cout] = hi
        split_ref[start : start + count, cout:] = lo

    for n in range(depth):
        starts.append((spot, rows))
        jobs.append(functools.partial(centre, functools.partial(feat_ref.__getitem__, n), *starts[-1]))
        spot += rows
    for even, one_ref, two_ref in ((z_even, z1_ref, z2_ref), (y_even, y1_ref, y2_ref), (x_even, x1_ref, x2_ref)):
        for before, after in ((two_ref, one_ref), (one_ref, two_ref)):
            starts.append((spot, one_ref.shape[0]))
            read = lambda even=even, a=before, b=after: jnp.where(even, a[...], b[...])
            jobs.append(functools.partial(centre, read, *starts[-1]))
            spot += one_ref.shape[0]

    def some_jobs(count):
        for _ in range(min(count, len(jobs))):
            jobs.pop(0)()

    scaled_right = as_right(thirds(scaled))
    mat = jnp.where(eye, 1.5, 0.0) - 0.5 * scaled
    for _ in range(NEWTON - 1):
        parts = thirds(mat)
        taken = as_left(parts)
        once = dot_blocks(taken, scaled_right)
        twice = dot_blocks(taken, as_right(parts))
        mat = 1.5 * mat - 0.5 * dot_blocks(as_left(thirds(twice)), as_right(thirds(once)))
    some_jobs(len(jobs))
    mat = mat / jnp.sqrt(trace) * own(jnp.where(eye, gain_ref[...], 0.0))
    mat = jnp.concatenate([jnp.where(left, mat, 0.0), jnp.where(left, 0.0, mat)], axis=0)
    hi, lo = split(mat)
    mixer = jnp.concatenate(
        [jnp.concatenate([hi, hi], axis=1), jnp.concatenate([lo, jnp.zeros_like(lo)], axis=1)], axis=0
    )
    shift = shift_ref[...]

    def whitened(n):
        start, count = starts[n]
        both = dot(split_ref[start : start + count, :], mixer, ((1,), (1,)))
        scaled = both[:, :cout] + both[:, cout:] + shift
        return jnp.where(scaled >= 0, scaled, LEAK * scaled)

    base = 8
    def put(zp, yp, middle, left, right, inside):
        l_in, r_in = xb_in, xa_in
        if inside is not None:
            middle = jnp.where(inside, middle, 0.0)
            l_in, r_in = jnp.logical_and(l_in, inside), jnp.logical_and(r_in, inside)
        pad_ref[zp, yp, base : base + half, :] = middle
        wide_ref[zp, yp * half : (yp + 1) * half, cout : 2 * cout] = middle.astype(BF16)
        pad_ref[zp, yp, base - 1 : base, :] = jnp.where(l_in, left, 0.0)
        pad_ref[zp, yp, base + half : base + half + 1, :] = jnp.where(r_in, right, 0.0)

    ysides = [whitened(depth + 2 + m) for m in range(2)]
    xsides = [whitened(depth + 4 + m) for m in range(2)]
    spots = [(z + 1, None) for z in range(depth)] + [(0, zb_in), (depth + 1, za_in)]
    for n, (zp, z_in) in enumerate(spots):
        plane = whitened(n)
        for y in range(lines):
            k = n * lines + y
            put(zp, y + 1, plane[y * half : (y + 1) * half], xsides[0][k : k + 1], xsides[1][k : k + 1], z_in)
        for m, (yp, y_in) in enumerate(((0, yb_in), (lines + 1, ya_in))):
            k = (depth + 2) * (lines + m) + n
            inside = y_in if z_in is None else jnp.logical_and(z_in, y_in)
            put(zp, yp, ysides[m][n * half : (n + 1) * half], xsides[0][k : k + 1], xsides[1][k : k + 1], inside)
    for zp in range(depth + 2):
        for yp in range(lines + 2):
            for dx in (0, 2):
                wide_ref[zp, yp * half : (yp + 1) * half, dx * cout : (dx + 1) * cout] = pad_ref[
                    zp, yp, base - 1 + dx : base - 1 + dx + half, :
                ].astype(BF16)
    sums, copies = [None] * depth, []
    for zp in range(depth + 2):
        low, high = max(zp - 2, 0), min(zp, depth - 1)
        lanes = slice((low - zp + 2) * cout, (high - zp + 3) * cout)
        taken = [wide_ref[zp, dy * half : dy * half + rows, :] for dy in range(3)]
        got = dot(jnp.concatenate(taken, axis=1), w_ref[:, lanes])
        for n, z in enumerate(range(low, high + 1)):
            piece = got[:, n * cout : (n + 1) * cout]
            sums[z] = piece if sums[z] is None else sums[z] + piece
        if zp >= 2:
            done_ref[zp - 2] = sums[zp - 2].astype(BF16)
            copies.append(pltpu.make_async_copy(done_ref.at[zp - 2], out_ref.at[zp - 2], sem_ref.at[zp - 2]))
            copies[-1].start()
    for copy in copies:
        copy.wait()


def block(total_cells, moments, gain, shift, feats, zs, ys, xs, weights):
    depth, rows, cout = feats.shape
    half = ys[0].shape[0] // (depth + 2)
    lines = rows // half
    vmem = pl.BlockSpec(memory_space=pltpu.VMEM)
    return pl.pallas_call(
        functools.partial(block_kernel, total_cells),
        in_specs=[vmem] * 11,
        out_specs=pl.BlockSpec(memory_space=pl.ANY),
        out_shape=jax.ShapeDtypeStruct((depth, rows, cout), BF16),
        scratch_shapes=[
            pltpu.VMEM((depth + 2, lines + 2, half + 16, cout), F32),
            pltpu.VMEM((depth + 2, (lines + 2) * half, 3 * cout), BF16),
            pltpu.VMEM((depth * rows + 2 * sum(pair[0].shape[0] for pair in (zs, ys, xs)), 2 * cout), BF16),
            pltpu.VMEM((depth, rows, cout), BF16),
            pltpu.SemaphoreType.DMA((depth,)),
        ],
        compiler_params=pltpu.CompilerParams(vmem_limit_bytes=24 * MIB),
        name="block",
    )(moments, gain, shift, *in_vmem(feats, *zs, *ys, *xs, weights))


def power_of_two(size):
    return size & (size - 1) == 0


def first_pairs(axis):
    return [(i, i ^ 1) for i in range(lax.axis_size(axis))]


def second_pairs(axis):
    size = lax.axis_size(axis)
    return [(i, (i + 1 if i % 2 else i - 1) % size) for i in range(size)]


def second_face(axis, value):
    size = lax.axis_size(axis)
    inner = [(i, j) for i, j in second_pairs(axis) if abs(i - j) == 1]
    other = {"gz": "gy", "gy": "gx", "gx": "gy"}[axis]
    count = lax.axis_size(other)
    if count % 2:
        return lax.ppermute(value, axis, inner)
    place = (lambda k, i: i * count + k) if axis == "gx" else (lambda k, i: k * size + i)
    pairs = [(place(k, i), place(k, j)) for k in range(count) for i, j in inner]
    pairs += [(place(k, i), place(k ^ 1, i)) for k in range(count) for i in (0, size - 1)]
    return lax.ppermute(value, (axis, other) if axis == "gx" else (other, axis), pairs)


def faces(axis, even, low, high):
    size = lax.axis_size(axis)
    if size == 1:
        return low, high
    if not power_of_two(size):
        up = up_pairs(axis)
        return lax.ppermute(low, axis, [(j, i) for i, j in up]), lax.ppermute(high, axis, up)
    one = lax.ppermute(jnp.where(even, high, low), axis, first_pairs(axis))
    return one, one if size == 2 else second_face(axis, jnp.where(even, low, high))


def added(axis, value, first=True):
    size = lax.axis_size(axis)
    if size > 1 and not power_of_two(size):
        return lax.psum(value, axis)
    if first and size > 1:
        value = value + lax.ppermute(value, axis, first_pairs(axis))
    if size > 2:
        value = value + lax.ppermute(value, axis, second_pairs(axis))
    step = 4
    while step < size:
        value = value + lax.ppermute(value, axis, [(i, (i + step) % size) for i in range(size)])
        step *= 2
    return value


def added_with_faces(axis, even, value, low, high):
    size = lax.axis_size(axis)
    if size == 1 or not power_of_two(size):
        return added(axis, value), faces(axis, even, low, high)
    count = value.shape[0]
    both = jnp.concatenate([value, jnp.where(even, high, low)], axis=0)
    both = lax.ppermute(both, axis, first_pairs(axis))
    value, one = value + both[:count], both[count:]
    if size == 2:
        return value, (one, one)
    two = second_face(axis, jnp.where(even, low, high))
    return added(axis, value, first=False), (one, two)


def sided(even, pair):
    one, two = pair
    return jnp.where(even, two, one), jnp.where(even, one, two)


def up_pairs(axis):
    return [(i, i + 1) for i in range(lax.axis_size(axis) - 1)]


def ring(axis):
    size = lax.axis_size(axis)
    return [(i, (i + 1) % size) for i in range(size)]


def diagonal(first, second):
    n, m = lax.axis_size(first), lax.axis_size(second)
    return [(a * m + b, (a + 1) % n * m + (b + 1) % m) for a in range(n) for b in range(m)]


def stacked(parts):
    count = sum(part.shape[0] for part in parts)
    count += -count % 16
    total, spot, zero = None, 0, jnp.zeros((), parts[0].dtype)
    for part in parts:
        wide = lax.pad(part, zero, ((spot, count - spot - part.shape[0], 0), (0, 0, 0)))
        total = wide if total is None else total + wide
        spot += part.shape[0]
    return total


def body(field, conv_first, norm_gain, norm_shift, conv_second):
    cin, depth_in, height_in, width_in = field.shape
    cout = conv_second.shape[-1]
    depth, lines, half = depth_in // 2, height_in // 2, width_in // 2
    (last, yface, _, flags), (cells, xface) = relayout(field)
    x_even, y_even, z_even = (flags[k : k + 1, :] > 0 for k in range(3))
    yzhalo = lax.ppermute(yface[-half:], ("gy", "gz"), diagonal("gy", "gz"))
    zhalo = lax.ppermute(last, "gz", ring("gz"))
    yhalo = lax.ppermute(yface, "gy", ring("gy"))
    xzhalo = lax.ppermute(stacked([xface[-1]]), ("gx", "gz"), diagonal("gx", "gz"))
    xown = [xface.reshape(depth_in * lines, 2 * cin)]
    xown += [yhalo.reshape(depth_in, half, 2 * cin)[:, -1], yzhalo[-1:]]
    xhalo = lax.ppermute(stacked(xown), "gx", ring("gx"))

    part, stats, wz, wy, wx, second = interior(lines, cells, last, conv_first, conv_second.reshape(3, 3, 3 * cout, cout))
    feats, moments, xfaces = finish(part, stats, zhalo, yhalo, yzhalo, xhalo, xzhalo, wz, wy, wx)
    rows = lines * half
    zs = faces("gz", z_even, feats[0], feats[-1])
    moments = added("gz", moments)
    zsides = sided(z_even, zs)

    def yside(y):
        here = slice(y * half, (y + 1) * half)
        return jnp.concatenate([feats[z, here] for z in range(depth)] + [side[here] for side in zsides], axis=0)

    moments, ys = added_with_faces("gy", y_even, moments, yside(0), yside(lines - 1))
    ysides = sided(y_even, ys)

    def xside(n, x):
        own = [xfaces[n]] + [side.reshape(-1, half, cout)[:, x] for side in zsides + ysides]
        return stacked(own)

    low, high = xside(0, 0), xside(1, half - 1)
    moments, xs = added_with_faces("gx", x_even, moments, low, high)
    total_cells = rows * depth * lax.axis_size("gx") * lax.axis_size("gy") * lax.axis_size("gz")
    result = block(
        total_cells, moments, norm_gain[None], norm_shift[None], feats, zs, ys, xs, second,
    )
    return jnp.transpose(result.reshape(depth, lines, half, cout), (3, 0, 1, 2))


def solution(mesh):
    in_specs = (P(None, "gz", "gy", "gx"), P(), P(), P(), P())
    out_specs = P(None, "gz", "gy", "gx")
    return jax.shard_map(body, mesh=mesh, in_specs=in_specs, out_specs=out_specs, check_vma=False)
```

```python
import functools

import jax
import jax.numpy as jnp
from jax import lax
from jax.experimental import pallas as pl
from jax.experimental.pallas import tpu as pltpu
from jax.sharding import PartitionSpec as P

NEWTON = 5
EPSILON = 1e-05
LEAK = 0.2
F32, BF16 = jnp.float32, jnp.bfloat16
MIB = 1024 * 1024


def places():
    even, inside = [], []
    for axis in ("gx", "gy", "gz"):
        size, place = lax.axis_size(axis), lax.axis_index(axis)
        even.append(lax.rem(place, 2) == 0 if size > 1 and power_of_two(size) else place >= 0)
        inside += [place > 0, place < size - 1]
    return even + inside


def in_vmem(*values):
    return [pltpu.with_memory_space_constraint(value, pltpu.VMEM) for value in values]


def dot(a, b, dims=((1,), (0,))):
    return lax.dot_general(a, b, (dims, ((), ())), preferred_element_type=F32)


def thirds(value):
    one = value.astype(BF16).astype(F32)
    rest = value - one
    two = rest.astype(BF16).astype(F32)
    return one, two, rest - two


def as_left(parts):
    one, two, three = (part.astype(BF16) for part in parts)
    return jnp.concatenate([one, two], axis=1), jnp.concatenate([three, one], axis=1)


def as_right(parts):
    count, width = parts[0].shape
    left = iota((count, width), 1) < width // 2
    one, two, three = (
        jnp.concatenate([jnp.where(left, part, 0.0), jnp.where(left, 0.0, part)], axis=0).astype(BF16) for part in parts
    )
    pair = jnp.concatenate([one, two], axis=1)
    return jnp.concatenate([pair, pair], axis=0), jnp.concatenate([one, three], axis=0)


def dot_blocks(a, b):
    main, rest = dot(a[0], b[0]), dot(a[1], b[1])
    width = rest.shape[1]
    return main[:, :width] + (main[:, width:] + rest)


def split(value):
    hi = value.astype(BF16)
    lo = (value - hi.astype(F32)).astype(BF16)
    return hi, lo


def iota(shape, dim):
    return lax.broadcasted_iota(jnp.int32, shape, dim)


def pick_matrix(width):
    out, half = iota((width, width), 0), width // 2
    source = jnp.where(out < half, 2 * out, 2 * (out - half) + 1)
    return (source == iota((width, width), 1)).astype(F32).astype(BF16)


def turn_plane(pick, plane, rows_ref, cells_ref):
    cin, height, width = plane.shape
    half, last = width // 2, []
    rows_ref[...] = plane.astype(F32).reshape(cin * height, width)
    for pair in range(height // 4):
        lines = [rows_ref[pl.ds(4 * pair + k, cin, stride=height), :] for k in range(4)]
        turned = dot(pick, jnp.concatenate(lines, axis=0).astype(BF16), ((1,), (1,)))
        for k in range(2):
            span = pl.ds((2 * pair + k) * half, half)
            lanes = slice(2 * cin * k, 2 * cin * (k + 1))
            cells_ref[span, : 2 * cin] = turned[:half, lanes].astype(BF16)
            cells_ref[span, 2 * cin :] = turned[half:, lanes].astype(BF16)
            last.append(turned[width - 1 :, lanes])
    return jnp.concatenate(last, axis=0)


def faces_kernel(field_ref, cells_ref, yface_ref, xface_ref, flag_ref, rows_ref, edge_ref):
    cin, depth, height, width = field_ref.shape
    half, part = width // 2, edge_ref.shape[1] // cin
    for k, flag in enumerate(places()):
        flag_ref[k : k + 1, :] = jnp.full((1, flag_ref.shape[1]), flag.astype(jnp.int32)).astype(F32)
    pick = pick_matrix(width)
    xface_ref[...] = turn_plane(pick, field_ref[:, depth - 1], rows_ref, cells_ref).astype(BF16)
    for z in range(depth):
        edge_ref[z] = field_ref[:, z].astype(F32)[:, height - part :].reshape(cin * part, width)
    group = 4 if depth % 4 == 0 else 1
    for first in range(0, depth, group):
        lines = [edge_ref[first + k, pl.ds(part - 1, cin, stride=part), :] for k in range(group)]
        turned = dot(pick, jnp.concatenate(lines, axis=0).astype(BF16), ((1,), (1,)))
        for k in range(group):
            line = turned[:, cin * k : cin * (k + 1)]
            span = pl.ds((first + k) * half, half)
            yface_ref[span, :] = jnp.concatenate([line[:half], line[half:]], axis=1).astype(BF16)


def planes_kernel(field_ref, xlast_ref, cells_ref, xface_ref, rows_ref):
    xface_ref[field_ref.shape[1] - 1] = xlast_ref[...]
    pick = pick_matrix(field_ref.shape[3])
    for z in range(field_ref.shape[1] - 1):
        xface_ref[z] = turn_plane(pick, field_ref[:, z], rows_ref.at[z], cells_ref.at[z]).astype(BF16)


def relayout(field):
    cin, depth, height, width = field.shape
    half, lines = width // 2, height // 2
    part = 8 if height % 8 == 0 else height
    vmem = pl.BlockSpec(memory_space=pltpu.VMEM)
    faces = pl.pallas_call(
        faces_kernel,
        in_specs=[vmem],
        out_specs=[vmem] * 4,
        out_shape=[
            pltpu.VMEM((lines * half, 4 * cin), BF16),
            pltpu.VMEM((depth * half, 2 * cin), BF16),
            pltpu.VMEM((lines, 2 * cin), BF16),
            pltpu.VMEM((16, 2 * cin), F32),
        ],
        scratch_shapes=[pltpu.VMEM((cin * height, width), F32), pltpu.VMEM((depth, cin * part, width), F32)],
        compiler_params=pltpu.CompilerParams(vmem_limit_bytes=12 * MIB),
        name="faces",
    )(*in_vmem(field))
    planes = pl.pallas_call(
        planes_kernel,
        in_specs=[vmem] * 2,
        out_specs=[vmem] * 2,
        out_shape=[
            pltpu.VMEM((depth - 1, lines * half, 4 * cin), BF16),
            pltpu.VMEM((depth, lines, 2 * cin), BF16),
        ],
        scratch_shapes=[pltpu.VMEM((depth - 1, cin * height, width), F32)],
        compiler_params=pltpu.CompilerParams(vmem_limit_bytes=12 * MIB),
        name="planes",
    )(*in_vmem(field, faces[2]))
    return faces, planes


def moved_down(value):
    return jnp.where(iota(value.shape, 0) == 0, 0.0, pltpu.roll(value, 1, 0))


def line_sums(acc_ref, line, half, cout):
    span = pl.ds(line * half, half)
    straight = acc_ref[span, :cout]
    shifted = acc_ref[span, 2 * cout : 3 * cout]
    if line > 0:
        above = pl.ds((line - 1) * half, half)
        straight = straight + acc_ref[above, cout : 2 * cout]
        shifted = shifted + acc_ref[above, 3 * cout :]
    return straight + moved_down(shifted)


def interior_kernel(
    lines, cells_ref, last_ref, w_ref, v_ref, part_ref, stat_ref, wz_ref, wy_ref, wx_ref, v3_ref, w4_ref, acc_ref
):
    depth = (cells_ref.shape[0] + 1) // 2
    cin, cout = w_ref.shape[3:]
    rows = cells_ref.shape[1]
    half = rows // lines
    w4_ref[...] = jnp.zeros(w4_ref.shape, BF16)
    wx_ref[...] = jnp.zeros(wx_ref.shape, BF16)
    wy_ref[...] = jnp.zeros(wy_ref.shape, BF16)
    for dz in range(3):
        for px in range(2):
            for py in range(2):
                k = (2 * px + py) * cin
                w4_ref[dz, k : k + cin, :cout] = w_ref[dz, 1 + py, 1 + px]
                if py == 1:
                    w4_ref[dz, k : k + cin, cout : 2 * cout] = w_ref[dz, 0, 1 + px]
                if px == 1:
                    w4_ref[dz, k : k + cin, 2 * cout : 3 * cout] = w_ref[dz, 1 + py, 0]
                if px == 1 and py == 1:
                    w4_ref[dz, k : k + cin, 3 * cout :] = w_ref[dz, 0, 0]
            k = (2 * dz + px) * cin
            wy_ref[k : k + cin, :cout] = w_ref[dz, 0, 1 + px]
        k = (2 * dz + 1) * cin
        wy_ref[k : k + cin, cout:] = w_ref[dz, 0, 0]
        k = 4 * dz * cin
        wx_ref[k : k + cin, :] = w_ref[dz, 1, 0]
        wx_ref[k + cin : k + 2 * cin, :] = w_ref[dz, 2, 0]
        wx_ref[k + 3 * cin : k + 4 * cin, :] = w_ref[dz, 0, 0]
    wz_ref[...] = w4_ref[0]
    for dz in range(3):
        for dy in range(3):
            v3_ref[dy * 3 * cout : (dy + 1) * 3 * cout, (2 - dz) * cout : (3 - dz) * cout] = v_ref[dz, dy]
    for zo in range(depth):
        first = 0 if zo else 1
        planes = [cells_ref[z] if z < 2 * depth - 1 else last_ref[...] for z in range(2 * zo - 1 + first, 2 * zo + 2)]
        acc_ref[...] = dot(
            jnp.concatenate(planes, axis=1), w4_ref[first:].reshape((3 - first) * 4 * cin, 4 * cout)
        )
        for line in range(lines):
            part_ref[zo, pl.ds(line * half, half), :] = line_sums(acc_ref, line, half, cout)
    inner = (lines - 1) * half
    inside = iota((inner, cout), 0) % half != 0
    total = jnp.zeros((1, cout), F32)
    for zo in range(1, depth):
        total = total + jnp.sum(part_ref[zo, half:, :], axis=0, keepdims=True)
    offset = total * (1.0 / max(1, (depth - 1) * inner))
    gram, sums = jnp.zeros((cout, 2 * cout), F32), jnp.zeros((1, cout), F32)
    for zo in range(1, depth):
        value = jnp.where(inside, part_ref[zo, half:, :] - offset, 0.0)
        hi, lo = split(value)
        gram = gram + dot(hi, jnp.concatenate([hi, lo], axis=1), ((0,), (0,)))
        sums = sums + jnp.sum(value, axis=0, keepdims=True)
    stat_ref[:cout, :] = gram[:, :cout]
    stat_ref[cout : 2 * cout, :] = gram[:, cout:]
    stat_ref[2 * cout : 2 * cout + 8, :] = jnp.broadcast_to(sums, (8, cout))
    stat_ref[2 * cout + 8 :, :] = jnp.broadcast_to(offset, (8, cout))


def interior(lines, cells, last, weights, second):
    depth, rows, wide = cells.shape
    depth += 1
    cin, cout = weights.shape[3:]
    vmem = pl.BlockSpec(memory_space=pltpu.VMEM)
    flops = depth // 2 * rows * 3 * wide * 8 * cout
    return pl.pallas_call(
        functools.partial(interior_kernel, lines),
        in_specs=[vmem] * 4,
        out_specs=[vmem] * 6,
        out_shape=[
            pltpu.VMEM((depth // 2, rows, cout), F32),
            pltpu.VMEM((2 * cout + 16, cout), F32),
            pltpu.VMEM((wide, 4 * cout), BF16),
            pltpu.VMEM((6 * cin, 2 * cout), BF16),
            pltpu.VMEM((12 * cin, cout), BF16),
            pltpu.VMEM((9 * cout, 3 * cout), BF16),
        ],
        scratch_shapes=[pltpu.VMEM((3, wide, 4 * cout), BF16), pltpu.VMEM((rows, 4 * cout), F32)],
        compiler_params=pltpu.CompilerParams(vmem_limit_bytes=20 * MIB),
        cost_estimate=pl.CostEstimate(flops=flops, bytes_accessed=6 * MIB, transcendentals=0),
        name="interior",
    )(*in_vmem(cells, last), weights, second)


def finish_kernel(
    part_ref, stat_ref, zhalo_ref, yhalo_ref, yzhalo_ref, xhalo_ref, xzhalo_ref, wz_ref, wy_ref, wx_ref,
    feat_ref, mom_ref, xface_ref, acc_ref, rim_ref,
):
    depth, rows, cout = part_ref.shape
    half = yzhalo_ref.shape[0]
    lines = rows // half
    _, _, _, x_in, _, y_in, _, z_in, _ = places()
    zhalo = jnp.where(z_in, zhalo_ref[...], jnp.zeros(zhalo_ref.shape, BF16))
    yhalo = [yzhalo_ref[...]] + [yhalo_ref[z * half : (z + 1) * half, :] for z in range(2 * depth)]
    yhalo = [jnp.where(y_in, value, jnp.zeros_like(value)) for value in yhalo]
    yhalo[0] = jnp.where(z_in, yhalo[0], jnp.zeros_like(yhalo[0]))
    xhalo = jnp.where(x_in, xhalo_ref[...].astype(F32), 0.0)
    here = [jnp.where(jnp.logical_and(x_in, z_in), xzhalo_ref[...].astype(F32)[:lines], 0.0)]
    here += [xhalo[z * lines : (z + 1) * lines] for z in range(2 * depth)]
    spot = 2 * depth * lines
    over = [xhalo[spot + 2 * depth : spot + 2 * depth + 1]] + [xhalo[spot + z : spot + z + 1] for z in range(2 * depth)]
    over = [jnp.where(y_in, value, 0.0) for value in over]
    over[0] = jnp.where(z_in, over[0], 0.0)
    over = [jnp.concatenate([line, value[: lines - 1]], axis=0) for line, value in zip(over, here, strict=True)]
    xparts = []
    for zo in range(depth):
        row = [part for dz in range(3) for part in (here[2 * zo + dz], over[2 * zo + dz])]
        xparts.append(jnp.concatenate(row, axis=1))
    xsum = dot(jnp.concatenate(xparts, axis=0).astype(BF16), wx_ref[...])
    yparts = [jnp.concatenate(yhalo[2 * zo : 2 * zo + 3], axis=1) for zo in range(depth)]
    ysum = dot(jnp.concatenate(yparts, axis=0), wy_ref[...])
    acc_ref[...] = dot(zhalo, wz_ref[...])
    offset = stat_ref[2 * cout + 8 : 2 * cout + 9, :]
    rim_ref[...] = jnp.zeros(rim_ref.shape, F32)
    first = iota((8, cout), 0) == 0
    edges = rows + (depth - 1) * half
    for zo in range(depth):
        for line in range(lines):
            span = pl.ds(line * half, half)
            k = zo * lines + line
            if zo == 0 or line == 0:
                value = part_ref[zo, span, :]
                if zo == 0:
                    value = value + line_sums(acc_ref, line, half, cout)
                if line == 0:
                    more = ysum[zo * half : (zo + 1) * half]
                    value = value + (more[:, :cout] + moved_down(more[:, cout:]))
                value = value + jnp.where(iota((half, cout), 0) == 0, xsum[k : k + 1], 0.0)
                feat_ref[zo, span, :] = value
                spot = line * half if zo == 0 else rows + (zo - 1) * half
                rim_ref[spot : spot + half, :] = value - offset
                xface_ref[0, k : k + 1, :] = value[:1]
                xface_ref[1, k : k + 1, :] = value[half - 1 :]
            else:
                top = pl.ds(line * half, 8)
                value = part_ref[zo, top, :] + jnp.where(first, xsum[k : k + 1], 0.0)
                feat_ref[zo, top, :] = value
                feat_ref[zo, pl.ds(line * half + 8, half - 8), :] = part_ref[zo, pl.ds(line * half + 8, half - 8), :]
                spot = edges + (zo - 1) * (lines - 1) + line - 1
                rim_ref[spot : spot + 1, :] = value[:1] - offset
                xface_ref[0, k : k + 1, :] = value[:1]
                xface_ref[1, k : k + 1, :] = part_ref[zo, pl.ds((line + 1) * half - 1, 1), :]
    rim = rim_ref[...]
    hi, lo = split(rim)
    gram = dot(hi, jnp.concatenate([hi, lo], axis=1), ((0,), (0,)))
    cross = gram[:, cout:] + stat_ref[cout : 2 * cout, :]
    gram = gram[:, :cout] + stat_ref[:cout, :] + cross + cross.T
    sums = jnp.sum(rim, axis=0, keepdims=True) + stat_ref[2 * cout : 2 * cout + 1, :]
    total = sums + offset * float(depth * rows)
    eye = iota((cout, cout), 0) == iota((cout, cout), 1)
    sums_column = jnp.sum(jnp.where(eye, sums, 0.0), axis=1, keepdims=True)
    offset_column = jnp.sum(jnp.where(eye, offset, 0.0), axis=1, keepdims=True)
    gram = gram + (sums_column * offset + offset_column * total)
    group = cout // 2
    row, lane = iota((group, cout), 0), iota((group, cout), 1)
    both = jnp.where(lane < group, gram[:group], gram[group:])
    other = pltpu.roll(both, group, 1)
    mixed = jnp.where(lane >= row, both, other)
    beside = pltpu.roll(mixed, group, 1)
    mom_ref[: group // 2, :] = jnp.where(lane[: group // 2] < group, mixed[: group // 2], beside[group // 2 :])
    diag = jnp.sum(jnp.where(lane == row, other, 0.0), axis=0, keepdims=True)
    place = iota((8, cout), 0)
    mom_ref[group // 2 :, :] = jnp.where(place == 0, total, jnp.where(place == 1, diag, 0.0))


def finish(part, stats, zhalo, yhalo, yzhalo, xhalo, xzhalo, wz, wy, wx):
    depth, rows, cout = part.shape
    half = yzhalo.shape[0]
    lines = rows // half
    rim = rows + (depth - 1) * (half + lines - 1)
    vmem = pl.BlockSpec(memory_space=pltpu.VMEM)
    return pl.pallas_call(
        finish_kernel,
        in_specs=[vmem] * 10,
        out_specs=[vmem] * 3,
        out_shape=[
            pltpu.VMEM((depth, rows, cout), F32),
            pltpu.VMEM((cout // 4 + 8, cout), F32),
            pltpu.VMEM((2, depth * lines, cout), F32),
        ],
        scratch_shapes=[pltpu.VMEM((rows, 4 * cout), F32), pltpu.VMEM((rim + (-rim) % 16, cout), F32)],
        compiler_params=pltpu.CompilerParams(vmem_limit_bytes=16 * MIB),
        name="finish",
    )(*in_vmem(part, stats, zhalo, yhalo, yzhalo, xhalo, xzhalo, wz, wy, wx))


def block_kernel(
    total_cells,
    mom_ref, gain_ref, shift_ref, feat_ref, z1_ref, z2_ref, y1_ref, y2_ref, x1_ref, x2_ref, w_ref,
    out_ref, pad_ref, wide_ref, split_ref, done_ref, sem_ref,
):
    depth, rows, cout = feat_ref.shape
    half = y1_ref.shape[0] // (depth + 2)
    lines = rows // half
    group = cout // 2
    side = (group, cout)
    left = iota(side, 1) < group
    eye = iota(side, 0) == iota(side, 1) % group
    row, lane = iota(side, 0), iota(side, 1)
    mixed = mom_ref[: group // 2, :]
    mixed = jnp.concatenate([mixed, pltpu.roll(mixed, group, 1)], axis=0)
    turned = jnp.concatenate([jnp.where(left, mixed, 0.0), jnp.zeros(side, F32)], axis=0).T[:group]
    two = jnp.where(lane < row, mixed, jnp.where(lane == row, mom_ref[group // 2 + 1 : group // 2 + 2, :], turned))
    moments = jnp.where(left, jnp.where(lane >= row, mixed, turned), pltpu.roll(two, group, 1)) * (1.0 / total_cells)
    average = mom_ref[group // 2 : group // 2 + 1, :] * (1.0 / total_cells)

    def own(value, fill=0.0):
        one = jnp.sum(jnp.where(left, value, fill), axis=1, keepdims=True)
        two = jnp.sum(jnp.where(left, fill, value), axis=1, keepdims=True)
        return jnp.where(left, one, two)

    column = own(jnp.where(eye, average, 0.0))
    cov = moments - column * average + jnp.where(eye, EPSILON, 0.0)
    trace = jnp.sum(own(jnp.where(eye, cov, 0.0)), axis=0, keepdims=True)
    scaled = cov / trace
    x_even, y_even, z_even, xb_in, xa_in, yb_in, ya_in, zb_in, za_in = places()
    starts, jobs, spot = [], [], 0

    def centre(read, start, count):
        hi, lo = split(read() - average)
        split_ref[start : start + count, :cout] = hi
        split_ref[start : start + count, cout:] = lo

    for n in range(depth):
        starts.append((spot, rows))
        jobs.append(functools.partial(centre, functools.partial(feat_ref.__getitem__, n), *starts[-1]))
        spot += rows
    for even, one_ref, two_ref in ((z_even, z1_ref, z2_ref), (y_even, y1_ref, y2_ref), (x_even, x1_ref, x2_ref)):
        for before, after in ((two_ref, one_ref), (one_ref, two_ref)):
            starts.append((spot, one_ref.shape[0]))
            read = lambda even=even, a=before, b=after: jnp.where(even, a[...], b[...])
            jobs.append(functools.partial(centre, read, *starts[-1]))
            spot += one_ref.shape[0]

    def some_jobs(count):
        for _ in range(min(count, len(jobs))):
            jobs.pop(0)()

    scaled_right = as_right(thirds(scaled))
    mat = jnp.where(eye, 1.5, 0.0) - 0.5 * scaled
    for _ in range(NEWTON - 1):
        parts = thirds(mat)
        taken = as_left(parts)
        once = dot_blocks(taken, scaled_right)
        twice = dot_blocks(taken, as_right(parts))
        mat = 1.5 * mat - 0.5 * dot_blocks(as_left(thirds(twice)), as_right(thirds(once)))
    some_jobs(len(jobs))
    mat = mat / jnp.sqrt(trace) * own(jnp.where(eye, gain_ref[...], 0.0))
    mat = jnp.concatenate([jnp.where(left, mat, 0.0), jnp.where(left, 0.0, mat)], axis=0)
    hi, lo = split(mat)
    mixer = jnp.concatenate(
        [jnp.concatenate([hi, hi], axis=1), jnp.concatenate([lo, jnp.zeros_like(lo)], axis=1)], axis=0
    )
    shift = shift_ref[...]

    def whitened(n):
        start, count = starts[n]
        both = dot(split_ref[start : start + count, :], mixer, ((1,), (1,)))
        scaled = both[:, :cout] + both[:, cout:] + shift
        return jnp.where(scaled >= 0, scaled, LEAK * scaled)

    base = 8
    def put(zp, yp, middle, left, right, inside):
        l_in, r_in = xb_in, xa_in
        if inside is not None:
            middle = jnp.where(inside, middle, 0.0)
            l_in, r_in = jnp.logical_and(l_in, inside), jnp.logical_and(r_in, inside)
        pad_ref[zp, yp, base : base + half, :] = middle
        wide_ref[zp, yp * half : (yp + 1) * half, cout : 2 * cout] = middle.astype(BF16)
        pad_ref[zp, yp, base - 1 : base, :] = jnp.where(l_in, left, 0.0)
        pad_ref[zp, yp, base + half : base + half + 1, :] = jnp.where(r_in, right, 0.0)

    ysides = [whitened(depth + 2 + m) for m in range(2)]
    xsides = [whitened(depth + 4 + m) for m in range(2)]
    spots = [(z + 1, None) for z in range(depth)] + [(0, zb_in), (depth + 1, za_in)]
    for n, (zp, z_in) in enumerate(spots):
        plane = whitened(n)
        for y in range(lines):
            k = n * lines + y
            put(zp, y + 1, plane[y * half : (y + 1) * half], xsides[0][k : k + 1], xsides[1][k : k + 1], z_in)
        for m, (yp, y_in) in enumerate(((0, yb_in), (lines + 1, ya_in))):
            k = (depth + 2) * (lines + m) + n
            inside = y_in if z_in is None else jnp.logical_and(z_in, y_in)
            put(zp, yp, ysides[m][n * half : (n + 1) * half], xsides[0][k : k + 1], xsides[1][k : k + 1], inside)
    for zp in range(depth + 2):
        for yp in range(lines + 2):
            for dx in (0, 2):
                wide_ref[zp, yp * half : (yp + 1) * half, dx * cout : (dx + 1) * cout] = pad_ref[
                    zp, yp, base - 1 + dx : base - 1 + dx + half, :
                ].astype(BF16)
    sums, copies = [None] * depth, []
    for zp in range(depth + 2):
        low, high = max(zp - 2, 0), min(zp, depth - 1)
        lanes = slice((low - zp + 2) * cout, (high - zp + 3) * cout)
        taken = [wide_ref[zp, dy * half : dy * half + rows, :] for dy in range(3)]
        got = dot(jnp.concatenate(taken, axis=1), w_ref[:, lanes])
        for n, z in enumerate(range(low, high + 1)):
            piece = got[:, n * cout : (n + 1) * cout]
            sums[z] = piece if sums[z] is None else sums[z] + piece
        if zp >= 2:
            done_ref[zp - 2] = sums[zp - 2].astype(BF16)
            copies.append(pltpu.make_async_copy(done_ref.at[zp - 2], out_ref.at[zp - 2], sem_ref.at[zp - 2]))
            copies[-1].start()
    for copy in copies:
        copy.wait()


def block(total_cells, moments, gain, shift, feats, zs, ys, xs, weights):
    depth, rows, cout = feats.shape
    half = ys[0].shape[0] // (depth + 2)
    lines = rows // half
    vmem = pl.BlockSpec(memory_space=pltpu.VMEM)
    return pl.pallas_call(
        functools.partial(block_kernel, total_cells),
        in_specs=[vmem] * 11,
        out_specs=pl.BlockSpec(memory_space=pl.ANY),
        out_shape=jax.ShapeDtypeStruct((depth, rows, cout), BF16),
        scratch_shapes=[
            pltpu.VMEM((depth + 2, lines + 2, half + 16, cout), F32),
            pltpu.VMEM((depth + 2, (lines + 2) * half, 3 * cout), BF16),
            pltpu.VMEM((depth * rows + 2 * sum(pair[0].shape[0] for pair in (zs, ys, xs)), 2 * cout), BF16),
            pltpu.VMEM((depth, rows, cout), BF16),
            pltpu.SemaphoreType.DMA((depth,)),
        ],
        compiler_params=pltpu.CompilerParams(vmem_limit_bytes=24 * MIB),
        name="block",
    )(moments, gain, shift, *in_vmem(feats, *zs, *ys, *xs, weights))


def power_of_two(size):
    return size & (size - 1) == 0


def first_pairs(axis):
    return [(i, i ^ 1) for i in range(lax.axis_size(axis))]


def second_pairs(axis):
    size = lax.axis_size(axis)
    return [(i, (i + 1 if i % 2 else i - 1) % size) for i in range(size)]


def second_face(axis, value):
    size = lax.axis_size(axis)
    inner = [(i, j) for i, j in second_pairs(axis) if abs(i - j) == 1]
    other = {"gz": "gy", "gy": "gx", "gx": "gy"}[axis]
    count = lax.axis_size(other)
    if count % 2:
        return lax.ppermute(value, axis, inner)
    place = (lambda k, i: i * count + k) if axis == "gx" else (lambda k, i: k * size + i)
    pairs = [(place(k, i), place(k, j)) for k in range(count) for i, j in inner]
    pairs += [(place(k, i), place(k ^ 1, i)) for k in range(count) for i in (0, size - 1)]
    return lax.ppermute(value, (axis, other) if axis == "gx" else (other, axis), pairs)


def faces(axis, even, low, high):
    size = lax.axis_size(axis)
    if size == 1:
        return low, high
    if not power_of_two(size):
        up = up_pairs(axis)
        return lax.ppermute(low, axis, [(j, i) for i, j in up]), lax.ppermute(high, axis, up)
    one = lax.ppermute(jnp.where(even, high, low), axis, first_pairs(axis))
    return one, one if size == 2 else second_face(axis, jnp.where(even, low, high))


def added(axis, value, first=True):
    size = lax.axis_size(axis)
    if size > 1 and not power_of_two(size):
        return lax.psum(value, axis)
    if first and size > 1:
        value = value + lax.ppermute(value, axis, first_pairs(axis))
    if size > 2:
        value = value + lax.ppermute(value, axis, second_pairs(axis))
    step = 4
    while step < size:
        value = value + lax.ppermute(value, axis, [(i, (i + step) % size) for i in range(size)])
        step *= 2
    return value


def added_with_faces(axis, even, value, low, high):
    size = lax.axis_size(axis)
    if size == 1 or not power_of_two(size):
        return added(axis, value), faces(axis, even, low, high)
    count = value.shape[0]
    both = jnp.concatenate([value, jnp.where(even, high, low)], axis=0)
    both = lax.ppermute(both, axis, first_pairs(axis))
    value, one = value + both[:count], both[count:]
    if size == 2:
        return value, (one, one)
    two = second_face(axis, jnp.where(even, low, high))
    return added(axis, value, first=False), (one, two)


def sided(even, pair):
    one, two = pair
    return jnp.where(even, two, one), jnp.where(even, one, two)


def up_pairs(axis):
    return [(i, i + 1) for i in range(lax.axis_size(axis) - 1)]


def ring(axis):
    size = lax.axis_size(axis)
    return [(i, (i + 1) % size) for i in range(size)]


def diagonal(first, second):
    n, m = lax.axis_size(first), lax.axis_size(second)
    return [(a * m + b, (a + 1) % n * m + (b + 1) % m) for a in range(n) for b in range(m)]


def stacked(parts):
    count = sum(part.shape[0] for part in parts)
    count += -count % 16
    total, spot, zero = None, 0, jnp.zeros((), parts[0].dtype)
    for part in parts:
        wide = lax.pad(part, zero, ((spot, count - spot - part.shape[0], 0), (0, 0, 0)))
        total = wide if total is None else total + wide
        spot += part.shape[0]
    return total


def body(field, conv_first, norm_gain, norm_shift, conv_second):
    cin, depth_in, height_in, width_in = field.shape
    cout = conv_second.shape[-1]
    depth, lines, half = depth_in // 2, height_in // 2, width_in // 2
    (last, yface, _, flags), (cells, xface) = relayout(field)
    x_even, y_even, z_even = (flags[k : k + 1, :] > 0 for k in range(3))
    yzhalo = lax.ppermute(yface[-half:], ("gy", "gz"), diagonal("gy", "gz"))
    zhalo = lax.ppermute(last, "gz", ring("gz"))
    yhalo = lax.ppermute(yface, "gy", ring("gy"))
    xzhalo = lax.ppermute(stacked([xface[-1]]), ("gx", "gz"), diagonal("gx", "gz"))
    xown = [xface.reshape(depth_in * lines, 2 * cin)]
    xown += [yhalo.reshape(depth_in, half, 2 * cin)[:, -1], yzhalo[-1:]]
    xhalo = lax.ppermute(stacked(xown), "gx", ring("gx"))

    part, stats, wz, wy, wx, second = interior(lines, cells, last, conv_first, conv_second.reshape(3, 3, 3 * cout, cout))
    feats, moments, xfaces = finish(part, stats, zhalo, yhalo, yzhalo, xhalo, xzhalo, wz, wy, wx)
    rows = lines * half
    zs = faces("gz", z_even, feats[0], feats[-1])
    moments = added("gz", moments)
    zsides = sided(z_even, zs)

    def yside(y):
        here = slice(y * half, (y + 1) * half)
        return jnp.concatenate([feats[z, here] for z in range(depth)] + [side[here] for side in zsides], axis=0)

    moments, ys = added_with_faces("gy", y_even, moments, yside(0), yside(lines - 1))
    ysides = sided(y_even, ys)

    def xside(n, x):
        own = [xfaces[n]] + [side.reshape(-1, half, cout)[:, x] for side in zsides + ysides]
        return stacked(own)

    low, high = xside(0, 0), xside(1, half - 1)
    moments, xs = added_with_faces("gx", x_even, moments, low, high)
    total_cells = rows * depth * lax.axis_size("gx") * lax.axis_size("gy") * lax.axis_size("gz")
    result = block(
        total_cells, moments, norm_gain[None], norm_shift[None], feats, zs, ys, xs, second,
    )
    return jnp.transpose(result.reshape(depth, lines, half, cout), (3, 0, 1, 2))


def solution(mesh):
    in_specs = (P(None, "gz", "gy", "gx"), P(), P(), P(), P())
    out_specs = P(None, "gz", "gy", "gx")
    return jax.shard_map(body, mesh=mesh, in_specs=in_specs, out_specs=out_specs, check_vma=False)
```

```python
import functools

import jax
import jax.numpy as jnp
from jax import lax
from jax.experimental import pallas as pl
from jax.experimental.pallas import tpu as pltpu
from jax.sharding import PartitionSpec as P

NEWTON = 5
EPSILON = 1e-05
LEAK = 0.2
F32, BF16 = jnp.float32, jnp.bfloat16
MIB = 1024 * 1024


def places():
    even, inside = [], []
    for axis in ("gx", "gy", "gz"):
        size, place = lax.axis_size(axis), lax.axis_index(axis)
        even.append(lax.rem(place, 2) == 0 if size > 1 and power_of_two(size) else place >= 0)
        inside += [place > 0, place < size - 1]
    return even + inside


def in_vmem(*values):
    return [pltpu.with_memory_space_constraint(value, pltpu.VMEM) for value in values]


def dot(a, b, dims=((1,), (0,))):
    return lax.dot_general(a, b, (dims, ((), ())), preferred_element_type=F32)


def thirds(value):
    one = value.astype(BF16).astype(F32)
    rest = value - one
    two = rest.astype(BF16).astype(F32)
    return one, two, rest - two


def as_left(parts):
    one, two, three = (part.astype(BF16) for part in parts)
    return jnp.concatenate([one, two], axis=1), jnp.concatenate([three, one], axis=1)


def as_right(parts):
    count, width = parts[0].shape
    left = iota((count, width), 1) < width // 2
    one, two, three = (
        jnp.concatenate([jnp.where(left, part, 0.0), jnp.where(left, 0.0, part)], axis=0).astype(BF16) for part in parts
    )
    pair = jnp.concatenate([one, two], axis=1)
    return jnp.concatenate([pair, pair], axis=0), jnp.concatenate([one, three], axis=0)


def dot_blocks(a, b):
    main, rest = dot(a[0], b[0]), dot(a[1], b[1])
    width = rest.shape[1]
    return main[:, :width] + (main[:, width:] + rest)


def split(value):
    hi = value.astype(BF16)
    lo = (value - hi.astype(F32)).astype(BF16)
    return hi, lo


def iota(shape, dim):
    return lax.broadcasted_iota(jnp.int32, shape, dim)


def pick_matrix(width):
    out, half = iota((width, width), 0), width // 2
    source = jnp.where(out < half, 2 * out, 2 * (out - half) + 1)
    return (source == iota((width, width), 1)).astype(F32).astype(BF16)


def turn_plane(pick, plane, rows_ref, cells_ref):
    cin, height, width = plane.shape
    half, last = width // 2, []
    rows_ref[...] = plane.astype(F32).reshape(cin * height, width)
    for pair in range(height // 4):
        lines = [rows_ref[pl.ds(4 * pair + k, cin, stride=height), :] for k in range(4)]
        turned = dot(pick, jnp.concatenate(lines, axis=0).astype(BF16), ((1,), (1,)))
        for k in range(2):
            span = pl.ds((2 * pair + k) * half, half)
            lanes = slice(2 * cin * k, 2 * cin * (k + 1))
            cells_ref[span, : 2 * cin] = turned[:half, lanes].astype(BF16)
            cells_ref[span, 2 * cin :] = turned[half:, lanes].astype(BF16)
            last.append(turned[width - 1 :, lanes])
    return jnp.concatenate(last, axis=0)


def faces_kernel(field_ref, cells_ref, yface_ref, xface_ref, flag_ref, rows_ref, edge_ref):
    cin, depth, height, width = field_ref.shape
    half, part = width // 2, edge_ref.shape[1] // cin
    for k, flag in enumerate(places()):
        flag_ref[k : k + 1, :] = jnp.full((1, flag_ref.shape[1]), flag.astype(jnp.int32)).astype(F32)
    pick = pick_matrix(width)
    xface_ref[...] = turn_plane(pick, field_ref[:, depth - 1], rows_ref, cells_ref).astype(BF16)
    for z in range(depth):
        edge_ref[z] = field_ref[:, z].astype(F32)[:, height - part :].reshape(cin * part, width)
    group = 4 if depth % 4 == 0 else 1
    for first in range(0, depth, group):
        lines = [edge_ref[first + k, pl.ds(part - 1, cin, stride=part), :] for k in range(group)]
        turned = dot(pick, jnp.concatenate(lines, axis=0).astype(BF16), ((1,), (1,)))
        for k in range(group):
            line = turned[:, cin * k : cin * (k + 1)]
            span = pl.ds((first + k) * half, half)
            yface_ref[span, :] = jnp.concatenate([line[:half], line[half:]], axis=1).astype(BF16)


def planes_kernel(field_ref, xlast_ref, cells_ref, xface_ref, rows_ref):
    xface_ref[field_ref.shape[1] - 1] = xlast_ref[...]
    pick = pick_matrix(field_ref.shape[3])
    for z in range(field_ref.shape[1] - 1):
        xface_ref[z] = turn_plane(pick, field_ref[:, z], rows_ref.at[z], cells_ref.at[z]).astype(BF16)


def relayout(field):
    cin, depth, height, width = field.shape
    half, lines = width // 2, height // 2
    part = 8 if height % 8 == 0 else height
    vmem = pl.BlockSpec(memory_space=pltpu.VMEM)
    faces = pl.pallas_call(
        faces_kernel,
        in_specs=[vmem],
        out_specs=[vmem] * 4,
        out_shape=[
            pltpu.VMEM((lines * half, 4 * cin), BF16),
            pltpu.VMEM((depth * half, 2 * cin), BF16),
            pltpu.VMEM((lines, 2 * cin), BF16),
            pltpu.VMEM((16, 2 * cin), F32),
        ],
        scratch_shapes=[pltpu.VMEM((cin * height, width), F32), pltpu.VMEM((depth, cin * part, width), F32)],
        compiler_params=pltpu.CompilerParams(vmem_limit_bytes=12 * MIB),
        name="faces",
    )(*in_vmem(field))
    planes = pl.pallas_call(
        planes_kernel,
        in_specs=[vmem] * 2,
        out_specs=[vmem] * 2,
        out_shape=[
            pltpu.VMEM((depth - 1, lines * half, 4 * cin), BF16),
            pltpu.VMEM((depth, lines, 2 * cin), BF16),
        ],
        scratch_shapes=[pltpu.VMEM((depth - 1, cin * height, width), F32)],
        compiler_params=pltpu.CompilerParams(vmem_limit_bytes=12 * MIB),
        name="planes",
    )(*in_vmem(field, faces[2]))
    return faces, planes


def moved_down(value):
    return jnp.where(iota(value.shape, 0) == 0, 0.0, pltpu.roll(value, 1, 0))


def line_sums(acc_ref, line, half, cout):
    span = pl.ds(line * half, half)
    straight = acc_ref[span, :cout]
    shifted = acc_ref[span, 2 * cout : 3 * cout]
    if line > 0:
        above = pl.ds((line - 1) * half, half)
        straight = straight + acc_ref[above, cout : 2 * cout]
        shifted = shifted + acc_ref[above, 3 * cout :]
    return straight + moved_down(shifted)


def interior_kernel(
    lines, cells_ref, last_ref, w_ref, v_ref, part_ref, stat_ref, wz_ref, wy_ref, wx_ref, v3_ref, w4_ref, acc_ref
):
    depth = (cells_ref.shape[0] + 1) // 2
    cin, cout = w_ref.shape[3:]
    rows = cells_ref.shape[1]
    half = rows // lines
    w4_ref[...] = jnp.zeros(w4_ref.shape, BF16)
    wx_ref[...] = jnp.zeros(wx_ref.shape, BF16)
    wy_ref[...] = jnp.zeros(wy_ref.shape, BF16)
    for dz in range(3):
        for px in range(2):
            for py in range(2):
                k = (2 * px + py) * cin
                w4_ref[dz, k : k + cin, :cout] = w_ref[dz, 1 + py, 1 + px]
                if py == 1:
                    w4_ref[dz, k : k + cin, cout : 2 * cout] = w_ref[dz, 0, 1 + px]
                if px == 1:
                    w4_ref[dz, k : k + cin, 2 * cout : 3 * cout] = w_ref[dz, 1 + py, 0]
                if px == 1 and py == 1:
                    w4_ref[dz, k : k + cin, 3 * cout :] = w_ref[dz, 0, 0]
            k = (2 * dz + px) * cin
            wy_ref[k : k + cin, :cout] = w_ref[dz, 0, 1 + px]
        k = (2 * dz + 1) * cin
        wy_ref[k : k + cin, cout:] = w_ref[dz, 0, 0]
        k = 4 * dz * cin
        wx_ref[k : k + cin, :] = w_ref[dz, 1, 0]
        wx_ref[k + cin : k + 2 * cin, :] = w_ref[dz, 2, 0]
        wx_ref[k + 3 * cin : k + 4 * cin, :] = w_ref[dz, 0, 0]
    wz_ref[...] = w4_ref[0]
    for dz in range(3):
        for dy in range(3):
            v3_ref[dy * 3 * cout : (dy + 1) * 3 * cout, (2 - dz) * cout : (3 - dz) * cout] = v_ref[dz, dy]
    for zo in range(depth):
        first = 0 if zo else 1
        planes = [cells_ref[z] if z < 2 * depth - 1 else last_ref[...] for z in range(2 * zo - 1 + first, 2 * zo + 2)]
        acc_ref[...] = dot(
            jnp.concatenate(planes, axis=1), w4_ref[first:].reshape((3 - first) * 4 * cin, 4 * cout)
        )
        for line in range(lines):
            part_ref[zo, pl.ds(line * half, half), :] = line_sums(acc_ref, line, half, cout)
    inner = (lines - 1) * half
    inside = iota((inner, cout), 0) % half != 0
    total = jnp.zeros((1, cout), F32)
    for zo in range(1, depth):
        total = total + jnp.sum(part_ref[zo, half:, :], axis=0, keepdims=True)
    offset = total * (1.0 / max(1, (depth - 1) * inner))
    gram, sums = jnp.zeros((cout, 2 * cout), F32), jnp.zeros((1, cout), F32)
    for zo in range(1, depth):
        value = jnp.where(inside, part_ref[zo, half:, :] - offset, 0.0)
        hi, lo = split(value)
        gram = gram + dot(hi, jnp.concatenate([hi, lo], axis=1), ((0,), (0,)))
        sums = sums + jnp.sum(value, axis=0, keepdims=True)
    stat_ref[:cout, :] = gram[:, :cout]
    stat_ref[cout : 2 * cout, :] = gram[:, cout:]
    stat_ref[2 * cout : 2 * cout + 8, :] = jnp.broadcast_to(sums, (8, cout))
    stat_ref[2 * cout + 8 :, :] = jnp.broadcast_to(offset, (8, cout))


def interior(lines, cells, last, weights, second):
    depth, rows, wide = cells.shape
    depth += 1
    cin, cout = weights.shape[3:]
    vmem = pl.BlockSpec(memory_space=pltpu.VMEM)
    flops = depth // 2 * rows * 3 * wide * 8 * cout
    return pl.pallas_call(
        functools.partial(interior_kernel, lines),
        in_specs=[vmem] * 4,
        out_specs=[vmem] * 6,
        out_shape=[
            pltpu.VMEM((depth // 2, rows, cout), F32),
            pltpu.VMEM((2 * cout + 16, cout), F32),
            pltpu.VMEM((wide, 4 * cout), BF16),
            pltpu.VMEM((6 * cin, 2 * cout), BF16),
            pltpu.VMEM((12 * cin, cout), BF16),
            pltpu.VMEM((9 * cout, 3 * cout), BF16),
        ],
        scratch_shapes=[pltpu.VMEM((3, wide, 4 * cout), BF16), pltpu.VMEM((rows, 4 * cout), F32)],
        compiler_params=pltpu.CompilerParams(vmem_limit_bytes=20 * MIB),
        cost_estimate=pl.CostEstimate(flops=flops, bytes_accessed=6 * MIB, transcendentals=0),
        name="interior",
    )(*in_vmem(cells, last), weights, second)


def finish_kernel(
    part_ref, stat_ref, zhalo_ref, yhalo_ref, yzhalo_ref, xhalo_ref, xzhalo_ref, wz_ref, wy_ref, wx_ref,
    feat_ref, mom_ref, xface_ref, acc_ref, rim_ref,
):
    depth, rows, cout = part_ref.shape
    half = yzhalo_ref.shape[0]
    lines = rows // half
    _, _, _, x_in, _, y_in, _, z_in, _ = places()
    zhalo = jnp.where(z_in, zhalo_ref[...], jnp.zeros(zhalo_ref.shape, BF16))
    yhalo = [yzhalo_ref[...]] + [yhalo_ref[z * half : (z + 1) * half, :] for z in range(2 * depth)]
    yhalo = [jnp.where(y_in, value, jnp.zeros_like(value)) for value in yhalo]
    yhalo[0] = jnp.where(z_in, yhalo[0], jnp.zeros_like(yhalo[0]))
    xhalo = jnp.where(x_in, xhalo_ref[...].astype(F32), 0.0)
    xzhalo = jnp.where(jnp.logical_and(x_in, z_in), xzhalo_ref[...].astype(F32), 0.0)
    here = [xzhalo[:lines]] + [xhalo[z * lines : (z + 1) * lines] for z in range(2 * depth)]
    spot = 2 * depth * lines
    over = [xzhalo[lines : lines + 1]] + [xhalo[spot + z : spot + z + 1] for z in range(2 * depth)]
    over = [jnp.where(y_in, value, 0.0) for value in over]
    over = [jnp.concatenate([line, value[: lines - 1]], axis=0) for line, value in zip(over, here, strict=True)]
    xparts = []
    for zo in range(depth):
        row = [part for dz in range(3) for part in (here[2 * zo + dz], over[2 * zo + dz])]
        xparts.append(jnp.concatenate(row, axis=1))
    xsum = dot(jnp.concatenate(xparts, axis=0).astype(BF16), wx_ref[...])
    yparts = [jnp.concatenate(yhalo[2 * zo : 2 * zo + 3], axis=1) for zo in range(depth)]
    ysum = dot(jnp.concatenate(yparts, axis=0), wy_ref[...])
    acc_ref[...] = dot(zhalo, wz_ref[...])
    offset = stat_ref[2 * cout + 8 : 2 * cout + 9, :]
    rim_ref[...] = jnp.zeros(rim_ref.shape, F32)
    first = iota((8, cout), 0) == 0
    edges = rows + (depth - 1) * half
    for zo in range(depth):
        for line in range(lines):
            span = pl.ds(line * half, half)
            k = zo * lines + line
            if zo == 0 or line == 0:
                value = part_ref[zo, span, :]
                if zo == 0:
                    value = value + line_sums(acc_ref, line, half, cout)
                if line == 0:
                    more = ysum[zo * half : (zo + 1) * half]
                    value = value + (more[:, :cout] + moved_down(more[:, cout:]))
                value = value + jnp.where(iota((half, cout), 0) == 0, xsum[k : k + 1], 0.0)
                feat_ref[zo, span, :] = value
                spot = line * half if zo == 0 else rows + (zo - 1) * half
                rim_ref[spot : spot + half, :] = value - offset
                xface_ref[0, k : k + 1, :] = value[:1]
                xface_ref[1, k : k + 1, :] = value[half - 1 :]
            else:
                top = pl.ds(line * half, 8)
                value = part_ref[zo, top, :] + jnp.where(first, xsum[k : k + 1], 0.0)
                feat_ref[zo, top, :] = value
                feat_ref[zo, pl.ds(line * half + 8, half - 8), :] = part_ref[zo, pl.ds(line * half + 8, half - 8), :]
                spot = edges + (zo - 1) * (lines - 1) + line - 1
                rim_ref[spot : spot + 1, :] = value[:1] - offset
                xface_ref[0, k : k + 1, :] = value[:1]
                xface_ref[1, k : k + 1, :] = part_ref[zo, pl.ds((line + 1) * half - 1, 1), :]
    rim = rim_ref[...]
    hi, lo = split(rim)
    gram = dot(hi, jnp.concatenate([hi, lo], axis=1), ((0,), (0,)))
    cross = gram[:, cout:] + stat_ref[cout : 2 * cout, :]
    gram = gram[:, :cout] + stat_ref[:cout, :] + cross + cross.T
    sums = jnp.sum(rim, axis=0, keepdims=True) + stat_ref[2 * cout : 2 * cout + 1, :]
    total = sums + offset * float(depth * rows)
    eye = iota((cout, cout), 0) == iota((cout, cout), 1)
    sums_column = jnp.sum(jnp.where(eye, sums, 0.0), axis=1, keepdims=True)
    offset_column = jnp.sum(jnp.where(eye, offset, 0.0), axis=1, keepdims=True)
    gram = gram + (sums_column * offset + offset_column * total)
    group = cout // 2
    row, lane = iota((group, cout), 0), iota((group, cout), 1)
    both = jnp.where(lane < group, gram[:group], gram[group:])
    other = pltpu.roll(both, group, 1)
    mixed = jnp.where(lane >= row, both, other)
    beside = pltpu.roll(mixed, group, 1)
    mom_ref[: group // 2, :] = jnp.where(lane[: group // 2] < group, mixed[: group // 2], beside[group // 2 :])
    diag = jnp.sum(jnp.where(lane == row, other, 0.0), axis=0, keepdims=True)
    place = iota((8, cout), 0)
    mom_ref[group // 2 :, :] = jnp.where(place == 0, total, jnp.where(place == 1, diag, 0.0))


def finish(part, stats, zhalo, yhalo, yzhalo, xhalo, xzhalo, wz, wy, wx):
    depth, rows, cout = part.shape
    half = yzhalo.shape[0]
    lines = rows // half
    rim = rows + (depth - 1) * (half + lines - 1)
    vmem = pl.BlockSpec(memory_space=pltpu.VMEM)
    return pl.pallas_call(
        finish_kernel,
        in_specs=[vmem] * 10,
        out_specs=[vmem] * 3,
        out_shape=[
            pltpu.VMEM((depth, rows, cout), F32),
            pltpu.VMEM((cout // 4 + 8, cout), F32),
            pltpu.VMEM((2, depth * lines, cout), F32),
        ],
        scratch_shapes=[pltpu.VMEM((rows, 4 * cout), F32), pltpu.VMEM((rim + (-rim) % 16, cout), F32)],
        compiler_params=pltpu.CompilerParams(vmem_limit_bytes=16 * MIB),
        name="finish",
    )(*in_vmem(part, stats, zhalo, yhalo, yzhalo, xhalo, xzhalo, wz, wy, wx))


def block_kernel(
    total_cells,
    mom_ref, gain_ref, shift_ref, feat_ref, z1_ref, z2_ref, y1_ref, y2_ref, x1_ref, x2_ref, w_ref,
    out_ref, pad_ref, wide_ref, split_ref, done_ref, sem_ref,
):
    depth, rows, cout = feat_ref.shape
    half = y1_ref.shape[0] // (depth + 2)
    lines = rows // half
    group = cout // 2
    side = (group, cout)
    left = iota(side, 1) < group
    eye = iota(side, 0) == iota(side, 1) % group
    row, lane = iota(side, 0), iota(side, 1)
    mixed = mom_ref[: group // 2, :]
    mixed = jnp.concatenate([mixed, pltpu.roll(mixed, group, 1)], axis=0)
    turned = jnp.concatenate([jnp.where(left, mixed, 0.0), jnp.zeros(side, F32)], axis=0).T[:group]
    two = jnp.where(lane < row, mixed, jnp.where(lane == row, mom_ref[group // 2 + 1 : group // 2 + 2, :], turned))
    moments = jnp.where(left, jnp.where(lane >= row, mixed, turned), pltpu.roll(two, group, 1)) * (1.0 / total_cells)
    average = mom_ref[group // 2 : group // 2 + 1, :] * (1.0 / total_cells)

    def own(value, fill=0.0):
        one = jnp.sum(jnp.where(left, value, fill), axis=1, keepdims=True)
        two = jnp.sum(jnp.where(left, fill, value), axis=1, keepdims=True)
        return jnp.where(left, one, two)

    column = own(jnp.where(eye, average, 0.0))
    cov = moments - column * average + jnp.where(eye, EPSILON, 0.0)
    trace = jnp.sum(own(jnp.where(eye, cov, 0.0)), axis=0, keepdims=True)
    scaled = cov / trace
    x_even, y_even, z_even, xb_in, xa_in, yb_in, ya_in, zb_in, za_in = places()
    starts, jobs, spot = [], [], 0

    def centre(read, start, count):
        hi, lo = split(read() - average)
        split_ref[start : start + count, :cout] = hi
        split_ref[start : start + count, cout:] = lo

    for n in range(depth):
        starts.append((spot, rows))
        jobs.append(functools.partial(centre, functools.partial(feat_ref.__getitem__, n), *starts[-1]))
        spot += rows
    for even, one_ref, two_ref in ((z_even, z1_ref, z2_ref), (y_even, y1_ref, y2_ref), (x_even, x1_ref, x2_ref)):
        for before, after in ((two_ref, one_ref), (one_ref, two_ref)):
            starts.append((spot, one_ref.shape[0]))
            read = lambda even=even, a=before, b=after: jnp.where(even, a[...], b[...])
            jobs.append(functools.partial(centre, read, *starts[-1]))
            spot += one_ref.shape[0]

    def some_jobs(count):
        for _ in range(min(count, len(jobs))):
            jobs.pop(0)()

    scaled_right = as_right(thirds(scaled))
    mat = jnp.where(eye, 1.5, 0.0) - 0.5 * scaled
    for _ in range(NEWTON - 1):
        parts = thirds(mat)
        taken = as_left(parts)
        once = dot_blocks(taken, scaled_right)
        twice = dot_blocks(taken, as_right(parts))
        mat = 1.5 * mat - 0.5 * dot_blocks(as_left(thirds(twice)), as_right(thirds(once)))
    some_jobs(len(jobs))
    mat = mat / jnp.sqrt(trace) * own(jnp.where(eye, gain_ref[...], 0.0))
    mat = jnp.concatenate([jnp.where(left, mat, 0.0), jnp.where(left, 0.0, mat)], axis=0)
    hi, lo = split(mat)
    mixer = jnp.concatenate(
        [jnp.concatenate([hi, hi], axis=1), jnp.concatenate([lo, jnp.zeros_like(lo)], axis=1)], axis=0
    )
    shift = shift_ref[...]

    def whitened(n):
        start, count = starts[n]
        both = dot(split_ref[start : start + count, :], mixer, ((1,), (1,)))
        scaled = both[:, :cout] + both[:, cout:] + shift
        return jnp.where(scaled >= 0, scaled, LEAK * scaled)

    base = 8
    def put(zp, yp, middle, left, right, inside):
        l_in, r_in = xb_in, xa_in
        if inside is not None:
            middle = jnp.where(inside, middle, 0.0)
            l_in, r_in = jnp.logical_and(l_in, inside), jnp.logical_and(r_in, inside)
        pad_ref[zp, yp, base : base + half, :] = middle
        wide_ref[zp, yp * half : (yp + 1) * half, cout : 2 * cout] = middle.astype(BF16)
        pad_ref[zp, yp, base - 1 : base, :] = jnp.where(l_in, left, 0.0)
        pad_ref[zp, yp, base + half : base + half + 1, :] = jnp.where(r_in, right, 0.0)

    ysides = [whitened(depth + 2 + m) for m in range(2)]
    xsides = [whitened(depth + 4 + m) for m in range(2)]
    spots = [(z + 1, None) for z in range(depth)] + [(0, zb_in), (depth + 1, za_in)]
    for n, (zp, z_in) in enumerate(spots):
        plane = whitened(n)
        for y in range(lines):
            k = n * lines + y
            put(zp, y + 1, plane[y * half : (y + 1) * half], xsides[0][k : k + 1], xsides[1][k : k + 1], z_in)
        for m, (yp, y_in) in enumerate(((0, yb_in), (lines + 1, ya_in))):
            k = (depth + 2) * (lines + m) + n
            inside = y_in if z_in is None else jnp.logical_and(z_in, y_in)
            put(zp, yp, ysides[m][n * half : (n + 1) * half], xsides[0][k : k + 1], xsides[1][k : k + 1], inside)
    for zp in range(depth + 2):
        for yp in range(lines + 2):
            for dx in (0, 2):
                wide_ref[zp, yp * half : (yp + 1) * half, dx * cout : (dx + 1) * cout] = pad_ref[
                    zp, yp, base - 1 + dx : base - 1 + dx + half, :
                ].astype(BF16)
    sums, copies = [None] * depth, []
    for zp in range(depth + 2):
        low, high = max(zp - 2, 0), min(zp, depth - 1)
        lanes = slice((low - zp + 2) * cout, (high - zp + 3) * cout)
        taken = [wide_ref[zp, dy * half : dy * half + rows, :] for dy in range(3)]
        got = dot(jnp.concatenate(taken, axis=1), w_ref[:, lanes])
        for n, z in enumerate(range(low, high + 1)):
            piece = got[:, n * cout : (n + 1) * cout]
            sums[z] = piece if sums[z] is None else sums[z] + piece
        if zp >= 2:
            done_ref[zp - 2] = sums[zp - 2].astype(BF16)
            copies.append(pltpu.make_async_copy(done_ref.at[zp - 2], out_ref.at[zp - 2], sem_ref.at[zp - 2]))
            copies[-1].start()
    for copy in copies:
        copy.wait()


def block(total_cells, moments, gain, shift, feats, zs, ys, xs, weights):
    depth, rows, cout = feats.shape
    half = ys[0].shape[0] // (depth + 2)
    lines = rows // half
    vmem = pl.BlockSpec(memory_space=pltpu.VMEM)
    return pl.pallas_call(
        functools.partial(block_kernel, total_cells),
        in_specs=[vmem] * 11,
        out_specs=pl.BlockSpec(memory_space=pl.ANY),
        out_shape=jax.ShapeDtypeStruct((depth, rows, cout), BF16),
        scratch_shapes=[
            pltpu.VMEM((depth + 2, lines + 2, half + 16, cout), F32),
            pltpu.VMEM((depth + 2, (lines + 2) * half, 3 * cout), BF16),
            pltpu.VMEM((depth * rows + 2 * sum(pair[0].shape[0] for pair in (zs, ys, xs)), 2 * cout), BF16),
            pltpu.VMEM((depth, rows, cout), BF16),
            pltpu.SemaphoreType.DMA((depth,)),
        ],
        compiler_params=pltpu.CompilerParams(vmem_limit_bytes=24 * MIB),
        name="block",
    )(moments, gain, shift, *in_vmem(feats, *zs, *ys, *xs, weights))


def power_of_two(size):
    return size & (size - 1) == 0


def first_pairs(axis):
    return [(i, i ^ 1) for i in range(lax.axis_size(axis))]


def second_pairs(axis):
    size = lax.axis_size(axis)
    return [(i, (i + 1 if i % 2 else i - 1) % size) for i in range(size)]


def second_face(axis, value):
    size = lax.axis_size(axis)
    inner = [(i, j) for i, j in second_pairs(axis) if abs(i - j) == 1]
    other = {"gz": "gy", "gy": "gx", "gx": "gy"}[axis]
    count = lax.axis_size(other)
    if count % 2:
        return lax.ppermute(value, axis, inner)
    place = (lambda k, i: i * count + k) if axis == "gx" else (lambda k, i: k * size + i)
    pairs = [(place(k, i), place(k, j)) for k in range(count) for i, j in inner]
    pairs += [(place(k, i), place(k ^ 1, i)) for k in range(count) for i in (0, size - 1)]
    return lax.ppermute(value, (axis, other) if axis == "gx" else (other, axis), pairs)


def faces(axis, even, low, high):
    size = lax.axis_size(axis)
    if size == 1:
        return low, high
    if not power_of_two(size):
        up = up_pairs(axis)
        return lax.ppermute(low, axis, [(j, i) for i, j in up]), lax.ppermute(high, axis, up)
    one = lax.ppermute(jnp.where(even, high, low), axis, first_pairs(axis))
    return one, one if size == 2 else second_face(axis, jnp.where(even, low, high))


def added(axis, value, first=True):
    size = lax.axis_size(axis)
    if size > 1 and not power_of_two(size):
        return lax.psum(value, axis)
    if first and size > 1:
        value = value + lax.ppermute(value, axis, first_pairs(axis))
    if size > 2:
        value = value + lax.ppermute(value, axis, second_pairs(axis))
    step = 4
    while step < size:
        value = value + lax.ppermute(value, axis, [(i, (i + step) % size) for i in range(size)])
        step *= 2
    return value


def added_with_faces(axis, even, value, low, high):
    size = lax.axis_size(axis)
    if size == 1 or not power_of_two(size):
        return added(axis, value), faces(axis, even, low, high)
    count = value.shape[0]
    two = second_face(axis, jnp.where(even, low, high)) if size > 2 else None
    both = jnp.concatenate([value, jnp.where(even, high, low)], axis=0)
    both = lax.ppermute(both, axis, first_pairs(axis))
    value, one = value + both[:count], both[count:]
    if size == 2:
        return value, (one, one)
    value = added(axis, value, first=False)
    value, two = lax.optimization_barrier((value, two))
    return value, (one, two)


def added_beside_faces(axis, even, value, low, high):
    size = lax.axis_size(axis)
    if size < 4 or not power_of_two(size):
        return added(axis, value), faces(axis, even, low, high)
    value = value + lax.ppermute(value, axis, first_pairs(axis))
    one = lax.ppermute(jnp.where(even, high, low), axis, first_pairs(axis))
    value, other = lax.optimization_barrier((value, jnp.where(even, low, high)))
    two = second_face(axis, other)
    return added(axis, value, first=False), (one, two)


def sided(even, pair):
    one, two = pair
    return jnp.where(even, two, one), jnp.where(even, one, two)


def up_pairs(axis):
    return [(i, i + 1) for i in range(lax.axis_size(axis) - 1)]


def ring(axis):
    size = lax.axis_size(axis)
    return [(i, (i + 1) % size) for i in range(size)]


def diagonal(first, second):
    n, m = lax.axis_size(first), lax.axis_size(second)
    return [(a * m + b, (a + 1) % n * m + (b + 1) % m) for a in range(n) for b in range(m)]


def stacked(parts):
    count = sum(part.shape[0] for part in parts)
    count += -count % 16
    total, spot, zero = None, 0, jnp.zeros((), parts[0].dtype)
    for part in parts:
        wide = lax.pad(part, zero, ((spot, count - spot - part.shape[0], 0), (0, 0, 0)))
        total = wide if total is None else total + wide
        spot += part.shape[0]
    return total


def body(field, conv_first, norm_gain, norm_shift, conv_second):
    cin, depth_in, height_in, width_in = field.shape
    cout = conv_second.shape[-1]
    depth, lines, half = depth_in // 2, height_in // 2, width_in // 2
    (last, yface, _, flags), (cells, xface) = relayout(field)
    x_even, y_even, z_even = (flags[k : k + 1, :] > 0 for k in range(3))
    yzhalo = lax.ppermute(yface[-half:], ("gy", "gz"), diagonal("gy", "gz"))
    zhalo = lax.ppermute(last, "gz", ring("gz"))
    yhalo = lax.ppermute(yface, "gy", ring("gy"))
    yrim = yhalo.reshape(depth_in, half, 2 * cin)[:, -1]
    xhalo = lax.ppermute(stacked([xface.reshape(depth_in * lines, 2 * cin), yrim]), "gx", ring("gx"))
    xzhalo = lax.ppermute(stacked([xface[-1], yrim[-1:]]), ("gx", "gz"), diagonal("gx", "gz"))

    part, stats, wz, wy, wx, second = interior(lines, cells, last, conv_first, conv_second.reshape(3, 3, 3 * cout, cout))
    feats, moments, xfaces = finish(part, stats, zhalo, yhalo, yzhalo, xhalo, xzhalo, wz, wy, wx)
    rows = lines * half
    moments, zs = added_beside_faces("gz", z_even, moments, feats[0], feats[-1])
    zsides = sided(z_even, zs)

    def yside(y):
        here = slice(y * half, (y + 1) * half)
        return jnp.concatenate([feats[z, here] for z in range(depth)] + [side[here] for side in zsides], axis=0)

    moments, ys = added_with_faces("gy", y_even, moments, yside(0), yside(lines - 1))
    ysides = sided(y_even, ys)

    def xside(n, x):
        own = [xfaces[n]] + [side.reshape(-1, half, cout)[:, x] for side in zsides + ysides]
        return stacked(own)

    low, high = xside(0, 0), xside(1, half - 1)
    moments, xs = added_with_faces("gx", x_even, moments, low, high)
    total_cells = rows * depth * lax.axis_size("gx") * lax.axis_size("gy") * lax.axis_size("gz")
    result = block(
        total_cells, moments, norm_gain[None], norm_shift[None], feats, zs, ys, xs, second,
    )
    return jnp.transpose(result.reshape(depth, lines, half, cout), (3, 0, 1, 2))


def solution(mesh):
    in_specs = (P(None, "gz", "gy", "gx"), P(), P(), P(), P())
    out_specs = P(None, "gz", "gy", "gx")
    return jax.shard_map(body, mesh=mesh, in_specs=in_specs, out_specs=out_specs, check_vma=False)
```

```python
import functools

import jax
import jax.numpy as jnp
from jax import lax
from jax.experimental import pallas as pl
from jax.experimental.pallas import tpu as pltpu
from jax.sharding import PartitionSpec as P

NEWTON = 5
EPSILON = 1e-05
LEAK = 0.2
F32, BF16 = jnp.float32, jnp.bfloat16
MIB = 1024 * 1024


def places():
    even, inside = [], []
    for axis in ("gx", "gy", "gz"):
        size, place = lax.axis_size(axis), lax.axis_index(axis)
        even.append(lax.rem(place, 2) == 0 if size > 1 and power_of_two(size) else place >= 0)
        inside += [place > 0, place < size - 1]
    return even + inside


def in_vmem(*values):
    return [pltpu.with_memory_space_constraint(value, pltpu.VMEM) for value in values]


def dot(a, b, dims=((1,), (0,))):
    return lax.dot_general(a, b, (dims, ((), ())), preferred_element_type=F32)


def thirds(value):
    one = value.astype(BF16).astype(F32)
    rest = value - one
    two = rest.astype(BF16).astype(F32)
    return one, two, rest - two


def as_left(parts):
    one, two, three = (part.astype(BF16) for part in parts)
    return jnp.concatenate([one, two], axis=1), jnp.concatenate([three, one], axis=1)


def as_right(parts):
    count, width = parts[0].shape
    left = iota((count, width), 1) < width // 2
    one, two, three = (
        jnp.concatenate([jnp.where(left, part, 0.0), jnp.where(left, 0.0, part)], axis=0).astype(BF16) for part in parts
    )
    pair = jnp.concatenate([one, two], axis=1)
    return jnp.concatenate([pair, pair], axis=0), jnp.concatenate([one, three], axis=0)


def dot_blocks(a, b):
    main, rest = dot(a[0], b[0]), dot(a[1], b[1])
    width = rest.shape[1]
    return main[:, :width] + (main[:, width:] + rest)


def split(value):
    hi = value.astype(BF16)
    lo = (value - hi.astype(F32)).astype(BF16)
    return hi, lo


def iota(shape, dim):
    return lax.broadcasted_iota(jnp.int32, shape, dim)


def pick_matrix(width):
    out, half = iota((width, width), 0), width // 2
    source = jnp.where(out < half, 2 * out, 2 * (out - half) + 1)
    return (source == iota((width, width), 1)).astype(F32).astype(BF16)


def turn_plane(pick, plane, rows_ref, cells_ref):
    cin, height, width = plane.shape
    half, last = width // 2, []
    rows_ref[...] = plane.astype(F32).reshape(cin * height, width)
    for pair in range(height // 4):
        lines = [rows_ref[pl.ds(4 * pair + k, cin, stride=height), :] for k in range(4)]
        turned = dot(pick, jnp.concatenate(lines, axis=0).astype(BF16), ((1,), (1,)))
        for k in range(2):
            span = pl.ds((2 * pair + k) * half, half)
            lanes = slice(2 * cin * k, 2 * cin * (k + 1))
            cells_ref[span, : 2 * cin] = turned[:half, lanes].astype(BF16)
            cells_ref[span, 2 * cin :] = turned[half:, lanes].astype(BF16)
            last.append(turned[width - 1 :, lanes])
    return jnp.concatenate(last, axis=0)


def faces_kernel(field_ref, cells_ref, yface_ref, xface_ref, flag_ref, rows_ref, edge_ref):
    cin, depth, height, width = field_ref.shape
    half, part = width // 2, edge_ref.shape[1] // cin
    for k, flag in enumerate(places()):
        flag_ref[k : k + 1, :] = jnp.full((1, flag_ref.shape[1]), flag.astype(jnp.int32)).astype(F32)
    pick = pick_matrix(width)
    xface_ref[...] = turn_plane(pick, field_ref[:, depth - 1], rows_ref, cells_ref).astype(BF16)
    for z in range(depth):
        edge_ref[z] = field_ref[:, z].astype(F32)[:, height - part :].reshape(cin * part, width)
    group = 4 if depth % 4 == 0 else 1
    for first in range(0, depth, group):
        lines = [edge_ref[first + k, pl.ds(part - 1, cin, stride=part), :] for k in range(group)]
        turned = dot(pick, jnp.concatenate(lines, axis=0).astype(BF16), ((1,), (1,)))
        for k in range(group):
            line = turned[:, cin * k : cin * (k + 1)]
            span = pl.ds((first + k) * half, half)
            yface_ref[span, :] = jnp.concatenate([line[:half], line[half:]], axis=1).astype(BF16)


def planes_kernel(field_ref, xlast_ref, cells_ref, xface_ref, rows_ref):
    xface_ref[field_ref.shape[1] - 1] = xlast_ref[...]
    pick = pick_matrix(field_ref.shape[3])
    for z in range(field_ref.shape[1] - 1):
        xface_ref[z] = turn_plane(pick, field_ref[:, z], rows_ref.at[z], cells_ref.at[z]).astype(BF16)


def relayout(field):
    cin, depth, height, width = field.shape
    half, lines = width // 2, height // 2
    part = 8 if height % 8 == 0 else height
    vmem = pl.BlockSpec(memory_space=pltpu.VMEM)
    faces = pl.pallas_call(
        faces_kernel,
        in_specs=[vmem],
        out_specs=[vmem] * 4,
        out_shape=[
            pltpu.VMEM((lines * half, 4 * cin), BF16),
            pltpu.VMEM((depth * half, 2 * cin), BF16),
            pltpu.VMEM((lines, 2 * cin), BF16),
            pltpu.VMEM((16, 2 * cin), F32),
        ],
        scratch_shapes=[pltpu.VMEM((cin * height, width), F32), pltpu.VMEM((depth, cin * part, width), F32)],
        compiler_params=pltpu.CompilerParams(vmem_limit_bytes=12 * MIB),
        name="faces",
    )(*in_vmem(field))
    planes = pl.pallas_call(
        planes_kernel,
        in_specs=[vmem] * 2,
        out_specs=[vmem] * 2,
        out_shape=[
            pltpu.VMEM((depth - 1, lines * half, 4 * cin), BF16),
            pltpu.VMEM((depth, lines, 2 * cin), BF16),
        ],
        scratch_shapes=[pltpu.VMEM((depth - 1, cin * height, width), F32)],
        compiler_params=pltpu.CompilerParams(vmem_limit_bytes=12 * MIB),
        name="planes",
    )(*in_vmem(field, faces[2]))
    return faces, planes


def moved_down(value):
    return jnp.where(iota(value.shape, 0) == 0, 0.0, pltpu.roll(value, 1, 0))


def line_sums(acc_ref, line, half, cout):
    span = pl.ds(line * half, half)
    straight = acc_ref[span, :cout]
    shifted = acc_ref[span, 2 * cout : 3 * cout]
    if line > 0:
        above = pl.ds((line - 1) * half, half)
        straight = straight + acc_ref[above, cout : 2 * cout]
        shifted = shifted + acc_ref[above, 3 * cout :]
    return straight + moved_down(shifted)


def interior_kernel(
    lines, cells_ref, last_ref, w_ref, v_ref, part_ref, stat_ref, wz_ref, wy_ref, wx_ref, v3_ref, w4_ref, acc_ref
):
    depth = (cells_ref.shape[0] + 1) // 2
    cin, cout = w_ref.shape[3:]
    rows = cells_ref.shape[1]
    half = rows // lines
    w4_ref[...] = jnp.zeros(w4_ref.shape, BF16)
    wx_ref[...] = jnp.zeros(wx_ref.shape, BF16)
    wy_ref[...] = jnp.zeros(wy_ref.shape, BF16)
    for dz in range(3):
        for px in range(2):
            for py in range(2):
                k = (2 * px + py) * cin
                w4_ref[dz, k : k + cin, :cout] = w_ref[dz, 1 + py, 1 + px]
                if py == 1:
                    w4_ref[dz, k : k + cin, cout : 2 * cout] = w_ref[dz, 0, 1 + px]
                if px == 1:
                    w4_ref[dz, k : k + cin, 2 * cout : 3 * cout] = w_ref[dz, 1 + py, 0]
                if px == 1 and py == 1:
                    w4_ref[dz, k : k + cin, 3 * cout :] = w_ref[dz, 0, 0]
            k = (2 * dz + px) * cin
            wy_ref[k : k + cin, :cout] = w_ref[dz, 0, 1 + px]
        k = (2 * dz + 1) * cin
        wy_ref[k : k + cin, cout:] = w_ref[dz, 0, 0]
        k = 4 * dz * cin
        wx_ref[k : k + cin, :] = w_ref[dz, 1, 0]
        wx_ref[k + cin : k + 2 * cin, :] = w_ref[dz, 2, 0]
        wx_ref[k + 3 * cin : k + 4 * cin, :] = w_ref[dz, 0, 0]
    wz_ref[...] = w4_ref[0]
    for dz in range(3):
        for dy in range(3):
            v3_ref[dy * 3 * cout : (dy + 1) * 3 * cout, (2 - dz) * cout : (3 - dz) * cout] = v_ref[dz, dy]
    for zo in range(depth):
        first = 0 if zo else 1
        planes = [cells_ref[z] if z < 2 * depth - 1 else last_ref[...] for z in range(2 * zo - 1 + first, 2 * zo + 2)]
        acc_ref[...] = dot(
            jnp.concatenate(planes, axis=1), w4_ref[first:].reshape((3 - first) * 4 * cin, 4 * cout)
        )
        for line in range(lines):
            part_ref[zo, pl.ds(line * half, half), :] = line_sums(acc_ref, line, half, cout)
    inner = (lines - 1) * half
    inside = iota((inner, cout), 0) % half != 0
    total = jnp.zeros((1, cout), F32)
    for zo in range(1, depth):
        total = total + jnp.sum(part_ref[zo, half:, :], axis=0, keepdims=True)
    offset = total * (1.0 / max(1, (depth - 1) * inner))
    gram, sums = jnp.zeros((cout, 2 * cout), F32), jnp.zeros((1, cout), F32)
    for zo in range(1, depth):
        value = jnp.where(inside, part_ref[zo, half:, :] - offset, 0.0)
        hi, lo = split(value)
        gram = gram + dot(hi, jnp.concatenate([hi, lo], axis=1), ((0,), (0,)))
        sums = sums + jnp.sum(value, axis=0, keepdims=True)
    stat_ref[:cout, :] = gram[:, :cout]
    stat_ref[cout : 2 * cout, :] = gram[:, cout:]
    stat_ref[2 * cout : 2 * cout + 8, :] = jnp.broadcast_to(sums, (8, cout))
    stat_ref[2 * cout + 8 :, :] = jnp.broadcast_to(offset, (8, cout))


def interior(lines, cells, last, weights, second):
    depth, rows, wide = cells.shape
    depth += 1
    cin, cout = weights.shape[3:]
    vmem = pl.BlockSpec(memory_space=pltpu.VMEM)
    flops = depth // 2 * rows * 3 * wide * 8 * cout
    return pl.pallas_call(
        functools.partial(interior_kernel, lines),
        in_specs=[vmem] * 4,
        out_specs=[vmem] * 6,
        out_shape=[
            pltpu.VMEM((depth // 2, rows, cout), F32),
            pltpu.VMEM((2 * cout + 16, cout), F32),
            pltpu.VMEM((wide, 4 * cout), BF16),
            pltpu.VMEM((6 * cin, 2 * cout), BF16),
            pltpu.VMEM((12 * cin, cout), BF16),
            pltpu.VMEM((9 * cout, 3 * cout), BF16),
        ],
        scratch_shapes=[pltpu.VMEM((3, wide, 4 * cout), BF16), pltpu.VMEM((rows, 4 * cout), F32)],
        compiler_params=pltpu.CompilerParams(vmem_limit_bytes=20 * MIB),
        cost_estimate=pl.CostEstimate(flops=flops, bytes_accessed=6 * MIB, transcendentals=0),
        name="interior",
    )(*in_vmem(cells, last), weights, second)


def finish_kernel(
    part_ref, stat_ref, zhalo_ref, yhalo_ref, yzhalo_ref, xhalo_ref, xzhalo_ref, wz_ref, wy_ref, wx_ref,
    feat_ref, mom_ref, xface_ref, acc_ref, rim_ref,
):
    depth, rows, cout = part_ref.shape
    half = yzhalo_ref.shape[0]
    lines = rows // half
    _, _, _, x_in, _, y_in, _, z_in, _ = places()
    zhalo = jnp.where(z_in, zhalo_ref[...], jnp.zeros(zhalo_ref.shape, BF16))
    yhalo = [yzhalo_ref[...]] + [yhalo_ref[z * half : (z + 1) * half, :] for z in range(2 * depth)]
    yhalo = [jnp.where(y_in, value, jnp.zeros_like(value)) for value in yhalo]
    yhalo[0] = jnp.where(z_in, yhalo[0], jnp.zeros_like(yhalo[0]))
    xhalo = jnp.where(x_in, xhalo_ref[...].astype(F32), 0.0)
    xzhalo = jnp.where(jnp.logical_and(x_in, z_in), xzhalo_ref[...].astype(F32), 0.0)
    here = [xzhalo[:lines]] + [xhalo[z * lines : (z + 1) * lines] for z in range(2 * depth)]
    spot = 2 * depth * lines
    over = [xzhalo[lines : lines + 1]] + [xhalo[spot + z : spot + z + 1] for z in range(2 * depth)]
    over = [jnp.where(y_in, value, 0.0) for value in over]
    over = [jnp.concatenate([line, value[: lines - 1]], axis=0) for line, value in zip(over, here, strict=True)]
    xparts = []
    for zo in range(depth):
        row = [part for dz in range(3) for part in (here[2 * zo + dz], over[2 * zo + dz])]
        xparts.append(jnp.concatenate(row, axis=1))
    xsum = dot(jnp.concatenate(xparts, axis=0).astype(BF16), wx_ref[...])
    yparts = [jnp.concatenate(yhalo[2 * zo : 2 * zo + 3], axis=1) for zo in range(depth)]
    ysum = dot(jnp.concatenate(yparts, axis=0), wy_ref[...])
    acc_ref[...] = dot(zhalo, wz_ref[...])
    offset = stat_ref[2 * cout + 8 : 2 * cout + 9, :]
    rim_ref[...] = jnp.zeros(rim_ref.shape, F32)
    first = iota((8, cout), 0) == 0
    edges = rows + (depth - 1) * half
    for zo in range(depth):
        for line in range(lines):
            span = pl.ds(line * half, half)
            k = zo * lines + line
            if zo == 0 or line == 0:
                value = part_ref[zo, span, :]
                if zo == 0:
                    value = value + line_sums(acc_ref, line, half, cout)
                if line == 0:
                    more = ysum[zo * half : (zo + 1) * half]
                    value = value + (more[:, :cout] + moved_down(more[:, cout:]))
                value = value + jnp.where(iota((half, cout), 0) == 0, xsum[k : k + 1], 0.0)
                feat_ref[zo, span, :] = value
                spot = line * half if zo == 0 else rows + (zo - 1) * half
                rim_ref[spot : spot + half, :] = value - offset
                xface_ref[0, k : k + 1, :] = value[:1]
                xface_ref[1, k : k + 1, :] = value[half - 1 :]
            else:
                top = pl.ds(line * half, 8)
                value = part_ref[zo, top, :] + jnp.where(first, xsum[k : k + 1], 0.0)
                feat_ref[zo, top, :] = value
                feat_ref[zo, pl.ds(line * half + 8, half - 8), :] = part_ref[zo, pl.ds(line * half + 8, half - 8), :]
                spot = edges + (zo - 1) * (lines - 1) + line - 1
                rim_ref[spot : spot + 1, :] = value[:1] - offset
                xface_ref[0, k : k + 1, :] = value[:1]
                xface_ref[1, k : k + 1, :] = part_ref[zo, pl.ds((line + 1) * half - 1, 1), :]
    rim = rim_ref[...]
    hi, lo = split(rim)
    gram = dot(hi, jnp.concatenate([hi, lo], axis=1), ((0,), (0,)))
    cross = gram[:, cout:] + stat_ref[cout : 2 * cout, :]
    gram = gram[:, :cout] + stat_ref[:cout, :] + cross + cross.T
    sums = jnp.sum(rim, axis=0, keepdims=True) + stat_ref[2 * cout : 2 * cout + 1, :]
    total = sums + offset * float(depth * rows)
    eye = iota((cout, cout), 0) == iota((cout, cout), 1)
    sums_column = jnp.sum(jnp.where(eye, sums, 0.0), axis=1, keepdims=True)
    offset_column = jnp.sum(jnp.where(eye, offset, 0.0), axis=1, keepdims=True)
    gram = gram + (sums_column * offset + offset_column * total)
    group = cout // 2
    row, lane = iota((group, cout), 0), iota((group, cout), 1)
    both = jnp.where(lane < group, gram[:group], gram[group:])
    other = pltpu.roll(both, group, 1)
    mixed = jnp.where(lane >= row, both, other)
    beside = pltpu.roll(mixed, group, 1)
    mom_ref[: group // 2, :] = jnp.where(lane[: group // 2] < group, mixed[: group // 2], beside[group // 2 :])
    diag = jnp.sum(jnp.where(lane == row, other, 0.0), axis=0, keepdims=True)
    place = iota((8, cout), 0)
    mom_ref[group // 2 :, :] = jnp.where(place == 0, total, jnp.where(place == 1, diag, 0.0))


def finish(part, stats, zhalo, yhalo, yzhalo, xhalo, xzhalo, wz, wy, wx):
    depth, rows, cout = part.shape
    half = yzhalo.shape[0]
    lines = rows // half
    rim = rows + (depth - 1) * (half + lines - 1)
    vmem = pl.BlockSpec(memory_space=pltpu.VMEM)
    return pl.pallas_call(
        finish_kernel,
        in_specs=[vmem] * 10,
        out_specs=[vmem] * 3,
        out_shape=[
            pltpu.VMEM((depth, rows, cout), F32),
            pltpu.VMEM((cout // 4 + 8, cout), F32),
            pltpu.VMEM((2, depth * lines, cout), F32),
        ],
        scratch_shapes=[pltpu.VMEM((rows, 4 * cout), F32), pltpu.VMEM((rim + (-rim) % 16, cout), F32)],
        compiler_params=pltpu.CompilerParams(vmem_limit_bytes=16 * MIB),
        name="finish",
    )(*in_vmem(part, stats, zhalo, yhalo, yzhalo, xhalo, xzhalo, wz, wy, wx))


def block_kernel(
    total_cells,
    mom_ref, gain_ref, shift_ref, feat_ref, z1_ref, z2_ref, y1_ref, y2_ref, x1_ref, x2_ref, w_ref,
    out_ref, pad_ref, wide_ref, split_ref, done_ref, sem_ref,
):
    depth, rows, cout = feat_ref.shape
    half = y1_ref.shape[0] // (depth + 2)
    lines = rows // half
    group = cout // 2
    side = (group, cout)
    left = iota(side, 1) < group
    eye = iota(side, 0) == iota(side, 1) % group
    row, lane = iota(side, 0), iota(side, 1)
    mixed = mom_ref[: group // 2, :]
    mixed = jnp.concatenate([mixed, pltpu.roll(mixed, group, 1)], axis=0)
    turned = jnp.concatenate([jnp.where(left, mixed, 0.0), jnp.zeros(side, F32)], axis=0).T[:group]
    two = jnp.where(lane < row, mixed, jnp.where(lane == row, mom_ref[group // 2 + 1 : group // 2 + 2, :], turned))
    moments = jnp.where(left, jnp.where(lane >= row, mixed, turned), pltpu.roll(two, group, 1)) * (1.0 / total_cells)
    average = mom_ref[group // 2 : group // 2 + 1, :] * (1.0 / total_cells)

    def own(value, fill=0.0):
        one = jnp.sum(jnp.where(left, value, fill), axis=1, keepdims=True)
        two = jnp.sum(jnp.where(left, fill, value), axis=1, keepdims=True)
        return jnp.where(left, one, two)

    column = own(jnp.where(eye, average, 0.0))
    cov = moments - column * average + jnp.where(eye, EPSILON, 0.0)
    trace = jnp.sum(own(jnp.where(eye, cov, 0.0)), axis=0, keepdims=True)
    scaled = cov / trace
    x_even, y_even, z_even, xb_in, xa_in, yb_in, ya_in, zb_in, za_in = places()
    starts, jobs, spot = [], [], 0

    def centre(read, start, count):
        hi, lo = split(read() - average)
        split_ref[start : start + count, :cout] = hi
        split_ref[start : start + count, cout:] = lo

    for n in range(depth):
        starts.append((spot, rows))
        jobs.append(functools.partial(centre, functools.partial(feat_ref.__getitem__, n), *starts[-1]))
        spot += rows
    for even, one_ref, two_ref in ((z_even, z1_ref, z2_ref), (y_even, y1_ref, y2_ref), (x_even, x1_ref, x2_ref)):
        for before, after in ((two_ref, one_ref), (one_ref, two_ref)):
            starts.append((spot, one_ref.shape[0]))
            read = lambda even=even, a=before, b=after: jnp.where(even, a[...], b[...])
            jobs.append(functools.partial(centre, read, *starts[-1]))
            spot += one_ref.shape[0]

    def some_jobs(count):
        for _ in range(min(count, len(jobs))):
            jobs.pop(0)()

    scaled_right = as_right(thirds(scaled))
    mat = jnp.where(eye, 1.5, 0.0) - 0.5 * scaled
    for _ in range(NEWTON - 1):
        parts = thirds(mat)
        taken = as_left(parts)
        once = dot_blocks(taken, scaled_right)
        twice = dot_blocks(taken, as_right(parts))
        mat = 1.5 * mat - 0.5 * dot_blocks(as_left(thirds(twice)), as_right(thirds(once)))
    some_jobs(len(jobs))
    mat = mat / jnp.sqrt(trace) * own(jnp.where(eye, gain_ref[...], 0.0))
    mat = jnp.concatenate([jnp.where(left, mat, 0.0), jnp.where(left, 0.0, mat)], axis=0)
    hi, lo = split(mat)
    mixer = jnp.concatenate(
        [jnp.concatenate([hi, hi], axis=1), jnp.concatenate([lo, jnp.zeros_like(lo)], axis=1)], axis=0
    )
    shift = shift_ref[...]

    def whitened(n):
        start, count = starts[n]
        both = dot(split_ref[start : start + count, :], mixer, ((1,), (1,)))
        scaled = both[:, :cout] + both[:, cout:] + shift
        return jnp.where(scaled >= 0, scaled, LEAK * scaled)

    base = 8
    def put(zp, yp, middle, left, right, inside):
        l_in, r_in = xb_in, xa_in
        if inside is not None:
            middle = jnp.where(inside, middle, 0.0)
            l_in, r_in = jnp.logical_and(l_in, inside), jnp.logical_and(r_in, inside)
        pad_ref[zp, yp, base : base + half, :] = middle
        wide_ref[zp, yp * half : (yp + 1) * half, cout : 2 * cout] = middle.astype(BF16)
        pad_ref[zp, yp, base - 1 : base, :] = jnp.where(l_in, left, 0.0)
        pad_ref[zp, yp, base + half : base + half + 1, :] = jnp.where(r_in, right, 0.0)

    ysides = [whitened(depth + 2 + m) for m in range(2)]
    xsides = [whitened(depth + 4 + m) for m in range(2)]
    spots = [(z + 1, None) for z in range(depth)] + [(0, zb_in), (depth + 1, za_in)]
    for n, (zp, z_in) in enumerate(spots):
        plane = whitened(n)
        for y in range(lines):
            k = n * lines + y
            put(zp, y + 1, plane[y * half : (y + 1) * half], xsides[0][k : k + 1], xsides[1][k : k + 1], z_in)
        for m, (yp, y_in) in enumerate(((0, yb_in), (lines + 1, ya_in))):
            k = (depth + 2) * (lines + m) + n
            inside = y_in if z_in is None else jnp.logical_and(z_in, y_in)
            put(zp, yp, ysides[m][n * half : (n + 1) * half], xsides[0][k : k + 1], xsides[1][k : k + 1], inside)
    for zp in range(depth + 2):
        for yp in range(lines + 2):
            for dx in (0, 2):
                wide_ref[zp, yp * half : (yp + 1) * half, dx * cout : (dx + 1) * cout] = pad_ref[
                    zp, yp, base - 1 + dx : base - 1 + dx + half, :
                ].astype(BF16)
    sums, copies = [None] * depth, []
    for zp in range(depth + 2):
        low, high = max(zp - 2, 0), min(zp, depth - 1)
        lanes = slice((low - zp + 2) * cout, (high - zp + 3) * cout)
        taken = [wide_ref[zp, dy * half : dy * half + rows, :] for dy in range(3)]
        got = dot(jnp.concatenate(taken, axis=1), w_ref[:, lanes])
        for n, z in enumerate(range(low, high + 1)):
            piece = got[:, n * cout : (n + 1) * cout]
            sums[z] = piece if sums[z] is None else sums[z] + piece
        if zp >= 2:
            done_ref[zp - 2] = sums[zp - 2].astype(BF16)
            copies.append(pltpu.make_async_copy(done_ref.at[zp - 2], out_ref.at[zp - 2], sem_ref.at[zp - 2]))
            copies[-1].start()
    for copy in copies:
        copy.wait()


def block(total_cells, moments, gain, shift, feats, zs, ys, xs, weights):
    depth, rows, cout = feats.shape
    half = ys[0].shape[0] // (depth + 2)
    lines = rows // half
    vmem = pl.BlockSpec(memory_space=pltpu.VMEM)
    return pl.pallas_call(
        functools.partial(block_kernel, total_cells),
        in_specs=[vmem] * 11,
        out_specs=pl.BlockSpec(memory_space=pl.ANY),
        out_shape=jax.ShapeDtypeStruct((depth, rows, cout), BF16),
        scratch_shapes=[
            pltpu.VMEM((depth + 2, lines + 2, half + 16, cout), F32),
            pltpu.VMEM((depth + 2, (lines + 2) * half, 3 * cout), BF16),
            pltpu.VMEM((depth * rows + 2 * sum(pair[0].shape[0] for pair in (zs, ys, xs)), 2 * cout), BF16),
            pltpu.VMEM((depth, rows, cout), BF16),
            pltpu.SemaphoreType.DMA((depth,)),
        ],
        compiler_params=pltpu.CompilerParams(vmem_limit_bytes=24 * MIB),
        name="block",
    )(moments, gain, shift, *in_vmem(feats, *zs, *ys, *xs, weights))


def power_of_two(size):
    return size & (size - 1) == 0


def first_pairs(axis):
    return [(i, i ^ 1) for i in range(lax.axis_size(axis))]


def second_pairs(axis):
    size = lax.axis_size(axis)
    return [(i, (i + 1 if i % 2 else i - 1) % size) for i in range(size)]


def second_face(axis, value):
    size = lax.axis_size(axis)
    inner = [(i, j) for i, j in second_pairs(axis) if abs(i - j) == 1]
    other = {"gz": "gy", "gy": "gx", "gx": "gy"}[axis]
    count = lax.axis_size(other)
    if count % 2:
        return lax.ppermute(value, axis, inner)
    place = (lambda k, i: i * count + k) if axis == "gx" else (lambda k, i: k * size + i)
    pairs = [(place(k, i), place(k, j)) for k in range(count) for i, j in inner]
    pairs += [(place(k, i), place(k ^ 1, i)) for k in range(count) for i in (0, size - 1)]
    return lax.ppermute(value, (axis, other) if axis == "gx" else (other, axis), pairs)


def faces(axis, even, low, high):
    size = lax.axis_size(axis)
    if size == 1:
        return low, high
    if not power_of_two(size):
        up = up_pairs(axis)
        return lax.ppermute(low, axis, [(j, i) for i, j in up]), lax.ppermute(high, axis, up)
    one = lax.ppermute(jnp.where(even, high, low), axis, first_pairs(axis))
    return one, one if size == 2 else second_face(axis, jnp.where(even, low, high))


def added(axis, value, first=True):
    size = lax.axis_size(axis)
    if size > 1 and not power_of_two(size):
        return lax.psum(value, axis)
    if first and size > 1:
        value = value + lax.ppermute(value, axis, first_pairs(axis))
    if size > 2:
        value = value + lax.ppermute(value, axis, second_pairs(axis))
    step = 4
    while step < size:
        value = value + lax.ppermute(value, axis, [(i, (i + step) % size) for i in range(size)])
        step *= 2
    return value


def added_with_faces(axis, even, value, low, high):
    size = lax.axis_size(axis)
    if size == 1 or not power_of_two(size):
        return added(axis, value), faces(axis, even, low, high)
    count = value.shape[0]
    two = second_face(axis, jnp.where(even, low, high)) if size > 2 else None
    both = jnp.concatenate([value, jnp.where(even, high, low)], axis=0)
    both = lax.ppermute(both, axis, first_pairs(axis))
    value, one = value + both[:count], both[count:]
    if size == 2:
        return value, (one, one)
    value = added(axis, value, first=False)
    value, two = lax.optimization_barrier((value, two))
    return value, (one, two)


def added_beside_faces(axis, even, value, low, high):
    size = lax.axis_size(axis)
    if size < 4 or not power_of_two(size):
        return added(axis, value), faces(axis, even, low, high)
    one = lax.ppermute(jnp.where(even, high, low), axis, first_pairs(axis))
    two = second_face(axis, jnp.where(even, low, high))
    value, one, two = lax.optimization_barrier((added(axis, value), one, two))
    return value, (one, two)


def sided(even, pair):
    one, two = pair
    return jnp.where(even, two, one), jnp.where(even, one, two)


def up_pairs(axis):
    return [(i, i + 1) for i in range(lax.axis_size(axis) - 1)]


def ring(axis):
    size = lax.axis_size(axis)
    return [(i, (i + 1) % size) for i in range(size)]


def diagonal(first, second):
    n, m = lax.axis_size(first), lax.axis_size(second)
    return [(a * m + b, (a + 1) % n * m + (b + 1) % m) for a in range(n) for b in range(m)]


def stacked(parts):
    count = sum(part.shape[0] for part in parts)
    count += -count % 16
    total, spot, zero = None, 0, jnp.zeros((), parts[0].dtype)
    for part in parts:
        wide = lax.pad(part, zero, ((spot, count - spot - part.shape[0], 0), (0, 0, 0)))
        total = wide if total is None else total + wide
        spot += part.shape[0]
    return total


def body(field, conv_first, norm_gain, norm_shift, conv_second):
    cin, depth_in, height_in, width_in = field.shape
    cout = conv_second.shape[-1]
    depth, lines, half = depth_in // 2, height_in // 2, width_in // 2
    (last, yface, _, flags), (cells, xface) = relayout(field)
    x_even, y_even, z_even = (flags[k : k + 1, :] > 0 for k in range(3))
    yzhalo = lax.ppermute(yface[-half:], ("gy", "gz"), diagonal("gy", "gz"))
    zhalo = lax.ppermute(last, "gz", ring("gz"))
    yhalo = lax.ppermute(yface, "gy", ring("gy"))
    yrim = yhalo.reshape(depth_in, half, 2 * cin)[:, -1]
    xhalo = lax.ppermute(stacked([xface.reshape(depth_in * lines, 2 * cin), yrim]), "gx", ring("gx"))
    xzhalo = lax.ppermute(stacked([xface[-1], yrim[-1:]]), ("gx", "gz"), diagonal("gx", "gz"))

    part, stats, wz, wy, wx, second = interior(lines, cells, last, conv_first, conv_second.reshape(3, 3, 3 * cout, cout))
    feats, moments, xfaces = finish(part, stats, zhalo, yhalo, yzhalo, xhalo, xzhalo, wz, wy, wx)
    rows = lines * half
    moments, zs = added_beside_faces("gz", z_even, moments, feats[0], feats[-1])
    zsides = sided(z_even, zs)

    def yside(y):
        here = slice(y * half, (y + 1) * half)
        return jnp.concatenate([feats[z, here] for z in range(depth)] + [side[here] for side in zsides], axis=0)

    moments, ys = added_with_faces("gy", y_even, moments, yside(0), yside(lines - 1))
    ysides = sided(y_even, ys)

    def xside(n, x):
        own = [xfaces[n]] + [side.reshape(-1, half, cout)[:, x] for side in zsides + ysides]
        return stacked(own)

    low, high = xside(0, 0), xside(1, half - 1)
    moments, xs = added_with_faces("gx", x_even, moments, low, high)
    total_cells = rows * depth * lax.axis_size("gx") * lax.axis_size("gy") * lax.axis_size("gz")
    result = block(
        total_cells, moments, norm_gain[None], norm_shift[None], feats, zs, ys, xs, second,
    )
    return jnp.transpose(result.reshape(depth, lines, half, cout), (3, 0, 1, 2))


def solution(mesh):
    in_specs = (P(None, "gz", "gy", "gx"), P(), P(), P(), P())
    out_specs = P(None, "gz", "gy", "gx")
    return jax.shard_map(body, mesh=mesh, in_specs=in_specs, out_specs=out_specs, check_vma=False)
```

```python
import functools

import jax
import jax.numpy as jnp
from jax import lax
from jax.experimental import pallas as pl
from jax.experimental.pallas import tpu as pltpu
from jax.sharding import PartitionSpec as P

NEWTON = 5
EPSILON = 1e-05
LEAK = 0.2
F32, BF16 = jnp.float32, jnp.bfloat16
MIB = 1024 * 1024


def places():
    even, inside = [], []
    for axis in ("gx", "gy", "gz"):
        size, place = lax.axis_size(axis), lax.axis_index(axis)
        even.append(lax.rem(place, 2) == 0 if size > 1 and power_of_two(size) else place >= 0)
        inside += [place > 0, place < size - 1]
    return even + inside


def in_vmem(*values):
    return [pltpu.with_memory_space_constraint(value, pltpu.VMEM) for value in values]


def dot(a, b, dims=((1,), (0,))):
    return lax.dot_general(a, b, (dims, ((), ())), preferred_element_type=F32)


def thirds(value):
    one = value.astype(BF16).astype(F32)
    rest = value - one
    two = rest.astype(BF16).astype(F32)
    return one, two, rest - two


def as_left(parts):
    one, two, three = (part.astype(BF16) for part in parts)
    return jnp.concatenate([one, two], axis=1), jnp.concatenate([three, one], axis=1)


def as_right(parts):
    count, width = parts[0].shape
    left = iota((count, width), 1) < width // 2
    one, two, three = (
        jnp.concatenate([jnp.where(left, part, 0.0), jnp.where(left, 0.0, part)], axis=0).astype(BF16) for part in parts
    )
    pair = jnp.concatenate([one, two], axis=1)
    return jnp.concatenate([pair, pair], axis=0), jnp.concatenate([one, three], axis=0)


def dot_blocks(a, b):
    main, rest = dot(a[0], b[0]), dot(a[1], b[1])
    width = rest.shape[1]
    return main[:, :width] + (main[:, width:] + rest)


def split(value):
    hi = value.astype(BF16)
    lo = (value - hi.astype(F32)).astype(BF16)
    return hi, lo


def iota(shape, dim):
    return lax.broadcasted_iota(jnp.int32, shape, dim)


def pick_matrix(width):
    out, half = iota((width, width), 0), width // 2
    source = jnp.where(out < half, 2 * out, 2 * (out - half) + 1)
    return (source == iota((width, width), 1)).astype(F32).astype(BF16)


def turn_plane(pick, plane, rows_ref, cells_ref):
    cin, height, width = plane.shape
    half, last = width // 2, []
    rows_ref[...] = plane.astype(F32).reshape(cin * height, width)
    for pair in range(height // 4):
        lines = [rows_ref[pl.ds(4 * pair + k, cin, stride=height), :] for k in range(4)]
        turned = dot(pick, jnp.concatenate(lines, axis=0).astype(BF16), ((1,), (1,)))
        for k in range(2):
            span = pl.ds((2 * pair + k) * half, half)
            lanes = slice(2 * cin * k, 2 * cin * (k + 1))
            cells_ref[span, : 2 * cin] = turned[:half, lanes].astype(BF16)
            cells_ref[span, 2 * cin :] = turned[half:, lanes].astype(BF16)
            last.append(turned[width - 1 :, lanes])
    return jnp.concatenate(last, axis=0)


def faces_kernel(field_ref, cells_ref, yface_ref, xface_ref, flag_ref, rows_ref, edge_ref):
    cin, depth, height, width = field_ref.shape
    half, part = width // 2, edge_ref.shape[1] // cin
    for k, flag in enumerate(places()):
        flag_ref[k : k + 1, :] = jnp.full((1, flag_ref.shape[1]), flag.astype(jnp.int32)).astype(F32)
    pick = pick_matrix(width)
    xface_ref[...] = turn_plane(pick, field_ref[:, depth - 1], rows_ref, cells_ref).astype(BF16)
    for z in range(depth):
        edge_ref[z] = field_ref[:, z].astype(F32)[:, height - part :].reshape(cin * part, width)
    group = 4 if depth % 4 == 0 else 1
    for first in range(0, depth, group):
        lines = [edge_ref[first + k, pl.ds(part - 1, cin, stride=part), :] for k in range(group)]
        turned = dot(pick, jnp.concatenate(lines, axis=0).astype(BF16), ((1,), (1,)))
        for k in range(group):
            line = turned[:, cin * k : cin * (k + 1)]
            span = pl.ds((first + k) * half, half)
            yface_ref[span, :] = jnp.concatenate([line[:half], line[half:]], axis=1).astype(BF16)


def planes_kernel(field_ref, xlast_ref, cells_ref, xface_ref, rows_ref):
    xface_ref[field_ref.shape[1] - 1] = xlast_ref[...]
    pick = pick_matrix(field_ref.shape[3])
    for z in range(field_ref.shape[1] - 1):
        xface_ref[z] = turn_plane(pick, field_ref[:, z], rows_ref.at[z], cells_ref.at[z]).astype(BF16)


def relayout(field):
    cin, depth, height, width = field.shape
    half, lines = width // 2, height // 2
    part = 8 if height % 8 == 0 else height
    vmem = pl.BlockSpec(memory_space=pltpu.VMEM)
    faces = pl.pallas_call(
        faces_kernel,
        in_specs=[vmem],
        out_specs=[vmem] * 4,
        out_shape=[
            pltpu.VMEM((lines * half, 4 * cin), BF16),
            pltpu.VMEM((depth * half, 2 * cin), BF16),
            pltpu.VMEM((lines, 2 * cin), BF16),
            pltpu.VMEM((16, 2 * cin), F32),
        ],
        scratch_shapes=[pltpu.VMEM((cin * height, width), F32), pltpu.VMEM((depth, cin * part, width), F32)],
        compiler_params=pltpu.CompilerParams(vmem_limit_bytes=12 * MIB),
        name="faces",
    )(*in_vmem(field))
    planes = pl.pallas_call(
        planes_kernel,
        in_specs=[vmem] * 2,
        out_specs=[vmem] * 2,
        out_shape=[
            pltpu.VMEM((depth - 1, lines * half, 4 * cin), BF16),
            pltpu.VMEM((depth, lines, 2 * cin), BF16),
        ],
        scratch_shapes=[pltpu.VMEM((depth - 1, cin * height, width), F32)],
        compiler_params=pltpu.CompilerParams(vmem_limit_bytes=12 * MIB),
        name="planes",
    )(*in_vmem(field, faces[2]))
    return faces, planes


def moved_down(value):
    return jnp.where(iota(value.shape, 0) == 0, 0.0, pltpu.roll(value, 1, 0))


def line_sums(acc_ref, line, half, cout):
    span = pl.ds(line * half, half)
    straight = acc_ref[span, :cout]
    shifted = acc_ref[span, 2 * cout : 3 * cout]
    if line > 0:
        above = pl.ds((line - 1) * half, half)
        straight = straight + acc_ref[above, cout : 2 * cout]
        shifted = shifted + acc_ref[above, 3 * cout :]
    return straight + moved_down(shifted)


def interior_kernel(
    lines, cells_ref, last_ref, w_ref, v_ref, part_ref, stat_ref, wz_ref, wy_ref, wx_ref, v3_ref, w4_ref, acc_ref
):
    depth = (cells_ref.shape[0] + 1) // 2
    cin, cout = w_ref.shape[3:]
    rows = cells_ref.shape[1]
    half = rows // lines
    w4_ref[...] = jnp.zeros(w4_ref.shape, BF16)
    wx_ref[...] = jnp.zeros(wx_ref.shape, BF16)
    wy_ref[...] = jnp.zeros(wy_ref.shape, BF16)
    for dz in range(3):
        for px in range(2):
            for py in range(2):
                k = (2 * px + py) * cin
                w4_ref[dz, k : k + cin, :cout] = w_ref[dz, 1 + py, 1 + px]
                if py == 1:
                    w4_ref[dz, k : k + cin, cout : 2 * cout] = w_ref[dz, 0, 1 + px]
                if px == 1:
                    w4_ref[dz, k : k + cin, 2 * cout : 3 * cout] = w_ref[dz, 1 + py, 0]
                if px == 1 and py == 1:
                    w4_ref[dz, k : k + cin, 3 * cout :] = w_ref[dz, 0, 0]
            k = (2 * dz + px) * cin
            wy_ref[k : k + cin, :cout] = w_ref[dz, 0, 1 + px]
        k = (2 * dz + 1) * cin
        wy_ref[k : k + cin, cout:] = w_ref[dz, 0, 0]
        k = 4 * dz * cin
        wx_ref[k : k + cin, :] = w_ref[dz, 1, 0]
        wx_ref[k + cin : k + 2 * cin, :] = w_ref[dz, 2, 0]
        wx_ref[k + 3 * cin : k + 4 * cin, :] = w_ref[dz, 0, 0]
    wz_ref[...] = w4_ref[0]
    for dz in range(3):
        for dy in range(3):
            v3_ref[dy * 3 * cout : (dy + 1) * 3 * cout, (2 - dz) * cout : (3 - dz) * cout] = v_ref[dz, dy]
    for zo in range(depth):
        first = 0 if zo else 1
        planes = [cells_ref[z] if z < 2 * depth - 1 else last_ref[...] for z in range(2 * zo - 1 + first, 2 * zo + 2)]
        acc_ref[...] = dot(
            jnp.concatenate(planes, axis=1), w4_ref[first:].reshape((3 - first) * 4 * cin, 4 * cout)
        )
        for line in range(lines):
            part_ref[zo, pl.ds(line * half, half), :] = line_sums(acc_ref, line, half, cout)
    inner = (lines - 1) * half
    inside = iota((inner, cout), 0) % half != 0
    total = jnp.zeros((1, cout), F32)
    for zo in range(1, depth):
        total = total + jnp.sum(part_ref[zo, half:, :], axis=0, keepdims=True)
    offset = total * (1.0 / max(1, (depth - 1) * inner))
    gram, sums = jnp.zeros((cout, 2 * cout), F32), jnp.zeros((1, cout), F32)
    for zo in range(1, depth):
        value = jnp.where(inside, part_ref[zo, half:, :] - offset, 0.0)
        hi, lo = split(value)
        gram = gram + dot(hi, jnp.concatenate([hi, lo], axis=1), ((0,), (0,)))
        sums = sums + jnp.sum(value, axis=0, keepdims=True)
    stat_ref[:cout, :] = gram[:, :cout]
    stat_ref[cout : 2 * cout, :] = gram[:, cout:]
    stat_ref[2 * cout : 2 * cout + 8, :] = jnp.broadcast_to(sums, (8, cout))
    stat_ref[2 * cout + 8 :, :] = jnp.broadcast_to(offset, (8, cout))


def interior(lines, cells, last, weights, second):
    depth, rows, wide = cells.shape
    depth += 1
    cin, cout = weights.shape[3:]
    vmem = pl.BlockSpec(memory_space=pltpu.VMEM)
    flops = depth // 2 * rows * 3 * wide * 8 * cout
    return pl.pallas_call(
        functools.partial(interior_kernel, lines),
        in_specs=[vmem] * 4,
        out_specs=[vmem] * 6,
        out_shape=[
            pltpu.VMEM((depth // 2, rows, cout), F32),
            pltpu.VMEM((2 * cout + 16, cout), F32),
            pltpu.VMEM((wide, 4 * cout), BF16),
            pltpu.VMEM((6 * cin, 2 * cout), BF16),
            pltpu.VMEM((12 * cin, cout), BF16),
            pltpu.VMEM((9 * cout, 3 * cout), BF16),
        ],
        scratch_shapes=[pltpu.VMEM((3, wide, 4 * cout), BF16), pltpu.VMEM((rows, 4 * cout), F32)],
        compiler_params=pltpu.CompilerParams(vmem_limit_bytes=20 * MIB),
        cost_estimate=pl.CostEstimate(flops=flops, bytes_accessed=6 * MIB, transcendentals=0),
        name="interior",
    )(*in_vmem(cells, last), weights, second)


def finish_kernel(
    part_ref, stat_ref, zhalo_ref, yhalo_ref, yzhalo_ref, xhalo_ref, xzhalo_ref, wz_ref, wy_ref, wx_ref,
    feat_ref, mom_ref, xface_ref, acc_ref, rim_ref,
):
    depth, rows, cout = part_ref.shape
    half = yzhalo_ref.shape[0]
    lines = rows // half
    _, _, _, x_in, _, y_in, _, z_in, _ = places()
    zhalo = jnp.where(z_in, zhalo_ref[...], jnp.zeros(zhalo_ref.shape, BF16))
    yhalo = [yzhalo_ref[...]] + [yhalo_ref[z * half : (z + 1) * half, :] for z in range(2 * depth)]
    yhalo = [jnp.where(y_in, value, jnp.zeros_like(value)) for value in yhalo]
    yhalo[0] = jnp.where(z_in, yhalo[0], jnp.zeros_like(yhalo[0]))
    xhalo = jnp.where(x_in, xhalo_ref[...].astype(F32), 0.0)
    xzhalo = jnp.where(jnp.logical_and(x_in, z_in), xzhalo_ref[...].astype(F32), 0.0)
    here = [xzhalo[:lines]] + [xhalo[z * lines : (z + 1) * lines] for z in range(2 * depth)]
    spot = 2 * depth * lines
    over = [xzhalo[lines : lines + 1]] + [xhalo[spot + z : spot + z + 1] for z in range(2 * depth)]
    over = [jnp.where(y_in, value, 0.0) for value in over]
    over = [jnp.concatenate([line, value[: lines - 1]], axis=0) for line, value in zip(over, here, strict=True)]
    xparts = []
    for zo in range(depth):
        row = [part for dz in range(3) for part in (here[2 * zo + dz], over[2 * zo + dz])]
        xparts.append(jnp.concatenate(row, axis=1))
    xsum = dot(jnp.concatenate(xparts, axis=0).astype(BF16), wx_ref[...])
    yparts = [jnp.concatenate(yhalo[2 * zo : 2 * zo + 3], axis=1) for zo in range(depth)]
    ysum = dot(jnp.concatenate(yparts, axis=0), wy_ref[...])
    acc_ref[...] = dot(zhalo, wz_ref[...])
    offset = stat_ref[2 * cout + 8 : 2 * cout + 9, :]
    rim_ref[...] = jnp.zeros(rim_ref.shape, F32)
    first = iota((8, cout), 0) == 0
    edges = rows + (depth - 1) * half
    for zo in range(depth):
        for line in range(lines):
            span = pl.ds(line * half, half)
            k = zo * lines + line
            if zo == 0 or line == 0:
                value = part_ref[zo, span, :]
                if zo == 0:
                    value = value + line_sums(acc_ref, line, half, cout)
                if line == 0:
                    more = ysum[zo * half : (zo + 1) * half]
                    value = value + (more[:, :cout] + moved_down(more[:, cout:]))
                value = value + jnp.where(iota((half, cout), 0) == 0, xsum[k : k + 1], 0.0)
                feat_ref[zo, span, :] = value
                spot = line * half if zo == 0 else rows + (zo - 1) * half
                rim_ref[spot : spot + half, :] = value - offset
                xface_ref[0, k : k + 1, :] = value[:1]
                xface_ref[1, k : k + 1, :] = value[half - 1 :]
            else:
                top = pl.ds(line * half, 8)
                value = part_ref[zo, top, :] + jnp.where(first, xsum[k : k + 1], 0.0)
                feat_ref[zo, top, :] = value
                feat_ref[zo, pl.ds(line * half + 8, half - 8), :] = part_ref[zo, pl.ds(line * half + 8, half - 8), :]
                spot = edges + (zo - 1) * (lines - 1) + line - 1
                rim_ref[spot : spot + 1, :] = value[:1] - offset
                xface_ref[0, k : k + 1, :] = value[:1]
                xface_ref[1, k : k + 1, :] = part_ref[zo, pl.ds((line + 1) * half - 1, 1), :]
    rim = rim_ref[...]
    hi, lo = split(rim)
    gram = dot(hi, jnp.concatenate([hi, lo], axis=1), ((0,), (0,)))
    cross = gram[:, cout:] + stat_ref[cout : 2 * cout, :]
    gram = gram[:, :cout] + stat_ref[:cout, :] + cross + cross.T
    sums = jnp.sum(rim, axis=0, keepdims=True) + stat_ref[2 * cout : 2 * cout + 1, :]
    total = sums + offset * float(depth * rows)
    eye = iota((cout, cout), 0) == iota((cout, cout), 1)
    sums_column = jnp.sum(jnp.where(eye, sums, 0.0), axis=1, keepdims=True)
    offset_column = jnp.sum(jnp.where(eye, offset, 0.0), axis=1, keepdims=True)
    gram = gram + (sums_column * offset + offset_column * total)
    group = cout // 2
    row, lane = iota((group, cout), 0), iota((group, cout), 1)
    both = jnp.where(lane < group, gram[:group], gram[group:])
    other = pltpu.roll(both, group, 1)
    mixed = jnp.where(lane >= row, both, other)
    beside = pltpu.roll(mixed, group, 1)
    mom_ref[: group // 2, :] = jnp.where(lane[: group // 2] < group, mixed[: group // 2], beside[group // 2 :])
    diag = jnp.sum(jnp.where(lane == row, other, 0.0), axis=0, keepdims=True)
    place = iota((8, cout), 0)
    mom_ref[group // 2 :, :] = jnp.where(place == 0, total, jnp.where(place == 1, diag, 0.0))


def finish(part, stats, zhalo, yhalo, yzhalo, xhalo, xzhalo, wz, wy, wx):
    depth, rows, cout = part.shape
    half = yzhalo.shape[0]
    lines = rows // half
    rim = rows + (depth - 1) * (half + lines - 1)
    vmem = pl.BlockSpec(memory_space=pltpu.VMEM)
    return pl.pallas_call(
        finish_kernel,
        in_specs=[vmem] * 10,
        out_specs=[vmem] * 3,
        out_shape=[
            pltpu.VMEM((depth, rows, cout), F32),
            pltpu.VMEM((cout // 4 + 8, cout), F32),
            pltpu.VMEM((2, depth * lines, cout), F32),
        ],
        scratch_shapes=[pltpu.VMEM((rows, 4 * cout), F32), pltpu.VMEM((rim + (-rim) % 16, cout), F32)],
        compiler_params=pltpu.CompilerParams(vmem_limit_bytes=16 * MIB),
        name="finish",
    )(*in_vmem(part, stats, zhalo, yhalo, yzhalo, xhalo, xzhalo, wz, wy, wx))


def block_kernel(
    total_cells,
    mom_ref, gain_ref, shift_ref, feat_ref, z1_ref, z2_ref, y1_ref, y2_ref, x1_ref, x2_ref, w_ref,
    out_ref, pad_ref, wide_ref, split_ref, done_ref, sem_ref,
):
    depth, rows, cout = feat_ref.shape
    half = y1_ref.shape[0] // (depth + 2)
    lines = rows // half
    group = cout // 2
    side = (group, cout)
    left = iota(side, 1) < group
    eye = iota(side, 0) == iota(side, 1) % group
    row, lane = iota(side, 0), iota(side, 1)
    mixed = mom_ref[: group // 2, :]
    mixed = jnp.concatenate([mixed, pltpu.roll(mixed, group, 1)], axis=0)
    turned = jnp.concatenate([jnp.where(left, mixed, 0.0), jnp.zeros(side, F32)], axis=0).T[:group]
    two = jnp.where(lane < row, mixed, jnp.where(lane == row, mom_ref[group // 2 + 1 : group // 2 + 2, :], turned))
    moments = jnp.where(left, jnp.where(lane >= row, mixed, turned), pltpu.roll(two, group, 1)) * (1.0 / total_cells)
    average = mom_ref[group // 2 : group // 2 + 1, :] * (1.0 / total_cells)

    def own(value, fill=0.0):
        one = jnp.sum(jnp.where(left, value, fill), axis=1, keepdims=True)
        two = jnp.sum(jnp.where(left, fill, value), axis=1, keepdims=True)
        return jnp.where(left, one, two)

    column = own(jnp.where(eye, average, 0.0))
    cov = moments - column * average + jnp.where(eye, EPSILON, 0.0)
    trace = jnp.sum(own(jnp.where(eye, cov, 0.0)), axis=0, keepdims=True)
    scaled = cov / trace
    x_even, y_even, z_even, xb_in, xa_in, yb_in, ya_in, zb_in, za_in = places()
    starts, jobs, spot = [], [], 0

    def centre(read, start, count):
        hi, lo = split(read() - average)
        split_ref[start : start + count, :cout] = hi
        split_ref[start : start + count, cout:] = lo

    for n in range(depth):
        starts.append((spot, rows))
        jobs.append(functools.partial(centre, functools.partial(feat_ref.__getitem__, n), *starts[-1]))
        spot += rows
    for even, one_ref, two_ref in ((z_even, z1_ref, z2_ref), (y_even, y1_ref, y2_ref), (x_even, x1_ref, x2_ref)):
        for before, after in ((two_ref, one_ref), (one_ref, two_ref)):
            starts.append((spot, one_ref.shape[0]))
            read = lambda even=even, a=before, b=after: jnp.where(even, a[...], b[...])
            jobs.append(functools.partial(centre, read, *starts[-1]))
            spot += one_ref.shape[0]

    def some_jobs(count):
        for _ in range(min(count, len(jobs))):
            jobs.pop(0)()

    scaled_right = as_right(thirds(scaled))
    mat = jnp.where(eye, 1.5, 0.0) - 0.5 * scaled
    for _ in range(NEWTON - 1):
        parts = thirds(mat)
        taken = as_left(parts)
        once = dot_blocks(taken, scaled_right)
        twice = dot_blocks(taken, as_right(parts))
        mat = 1.5 * mat - 0.5 * dot_blocks(as_left(thirds(twice)), as_right(thirds(once)))
    some_jobs(len(jobs))
    mat = mat / jnp.sqrt(trace) * own(jnp.where(eye, gain_ref[...], 0.0))
    mat = jnp.concatenate([jnp.where(left, mat, 0.0), jnp.where(left, 0.0, mat)], axis=0)
    hi, lo = split(mat)
    mixer = jnp.concatenate([hi, hi, lo], axis=1)
    shift = shift_ref[...]

    def whitened(n):
        start, count = starts[n]
        parts = split_ref[start : start + count, :]
        scaled = dot(jnp.concatenate([parts, parts[:, :cout]], axis=1), mixer, ((1,), (1,))) + shift
        return jnp.where(scaled >= 0, scaled, LEAK * scaled)

    base = 8
    def put(zp, yp, middle, left, right, inside):
        l_in, r_in = xb_in, xa_in
        if inside is not None:
            middle = jnp.where(inside, middle, 0.0)
            l_in, r_in = jnp.logical_and(l_in, inside), jnp.logical_and(r_in, inside)
        pad_ref[zp, yp, base : base + half, :] = middle
        wide_ref[zp, yp * half : (yp + 1) * half, cout : 2 * cout] = middle.astype(BF16)
        pad_ref[zp, yp, base - 1 : base, :] = jnp.where(l_in, left, 0.0)
        pad_ref[zp, yp, base + half : base + half + 1, :] = jnp.where(r_in, right, 0.0)

    ysides = [whitened(depth + 2 + m) for m in range(2)]
    xsides = [whitened(depth + 4 + m) for m in range(2)]
    spots = [(z + 1, None) for z in range(depth)] + [(0, zb_in), (depth + 1, za_in)]
    for n, (zp, z_in) in enumerate(spots):
        plane = whitened(n)
        for y in range(lines):
            k = n * lines + y
            put(zp, y + 1, plane[y * half : (y + 1) * half], xsides[0][k : k + 1], xsides[1][k : k + 1], z_in)
        for m, (yp, y_in) in enumerate(((0, yb_in), (lines + 1, ya_in))):
            k = (depth + 2) * (lines + m) + n
            inside = y_in if z_in is None else jnp.logical_and(z_in, y_in)
            put(zp, yp, ysides[m][n * half : (n + 1) * half], xsides[0][k : k + 1], xsides[1][k : k + 1], inside)
    for zp in range(depth + 2):
        for yp in range(lines + 2):
            for dx in (0, 2):
                wide_ref[zp, yp * half : (yp + 1) * half, dx * cout : (dx + 1) * cout] = pad_ref[
                    zp, yp, base - 1 + dx : base - 1 + dx + half, :
                ].astype(BF16)
    sums, copies = [None] * depth, []
    for zp in range(depth + 2):
        low, high = max(zp - 2, 0), min(zp, depth - 1)
        lanes = slice((low - zp + 2) * cout, (high - zp + 3) * cout)
        taken = [wide_ref[zp, dy * half : dy * half + rows, :] for dy in range(3)]
        got = dot(jnp.concatenate(taken, axis=1), w_ref[:, lanes])
        for n, z in enumerate(range(low, high + 1)):
            piece = got[:, n * cout : (n + 1) * cout]
            sums[z] = piece if sums[z] is None else sums[z] + piece
        if zp >= 2:
            done_ref[zp - 2] = sums[zp - 2].astype(BF16)
            copies.append(pltpu.make_async_copy(done_ref.at[zp - 2], out_ref.at[zp - 2], sem_ref.at[zp - 2]))
            copies[-1].start()
    for copy in copies:
        copy.wait()


def block(total_cells, moments, gain, shift, feats, zs, ys, xs, weights):
    depth, rows, cout = feats.shape
    half = ys[0].shape[0] // (depth + 2)
    lines = rows // half
    vmem = pl.BlockSpec(memory_space=pltpu.VMEM)
    return pl.pallas_call(
        functools.partial(block_kernel, total_cells),
        in_specs=[vmem] * 11,
        out_specs=pl.BlockSpec(memory_space=pl.ANY),
        out_shape=jax.ShapeDtypeStruct((depth, rows, cout), BF16),
        scratch_shapes=[
            pltpu.VMEM((depth + 2, lines + 2, half + 16, cout), F32),
            pltpu.VMEM((depth + 2, (lines + 2) * half, 3 * cout), BF16),
            pltpu.VMEM((depth * rows + 2 * sum(pair[0].shape[0] for pair in (zs, ys, xs)), 2 * cout), BF16),
            pltpu.VMEM((depth, rows, cout), BF16),
            pltpu.SemaphoreType.DMA((depth,)),
        ],
        compiler_params=pltpu.CompilerParams(vmem_limit_bytes=24 * MIB),
        name="block",
    )(moments, gain, shift, *in_vmem(feats, *zs, *ys, *xs, weights))


def power_of_two(size):
    return size & (size - 1) == 0


def first_pairs(axis):
    return [(i, i ^ 1) for i in range(lax.axis_size(axis))]


def second_pairs(axis):
    size = lax.axis_size(axis)
    return [(i, (i + 1 if i % 2 else i - 1) % size) for i in range(size)]


def second_face(axis, value):
    size = lax.axis_size(axis)
    inner = [(i, j) for i, j in second_pairs(axis) if abs(i - j) == 1]
    other = {"gz": "gy", "gy": "gx", "gx": "gy"}[axis]
    count = lax.axis_size(other)
    if count % 2:
        return lax.ppermute(value, axis, inner)
    place = (lambda k, i: i * count + k) if axis == "gx" else (lambda k, i: k * size + i)
    pairs = [(place(k, i), place(k, j)) for k in range(count) for i, j in inner]
    pairs += [(place(k, i), place(k ^ 1, i)) for k in range(count) for i in (0, size - 1)]
    return lax.ppermute(value, (axis, other) if axis == "gx" else (other, axis), pairs)


def faces(axis, even, low, high):
    size = lax.axis_size(axis)
    if size == 1:
        return low, high
    if not power_of_two(size):
        up = up_pairs(axis)
        return lax.ppermute(low, axis, [(j, i) for i, j in up]), lax.ppermute(high, axis, up)
    one = lax.ppermute(jnp.where(even, high, low), axis, first_pairs(axis))
    return one, one if size == 2 else second_face(axis, jnp.where(even, low, high))


def added(axis, value, first=True):
    size = lax.axis_size(axis)
    if size > 1 and not power_of_two(size):
        return lax.psum(value, axis)
    if first and size > 1:
        value = value + lax.ppermute(value, axis, first_pairs(axis))
    if size > 2:
        value = value + lax.ppermute(value, axis, second_pairs(axis))
    step = 4
    while step < size:
        value = value + lax.ppermute(value, axis, [(i, (i + step) % size) for i in range(size)])
        step *= 2
    return value


def added_with_faces(axis, even, value, low, high):
    size = lax.axis_size(axis)
    if size == 1 or not power_of_two(size):
        return added(axis, value), faces(axis, even, low, high)
    count = value.shape[0]
    two = second_face(axis, jnp.where(even, low, high)) if size > 2 else None
    both = jnp.concatenate([value, jnp.where(even, high, low)], axis=0)
    both = lax.ppermute(both, axis, first_pairs(axis))
    value, one = value + both[:count], both[count:]
    if size == 2:
        return value, (one, one)
    value = added(axis, value, first=False)
    value, two = lax.optimization_barrier((value, two))
    return value, (one, two)


def added_beside_faces(axis, even, value, low, high):
    size = lax.axis_size(axis)
    if size < 4 or not power_of_two(size):
        return added(axis, value), faces(axis, even, low, high)
    one = lax.ppermute(jnp.where(even, high, low), axis, first_pairs(axis))
    two = second_face(axis, jnp.where(even, low, high))
    value, one, two = lax.optimization_barrier((added(axis, value), one, two))
    return value, (one, two)


def sided(even, pair):
    one, two = pair
    return jnp.where(even, two, one), jnp.where(even, one, two)


def up_pairs(axis):
    return [(i, i + 1) for i in range(lax.axis_size(axis) - 1)]


def ring(axis):
    size = lax.axis_size(axis)
    return [(i, (i + 1) % size) for i in range(size)]


def diagonal(first, second):
    n, m = lax.axis_size(first), lax.axis_size(second)
    return [(a * m + b, (a + 1) % n * m + (b + 1) % m) for a in range(n) for b in range(m)]


def stacked(parts):
    count = sum(part.shape[0] for part in parts)
    count += -count % 16
    total, spot, zero = None, 0, jnp.zeros((), parts[0].dtype)
    for part in parts:
        wide = lax.pad(part, zero, ((spot, count - spot - part.shape[0], 0), (0, 0, 0)))
        total = wide if total is None else total + wide
        spot += part.shape[0]
    return total


def body(field, conv_first, norm_gain, norm_shift, conv_second):
    cin, depth_in, height_in, width_in = field.shape
    cout = conv_second.shape[-1]
    depth, lines, half = depth_in // 2, height_in // 2, width_in // 2
    (last, yface, _, flags), (cells, xface) = relayout(field)
    x_even, y_even, z_even = (flags[k : k + 1, :] > 0 for k in range(3))
    yzhalo = lax.ppermute(yface[-half:], ("gy", "gz"), diagonal("gy", "gz"))
    zhalo = lax.ppermute(last, "gz", ring("gz"))
    yhalo = lax.ppermute(yface, "gy", ring("gy"))
    yrim = yhalo.reshape(depth_in, half, 2 * cin)[:, -1]
    xhalo = lax.ppermute(stacked([xface.reshape(depth_in * lines, 2 * cin), yrim]), "gx", ring("gx"))
    xzhalo = lax.ppermute(stacked([xface[-1], yrim[-1:]]), ("gx", "gz"), diagonal("gx", "gz"))

    part, stats, wz, wy, wx, second = interior(lines, cells, last, conv_first, conv_second.reshape(3, 3, 3 * cout, cout))
    feats, moments, xfaces = finish(part, stats, zhalo, yhalo, yzhalo, xhalo, xzhalo, wz, wy, wx)
    rows = lines * half
    moments, zs = added_beside_faces("gz", z_even, moments, feats[0], feats[-1])
    zsides = sided(z_even, zs)

    def yside(y):
        here = slice(y * half, (y + 1) * half)
        return jnp.concatenate([feats[z, here] for z in range(depth)] + [side[here] for side in zsides], axis=0)

    moments, ys = added_with_faces("gy", y_even, moments, yside(0), yside(lines - 1))
    ysides = sided(y_even, ys)

    def xside(n, x):
        own = [xfaces[n]] + [side.reshape(-1, half, cout)[:, x] for side in zsides + ysides]
        return stacked(own)

    low, high = xside(0, 0), xside(1, half - 1)
    moments, xs = added_with_faces("gx", x_even, moments, low, high)
    total_cells = rows * depth * lax.axis_size("gx") * lax.axis_size("gy") * lax.axis_size("gz")
    result = block(
        total_cells, moments, norm_gain[None], norm_shift[None], feats, zs, ys, xs, second,
    )
    return jnp.transpose(result.reshape(depth, lines, half, cout), (3, 0, 1, 2))


def solution(mesh):
    in_specs = (P(None, "gz", "gy", "gx"), P(), P(), P(), P())
    out_specs = P(None, "gz", "gy", "gx")
    return jax.shard_map(body, mesh=mesh, in_specs=in_specs, out_specs=out_specs, check_vma=False)
```
